32 devices in a mesh: col: 4 (over y, x), row: 8 (over z, core).
Axes of the slice: x: 2, y: 2, z: 4, core: 2. Of those that a mesh axis runs over, the one named last changes fastest.
Arguments:
- corner_top_left: bfloat16 [400, 800], P('col', 'row'), may hold values from -0.625 to 0.625
- corner_top_right: bfloat16 [400, 800], P('col', 'row'), may hold values from -0.625 to 0.625
- corner_bottom_left: bfloat16 [400, 800], P('col', 'row'), may hold values from -0.625 to 0.625
- edge_top: bfloat16 [400, 20000], P('col', 'row'), may hold values from -6 to 6
- edge_right: bfloat16 [400, 20000], P('col', 'row'), may hold values from -6 to 6
- edge_bottom: bfloat16 [400, 20000], P('col', 'row'), may hold values from -6 to 6
- edge_left: bfloat16 [400, 20000], P('col', 'row'), may hold values from -6 to 6
- tensors: bfloat16 [8, 625, 625], replicated, may hold values from -0.25 to 0.25
- pattern: int32 [4, 8], P('col', 'row'), may hold values from 0 to 7, as said below
- sketch_below: float32 [100, 100], replicated, may hold values from -0.4375 to 0.4375
- sketch_above: float32 [100, 100], replicated, may hold values from -0.4375 to 0.4375
- sketch_right: float32 [100, 100], replicated, may hold values from -0.4375 to 0.4375
- sketch_left: float32 [100, 100], replicated, may hold values from -0.4375 to 0.4375
Outputs:
- left_corner_top: bfloat16 [400, 800], P('col', 'row')
- left_edge: bfloat16 [400, 20000], P('col', 'row')
- left_corner_bottom: bfloat16 [400, 800], P('col', 'row')
- top_corner_left: bfloat16 [400, 800], P('col', 'row')
- top_edge: bfloat16 [400, 20000], P('col', 'row')
- top_corner_right: bfloat16 [400, 800], P('col', 'row')
The draws below stay inside these ranges and needn't reach their ends.
Inputs may be any that keep to these rules, and one draw needn't show every extreme that they name: `pattern`: each of the 8 tensors sits at exactly 4 sites.
All inputs are finite; a program needn't handle non-finite values.
Results may differ from the reference program's by a relative error of at most 0.039.
Values may be sent and summed in bfloat16 or wider, within the bound.
No kernel may reach another device: no remote copies, remote signals or barrier semaphores. Data moves between devices by JAX's collectives and lax.ppermute only.
A program may use at most 192 MiB of HBM per device.

```python
import jax
import jax.numpy as jnp
from jax import lax

CHI = 100
DD = 25
NT = 8
LX = 4
LY = 8


def draw_pattern(key, part):
    shuffled = jax.random.permutation(jax.random.fold_in(key, 11), LX * LY)
    return (shuffled % NT).astype(jnp.int32).reshape(LX, LY)


def level_of(own_key, shape, shards, least, high):
    def one(dim, blocks):
        steps = jax.random.uniform(jax.random.fold_in(jax.random.fold_in(own_key, 6), dim), (blocks,), jnp.float32, least / len(shards), high / len(shards))
        return jnp.repeat(jnp.exp(steps), shape[dim] // blocks).reshape((-1,) + (1,) * (len(shape) - dim - 1))

    factor_of = one(*shards[0])
    for cut in shards[1:]:
        factor_of = factor_of * one(*cut)
    return factor_of


def gaussian(stream_key, shape, spread, bound, cuts=(), dtype=jnp.bfloat16):
    array = spread * jax.random.normal(stream_key, shape, jnp.float32)
    if cuts:
        array = array * level_of(stream_key, shape, cuts, -0.22, 0.18)
    return jnp.clip(array, -bound, bound).astype(dtype)


def setup_inputs(seed: int = 0) -> dict:
    seeds = jax.random.split(jax.random.key(seed), 14)
    corner_top_left = gaussian(seeds[0], (LX * CHI, LY * CHI), CHI ** -0.5, 0.625, ((0, 4), (1, 8)))
    corner_top_right = gaussian(seeds[1], (LX * CHI, LY * CHI), CHI ** -0.5, 0.625, ((0, 4), (1, 8)))
    corner_bottom_left = gaussian(seeds[2], (LX * CHI, LY * CHI), CHI ** -0.5, 0.625, ((0, 4), (1, 8)))
    edge_top = gaussian(seeds[3], (LX * CHI, LY * DD * CHI), 1.0, 6.0, ((0, 4), (1, 8)))
    edge_right = gaussian(seeds[4], (LX * CHI, LY * DD * CHI), 1.0, 6.0, ((0, 4), (1, 8)))
    edge_bottom = gaussian(seeds[5], (LX * CHI, LY * DD * CHI), 1.0, 6.0, ((0, 4), (1, 8)))
    edge_left = gaussian(seeds[6], (LX * CHI, LY * DD * CHI), 1.0, 6.0, ((0, 4), (1, 8)))
    tensors = gaussian(seeds[7], (NT, DD * DD, DD * DD), (DD * DD) ** -0.5, 0.25)
    pattern = draw_pattern(jax.random.fold_in(seeds[13], 71), 0)
    sketch_below = gaussian(seeds[9], (CHI, CHI), (2 * CHI) ** -0.5, 0.4375, (), jnp.float32)
    sketch_above = gaussian(seeds[10], (CHI, CHI), (2 * CHI) ** -0.5, 0.4375, (), jnp.float32)
    sketch_right = gaussian(seeds[11], (CHI, CHI), (2 * CHI) ** -0.5, 0.4375, (), jnp.float32)
    sketch_left = gaussian(seeds[12], (CHI, CHI), (2 * CHI) ** -0.5, 0.4375, (), jnp.float32)
    return dict(corner_top_left=corner_top_left, corner_top_right=corner_top_right, corner_bottom_left=corner_bottom_left, edge_top=edge_top, edge_right=edge_right, edge_bottom=edge_bottom, edge_left=edge_left, tensors=tensors, pattern=pattern, sketch_below=sketch_below, sketch_above=sketch_above, sketch_right=sketch_right, sketch_left=sketch_left)


def unfold_edge(edge_field):
    return edge_field.reshape(LX, CHI, LY, DD, CHI).transpose(0, 2, 1, 3, 4).astype(jnp.float32)

def fold_edge(values):
    return values.transpose(0, 2, 1, 3, 4).reshape(LX * CHI, LY * DD * CHI)

def unfold_corner(corner):
    return corner.reshape(LX, CHI, LY, CHI).transpose(0, 2, 1, 3).astype(jnp.float32)

def fold_corner(values):
    return values.transpose(0, 2, 1, 3).reshape(LX * CHI, LY * CHI)

def rms_scale(values, count):
    axes_list = tuple(range(values.ndim - count, values.ndim))
    scale = jnp.sqrt(lax.optimization_barrier(jnp.mean(values * values, axis=axes_list, keepdims=True)) + 1e-06)
    return (values / scale).astype(jnp.bfloat16)

def orthonormal(sketched):
    gram_matrix = jnp.einsum('xyra,xyrb->xyab', sketched, sketched, precision=lax.Precision.HIGHEST)
    factor = jnp.linalg.cholesky(gram_matrix)
    solved = jax.scipy.linalg.solve_triangular(factor, jnp.swapaxes(sketched, -1, -2), lower=True)
    return jnp.swapaxes(solved, -1, -2)

def sketch_with(half_field, sketch):
    return jnp.einsum('xyrc,cd->xyrd', half_field, sketch, precision=lax.Precision.HIGHEST)

def as_blocks(frame):
    return frame.astype(jnp.bfloat16).astype(jnp.float32).reshape(LX * LY, CHI, DD, CHI)

def absorb_left(operands):
    frame_in, edge_field, tensor, frame_out = operands
    mixed_rows = jnp.einsum('uip,ujd->pdij', frame_in, edge_field).astype(jnp.bfloat16)
    pushed = jnp.dot(mixed_rows.reshape(CHI * CHI, DD * DD).astype(jnp.float32), tensor.astype(jnp.float32))
    pushed = pushed.astype(jnp.bfloat16).astype(jnp.float32).reshape(CHI, CHI, DD, DD)
    return jnp.einsum('pdkr,dks->prs', pushed, frame_out)

def absorb_top(operands):
    frame_in, edge_field, tensor, frame_out = operands
    mixed_rows = jnp.einsum('ljp,lir->prij', frame_in, edge_field).astype(jnp.bfloat16)
    pushed = jnp.dot(mixed_rows.reshape(CHI * CHI, DD * DD).astype(jnp.float32), tensor.astype(jnp.float32))
    pushed = pushed.astype(jnp.bfloat16).astype(jnp.float32).reshape(CHI, CHI, DD, DD)
    return jnp.einsum('prkq,rqs->pks', pushed, frame_out)

def reference(corner_top_left, corner_top_right, corner_bottom_left, edge_top, edge_right, edge_bottom, edge_left, tensors, pattern, sketch_below, sketch_above, sketch_right, sketch_left):
    corner_one = unfold_corner(corner_top_left)
    corner_two = unfold_corner(corner_top_right)
    corner_four = unfold_corner(corner_bottom_left)
    edge_one = unfold_edge(edge_top)
    edge_two = unfold_edge(edge_right)
    edge_three = unfold_edge(edge_bottom)
    edge_four = unfold_edge(edge_left)
    site_tensors = tensors[pattern.reshape(-1)]
    upper_half = jnp.einsum('xydr,xyrkq->xydkq', corner_one, edge_one).reshape(LX, LY, CHI * DD, CHI)
    lower_half = jnp.einsum('xyur,xyrkq->xyukq', corner_four, edge_three).reshape(LX, LY, CHI * DD, CHI)
    lower_sketch = sketch_with(lower_half, sketch_below)
    upper_sketch = sketch_with(upper_half, sketch_above)
    frame_below = orthonormal(lower_sketch + jnp.roll(upper_sketch, -1, axis=1))
    frame_above = jnp.roll(frame_below, 1, axis=1)
    corner_new = rms_scale(jnp.einsum('xyap,xyaq->xypq', frame_above, upper_half, precision=lax.Precision.HIGHEST), 2)
    bottom_new = rms_scale(jnp.einsum('xyap,xyaq->xypq', frame_below, lower_half, precision=lax.Precision.HIGHEST), 2)
    edge_flat = edge_four.reshape(LX * LY, CHI, DD, CHI)
    edge_new = lax.map(absorb_left, (as_blocks(frame_above), edge_flat, site_tensors, as_blocks(frame_below)))
    edge_new = rms_scale(edge_new.reshape(LX, LY, CHI, DD, CHI), 3)
    corner_new = jnp.roll(corner_new, 1, axis=0)
    bottom_new = jnp.roll(bottom_new, 1, axis=0)
    edge_new = jnp.roll(edge_new, 1, axis=0)
    corner_next = corner_new.astype(jnp.float32)
    edge_next = edge_new.astype(jnp.float32)
    head_half = jnp.einsum('xyur,xyukw->xyrkw', corner_next, edge_next).reshape(LX, LY, CHI * DD, CHI)
    side_half = jnp.einsum('xylu,xyukd->xylkd', corner_two, edge_two).reshape(LX, LY, CHI * DD, CHI)
    side_sketch = sketch_with(side_half, sketch_right)
    head_sketch = sketch_with(head_half, sketch_left)
    frame_right = orthonormal(side_sketch + jnp.roll(head_sketch, -1, axis=0))
    frame_left = jnp.roll(frame_right, 1, axis=0)
    top_corner = rms_scale(jnp.einsum('xyaw,xyap->xywp', head_half, frame_left, precision=lax.Precision.HIGHEST), 2)
    right_corner = rms_scale(jnp.einsum('xyap,xyad->xypd', frame_right, side_half, precision=lax.Precision.HIGHEST), 2)
    top_flat = edge_one.reshape(LX * LY, CHI, DD, CHI)
    top_new = lax.map(absorb_top, (as_blocks(frame_left), top_flat, site_tensors, as_blocks(frame_right)))
    top_new = rms_scale(top_new.reshape(LX, LY, CHI, DD, CHI), 3)
    top_corner = jnp.roll(top_corner, 1, axis=1)
    right_corner = jnp.roll(right_corner, 1, axis=1)
    top_new = jnp.roll(top_new, 1, axis=1)
    return (fold_corner(corner_new), fold_edge(edge_new), fold_corner(bottom_new), fold_corner(top_corner), fold_edge(top_new), fold_corner(right_corner))
```

```python
import functools

import jax
import jax.numpy as jnp
import numpy as np
from jax import lax
from jax.experimental import pallas as pl
from jax.experimental.pallas import tpu as pltpu
from jax.sharding import PartitionSpec as P

LANES = 128
ROWS = 8
SLOT = 32
GROUP = 10
MIB = 1 << 20
F32 = jnp.float32
BF16 = jnp.bfloat16

NN = (((1,), (0,)), ((), ()))
NT = (((1,), (1,)), ((), ()))
TN = (((0,), (0,)), ((), ()))


def product(left, right, dims=NN):
    return lax.dot_general(left, right, dims, preferred_element_type=F32)


def halves(values):
    high = values.astype(BF16)
    return high, (values - high.astype(F32)).astype(BF16)


def product_split(left, right, dims=NN):
    left_high, left_low = halves(left)
    right_high, right_low = halves(right)
    axis_left, axis_right = dims[0][0][0], dims[0][1][0]
    both = jnp.concatenate([left_high, left_low], axis_left)
    twice = jnp.concatenate([right_high, right_high], axis_right)
    return product(both, twice, dims) + product(left_high, right_low, dims)


def index_of(shape, axis):
    return lax.broadcasted_iota(jnp.int32, shape, axis)


def square_of(ref, bond):
    shape = (LANES, LANES)
    keep = (index_of(shape, 0) < bond) & (index_of(shape, 1) < bond)
    return jnp.where(keep, ref[...].astype(F32), 0.0)


def spread(ref, bond, site):
    shape = (LANES, LANES)
    row, lane = index_of(shape, 0), index_of(shape, 1)
    keep = (row < bond) & (lane < bond)
    pieces = []
    for k in range(site):
        tile, offset = divmod(k * bond, LANES)
        piece = ref[:, tile * LANES : (tile + 1) * LANES].astype(F32)
        if offset:
            piece = pltpu.roll(piece, LANES - offset, 1)
        if offset + bond > LANES:
            more = ref[:, (tile + 1) * LANES : (tile + 2) * LANES].astype(F32)
            piece = jnp.where(lane < LANES - offset, piece, pltpu.roll(more, LANES - offset, 1))
        pieces.append(jnp.where(keep, piece, 0.0).astype(BF16))
    return pieces


def gather_dense(tiles, ref, bond):
    lane = index_of((LANES, LANES), 1)
    total = len(tiles) * bond
    for tile in range(-(-total // LANES)):
        begin = tile * LANES
        value = None
        for k in range(begin // bond, min(len(tiles) - 1, (begin + LANES - 1) // bond) + 1):
            shift = k * bond - begin
            piece = pltpu.roll(tiles[k], shift % LANES, 1) if shift % LANES else tiles[k]
            value = piece if value is None else jnp.where(lane >= shift, piece, value)
        ref[:, begin : begin + LANES] = value.astype(ref.dtype)


def inverse_factors(grams, bond):
    count = -(-bond // ROWS) * ROWS
    shape = (count, LANES)
    row, lane = index_of(shape, 0), index_of(shape, 1)
    inside = (row < bond) & (lane < bond)
    eye = jnp.where(row == lane, 1.0, 0.0)
    work = [jnp.where(inside, gram[:count], eye) for gram in grams]
    done = [[] for _ in grams]
    for first in range(0, count, ROWS):
        height = count - first
        row, lane = index_of((height, LANES), 0), index_of((height, LANES), 1)
        block = (lane >= first) & (lane < first + ROWS)
        start = jnp.where(row == lane - first, 1.0, 0.0)
        small_row, small_lane = index_of((ROWS, LANES), 0), index_of((ROWS, LANES), 1)
        columns = []
        for n, matrix in enumerate(work):
            columns.append(
                [
                    jnp.broadcast_to(matrix[:, first + j : first + j + 1], (height, LANES))
                    for j in range(ROWS)
                ]
            )
            work[n] = jnp.where(block, start, matrix)
        pivots = [jnp.ones((ROWS, LANES), F32) for _ in work]
        for j in range(ROWS):
            for n in range(len(work)):
                column = columns[n]
                pivot = column[j][j : j + 1, :]
                factor = jnp.where(row > j, column[j] * (1.0 / pivot), 0.0)
                work[n] = work[n] - factor * work[n][j : j + 1, :]
                for later in range(j + 1, ROWS):
                    column[later] = column[later] - factor * column[later][j : j + 1, :]
                pivots[n] = jnp.where(small_row == j, pivot, pivots[n])
        for n in range(len(work)):
            scaled = work[n][:ROWS] * lax.rsqrt(pivots[n])
            done[n].append(jnp.where(small_lane <= small_row + first, scaled, 0.0))
            work[n] = work[n][ROWS:]
    tail = jnp.zeros((LANES - count, LANES), F32)
    keep = (index_of((LANES, LANES), 0) < bond) & (index_of((LANES, LANES), 1) < bond)
    return [jnp.where(keep, jnp.concatenate(parts + [tail], 0), 0.0) for parts in done]


def gram_of(values):
    high, low = halves(values)
    both = product(high, jnp.concatenate([high, low], 1), TN)
    mixed = both[:, LANES:]
    return both[:, :LANES] + mixed + mixed.T


def scaled_corner(values, bond):
    mean = jnp.sum(values * values) / (bond * bond)
    return (values / jnp.sqrt(mean + 1e-06)).astype(BF16)


def fill_half(corner, pieces, half_ref):
    for k, piece in enumerate(pieces):
        half_ref[k * LANES : (k + 1) * LANES, :] = product(corner, piece)


def store_frame_rows(inverse, sketched_ref, rows_ref, spare_ref, plain, moved, site):
    plain[...] = jnp.zeros_like(plain)
    moved[...] = jnp.zeros_like(moved)
    bond_rows = plain.shape[0] // SLOT
    for k in range(site):
        tile = product_split(inverse, sketched_ref[k * LANES : (k + 1) * LANES, :], NT)
        place = ROWS * (k // (ROWS - 1)) + 1 + k % (ROWS - 1)
        plain[pl.ds(k, bond_rows, stride=SLOT), :] = tile[:bond_rows]
        moved[pl.ds(place, bond_rows, stride=SLOT), :] = tile[:bond_rows]
    rows_ref[...] = plain[...].astype(BF16)
    spare_ref[...] = moved[...].astype(BF16)


def prepare_kernel(
    bond, site, c1, t1, c4, t3, c2, t2, t4, above, below, right,
    t1_wide, t4_wide, upper, upper_sketch, lower, lower_sketch, side, side_sketch, half,
):
    for k, piece in enumerate(spread(t4, bond, site)):
        t4_wide[:, k * LANES : (k + 1) * LANES] = piece
    first = spread(t1, bond, site)
    for k, piece in enumerate(first):
        t1_wide[:, k * LANES : (k + 1) * LANES] = piece
    jobs = (
        (c1, first, above, upper, upper_sketch),
        (c4, None, below, lower, lower_sketch),
        (c2, None, right, side, side_sketch),
    )
    edges = (None, t3, t2)
    for (corner, pieces, sketch, plain, sketched), edge in zip(jobs, edges):
        pieces = spread(edge, bond, site) if pieces is None else pieces
        fill_half(square_of(corner, bond).astype(BF16), pieces, half)
        plain[...] = half[...].astype(BF16)
        sketched[...] = product_split(half[...], square_of(sketch, bond))


def side_kernel(bond, site, c2, t2, right, side_sketch, half):
    fill_half(square_of(c2, bond).astype(BF16), spread(t2, bond, site), half)
    side_sketch[...] = product_split(half[...], square_of(right, bond))


def vertical_kernel(
    bond, site, c1, t1, c4, t3, above, below, upper, upper_sketch, lower, lower_sketch,
    rows_ref, spare_ref, frame_out, corner_top, corner_bottom, half, over, under, plain, moved,
):
    fill_half(square_of(c1, bond).astype(BF16), spread(t1, bond, site), half)
    under[...] = lower_sketch[...] + product_split(half[...], square_of(above, bond))
    fill_half(square_of(c4, bond).astype(BF16), spread(t3, bond, site), half)
    over[...] = upper_sketch[...] + product_split(half[...], square_of(below, bond))
    grams = [gram_of(over[...]), gram_of(under[...])]
    inverse_over, inverse_under = inverse_factors(grams, bond)
    store_frame_rows(inverse_over, over, rows_ref, spare_ref, plain, moved, site)
    frame_out[...] = product_split(under[...], inverse_under, NT).astype(BF16)
    bond_rows = plain.shape[0] // SLOT
    total = jnp.zeros((bond_rows, LANES), F32)
    for k in range(site):
        piece = plain[pl.ds(k, bond_rows, stride=SLOT), :].astype(BF16)
        total = total + product(piece, upper[k * LANES : (k + 1) * LANES, :])
    corner_top[...] = scaled_corner(total, bond)[:bond, :bond]
    bottom = product(frame_out[...], lower[...], TN)
    corner_bottom[...] = scaled_corner(bottom, bond)[:bond, :bond]


def horizontal_kernel(
    bond, site, c1, edge, left, side, side_sketch,
    inverse_ref, frame_out, corner_left, corner_right, half, total,
):
    corner = square_of(c1, bond).T.astype(BF16)
    for k in range(site):
        half[k * LANES : (k + 1) * LANES, :] = product(corner, edge[:, k * LANES : (k + 1) * LANES])
    total[...] = side_sketch[...] + product_split(half[...], square_of(left, bond))
    (inverse,) = inverse_factors([gram_of(total[...])], bond)
    inverse_ref[...] = inverse
    frame_out[...] = product_split(total[...], inverse, NT).astype(BF16)
    head = product(half[...].astype(BF16), frame_out[...], TN)
    corner_left[...] = scaled_corner(head, bond)[:bond, :bond]
    tail = product(frame_out[...], side[...], TN)
    corner_right[...] = scaled_corner(tail, bond)[:bond, :bond]


def arrive_kernel(
    bond, site, c1, t4, left, side_sketch, inverse_ref, rows_ref, spare_ref, half, total, plain, moved
):
    corner = square_of(c1, bond).T.astype(BF16)
    fill_half(corner, spread(t4, bond, site), half)
    total[...] = side_sketch[...] + product_split(half[...], square_of(left, bond))
    store_frame_rows(inverse_ref[...], total, rows_ref, spare_ref, plain, moved, site)


def absorb_kernel(
    bond, site, rows_ref, spare_ref, edge, tensor, frame_out,
    dense, wide, mixed, pushed, last, result,
):
    main = site - 1
    last[...] = jnp.zeros_like(last)
    result[bond * main :, :] = jnp.zeros((result.shape[0] - bond * main, LANES), F32)

    def step(group, carry):
        begin = pl.multiple_of(group * (GROUP * SLOT), GROUP * SLOT)
        frame = rows_ref[pl.ds(begin, GROUP * SLOT), :]
        spare = product(
            spare_ref[pl.ds(begin, GROUP * SLOT), :], edge[:, main * LANES : site * LANES]
        )
        for pair in range(main // 2):
            both = product(frame, edge[:, 2 * pair * LANES : (2 * pair + 2) * LANES])
            for side in range(2):
                j = 2 * pair + side
                for p in range(GROUP):
                    tile = both[p * SLOT : (p + 1) * SLOT, side * LANES : (side + 1) * LANES]
                    if j * (ROWS - 1) < site:
                        extra = spare[p * SLOT + j * ROWS : p * SLOT + (j + 1) * ROWS, :]
                        tile = jnp.concatenate([tile[: SLOT - ROWS], tile[SLOT - ROWS :] + extra], 0)
                    mixed[j * SLOT : (j + 1) * SLOT, p * LANES : (p + 1) * LANES] = tile.astype(BF16)
        for pair in range(GROUP // 2):
            out = product(tensor[...], mixed[:, 2 * pair * LANES : (2 * pair + 2) * LANES])
            for k in range(site):
                parts = [
                    out[k * main : (k + 1) * main, side * LANES : (side + 1) * LANES]
                    for side in range(2)
                ]
                pushed[2 * pair * main : (2 * pair + 2) * main, k * LANES : (k + 1) * LANES] = (
                    jnp.concatenate(parts, 0).astype(BF16)
                )
            for side in range(2):
                place = group * GROUP + 2 * pair + side
                last[pl.ds(place, site, stride=LANES), :] = out[
                    site * main : site * main + site, side * LANES : (side + 1) * LANES
                ]
        place = pl.multiple_of(group * (GROUP * main), GROUP * main)
        result[pl.ds(place, GROUP * main), :] = product(pushed[...], frame_out[...])
        return carry

    lax.fori_loop(0, bond // GROUP, step, 0)
    tiles = [result[pl.ds(k, LANES, stride=main), :] for k in range(main)]
    joined = jnp.concatenate(
        [last[k * LANES : (k + 1) * LANES, :].astype(BF16) for k in range(site)], 1
    )
    tiles.append(product(joined, frame_out[...]))
    squares = tiles[0] * tiles[0]
    for tile in tiles[1:]:
        squares = squares + tile * tile
    scale = 1.0 / jnp.sqrt(jnp.sum(squares) / (bond * bond * site) + 1e-06)
    tiles = [tile * scale for tile in tiles]
    for k, tile in enumerate(tiles):
        wide[:, k * LANES : (k + 1) * LANES] = tile.astype(BF16)
    gather_dense(tiles, dense, bond)


def arrange_kernel(pattern, tensor, rows_left, columns_left, rows_top, columns_top, left, top):
    square = tensor.shape[0]
    for rows, columns, out in ((rows_left, columns_left, left), (rows_top, columns_top, top)):
        pick_rows = jnp.where(index_of((rows.shape[0], square), 1) == rows[...], 1.0, 0.0)
        pick_columns = jnp.where(index_of((square, columns.shape[1]), 0) == columns[...], 1.0, 0.0)
        turned = product(pick_rows.astype(BF16), tensor[...], NT).astype(BF16)
        out[...] = product(turned, pick_columns.astype(BF16)).astype(BF16)


def places(site):
    main = site - 1
    height = -(-site * site // 16) * 16
    rows = np.full((2, height), -1, np.int32)
    columns = np.full((2, main * SLOT), -1, np.int32)
    for summed in range(site):
        for kept in range(site):
            at = summed * main + kept if kept < main else site * main + summed
            rows[0, at] = summed * site + kept
            rows[1, at] = kept * site + summed
    for edge in range(site):
        for frame in range(site):
            if edge < main:
                at = edge * SLOT + frame
            else:
                slot, offset = divmod(frame, ROWS - 1)
                at = slot * SLOT + SLOT - ROWS + 1 + offset
            columns[0, at] = frame * site + edge
            columns[1, at] = edge * site + frame
    return rows, columns


def call(kernel, args, outs, scratch, limit, blocks=None):
    specs = []
    for arg in args:
        if len(arg.shape) == 2 and (arg.shape[0] % 16 or arg.shape[1] % LANES):
            shape = tuple(-(-size // LANES) * LANES for size in arg.shape)
            specs.append(pl.BlockSpec(shape, lambda i: (0, 0)))
        else:
            specs.append(pl.BlockSpec(arg.shape, lambda i: (0, 0)))
    out_specs = []
    for n, out in enumerate(outs):
        block = out.shape if blocks is None or blocks[n] is None else blocks[n]
        out_specs.append(pl.BlockSpec(block, lambda i: (0, 0)))
    return pl.pallas_call(
        kernel,
        grid=(1,),
        in_specs=specs,
        out_specs=out_specs,
        out_shape=outs,
        scratch_shapes=scratch,
        compiler_params=pltpu.CompilerParams(vmem_limit_bytes=limit * MIB),
    )(*args)


def shape_of(shape, dtype=BF16):
    return jax.ShapeDtypeStruct(shape, dtype)


def shift(value, axis, steps):
    count = lax.axis_size(axis)
    pairs = [(source, (source + steps) % count) for source in range(count)]
    return lax.ppermute(value, axis, pairs)


def shift_both(value, steps_col, steps_row):
    columns, rows = lax.axis_size("col"), lax.axis_size("row")
    pairs = []
    for x in range(columns):
        for y in range(rows):
            target = (x + steps_col) % columns * rows + (y + steps_row) % rows
            pairs.append((x * rows + y, target))
    return lax.ppermute(value, ("col", "row"), pairs)


def body(c1, c2, c4, t1, t2, t3, t4, tensors, pattern, below, above, right, left):
    bond = c1.shape[0]
    site = t1.shape[1] // bond
    square = site * site
    tall = site * LANES
    bond_rows = -(-bond // ROWS) * ROWS
    rows_shape = (bond_rows * SLOT, LANES)
    padded = -(-site * bond // LANES) * LANES

    t1_up, c1_up = shift(t1, "row", -1), shift(c1, "row", -1)
    t3_down, c4_down = shift(t3, "row", 1), shift(c4, "row", 1)
    t2_back, c2_back = shift(t2, "col", 1), shift(c2, "col", 1)

    rows, columns = places(site)
    height, depth = rows.shape[1], columns.shape[1]
    full = lambda shape: pl.BlockSpec(shape, lambda i, pattern: (0, 0))
    tensor_left, tensor_top = pl.pallas_call(
        arrange_kernel,
        grid_spec=pltpu.PrefetchScalarGridSpec(
            num_scalar_prefetch=1,
            grid=(1,),
            in_specs=[
                pl.BlockSpec((None, square, square), lambda i, pattern: (pattern[0], 0, 0)),
                full((height, 1)),
                full((1, depth)),
                full((height, 1)),
                full((1, depth)),
            ],
            out_specs=[full((height, depth)), full((height, depth))],
        ),
        out_shape=[shape_of((height, depth)), shape_of((height, depth))],
        compiler_params=pltpu.CompilerParams(vmem_limit_bytes=24 * MIB),
    )(
        pattern.reshape(1),
        tensors,
        rows[0].reshape(height, 1),
        columns[0].reshape(1, depth),
        rows[1].reshape(height, 1),
        columns[1].reshape(1, depth),
    )

    wide = shape_of((LANES, tall))
    stack = shape_of((tall, LANES))
    stack_f32 = shape_of((tall, LANES), F32)
    half = pltpu.VMEM((tall, LANES), F32)
    frame_scratch = pltpu.VMEM(rows_shape, F32)
    corner = shape_of((bond, bond))

    (t1_wide, t4_wide, upper, upper_sketch, lower, lower_sketch, side, side_sketch) = call(
        functools.partial(prepare_kernel, bond, site),
        (c1, t1, c4, t3, c2, t2, t4, above, below, right),
        [wide, wide, stack, stack_f32, stack, stack_f32, stack, stack_f32],
        [half],
        40,
    )
    rows_left, spare_left, frame_below, corner_top, corner_bottom = call(
        functools.partial(vertical_kernel, bond, site),
        (c1_up, t1_up, c4_down, t3_down, above, below, upper, upper_sketch, lower, lower_sketch),
        [shape_of(rows_shape), shape_of(rows_shape), stack, corner, corner],
        [half, half, half, frame_scratch, frame_scratch],
        40,
    )

    def absorb(rows_in, spare_in, edge, tensor, frame_out):
        main = site - 1
        return call(
            functools.partial(absorb_kernel, bond, site),
            (rows_in, spare_in, edge, tensor, frame_out),
            [shape_of((bond, site * bond)), wide],
            [
                pltpu.VMEM((main * SLOT, GROUP * LANES), BF16),
                pltpu.VMEM((GROUP * main, tall), BF16),
                pltpu.VMEM((tall, LANES), F32),
                pltpu.VMEM((LANES * main, LANES), F32),
            ],
            48,
            [(LANES, padded), None],
        )

    edge_new, edge_wide = absorb(rows_left, spare_left, t4_wide, tensor_left, frame_below)
    left_corner = shift(corner_top, "col", 1)
    left_bottom = shift(corner_bottom, "col", 1)
    left_edge = shift(edge_new, "col", 1)

    inverse, frame_right, corner_left, corner_right = call(
        functools.partial(horizontal_kernel, bond, site),
        (corner_top, edge_wide, left, side, side_sketch),
        [shape_of((LANES, LANES), F32), stack, corner, corner],
        [half, half],
        32,
    )
    inverse_back = shift(inverse, "col", 1)
    top_left = shift_both(corner_left, 1, 1)
    top_right = shift(corner_right, "row", 1)
    (side_back,) = call(
        functools.partial(side_kernel, bond, site), (c2_back, t2_back, right), [stack_f32], [half], 32
    )
    rows_top, spare_top = call(
        functools.partial(arrive_kernel, bond, site),
        (left_corner, left_edge, left, side_back, inverse_back),
        [shape_of(rows_shape), shape_of(rows_shape)],
        [half, half, frame_scratch, frame_scratch],
        40,
    )
    top_new, _ = absorb(rows_top, spare_top, t1_wide, tensor_top, frame_right)
    top_edge = shift(top_new, "row", 1)
    return (left_corner, left_edge, left_bottom, top_left, top_edge, top_right)


def solution(mesh):
    block, whole = P("col", "row"), P()
    in_specs = (block,) * 7 + (whole, block) + (whole,) * 4
    return jax.shard_map(
        body, mesh=mesh, in_specs=in_specs, out_specs=(block,) * 6, check_vma=False
    )
```

```python
import functools

import jax
import jax.numpy as jnp
import numpy as np
from jax import lax
from jax.experimental import pallas as pl
from jax.experimental.pallas import tpu as pltpu
from jax.sharding import PartitionSpec as P

LANES = 128
ROWS = 8
SLOT = 32
GROUP = 20
QUARTERS = 4
MIB = 1 << 20
F32 = jnp.float32
BF16 = jnp.bfloat16

NN = (((1,), (0,)), ((), ()))
NT = (((1,), (1,)), ((), ()))
TN = (((0,), (0,)), ((), ()))


def product(left, right, dims=NN):
    return lax.dot_general(left, right, dims, preferred_element_type=F32)


def halves(values):
    high = values.astype(BF16)
    return high, (values - high.astype(F32)).astype(BF16)


def product_split(left, right, dims=NN):
    left_high, left_low = halves(left)
    right_high, right_low = halves(right)
    axis_left, axis_right = dims[0][0][0], dims[0][1][0]
    both = jnp.concatenate([left_high, left_low], axis_left)
    twice = jnp.concatenate([right_high, right_high], axis_right)
    return product(both, twice, dims) + product(left_high, right_low, dims)


def index_of(shape, axis):
    return lax.broadcasted_iota(jnp.int32, shape, axis)


def square_of(ref, bond):
    shape = (LANES, LANES)
    keep = (index_of(shape, 0) < bond) & (index_of(shape, 1) < bond)
    return jnp.where(keep, ref[...].astype(F32), 0.0)


def spread(ref, bond, site):
    shape = (LANES, LANES)
    row, lane = index_of(shape, 0), index_of(shape, 1)
    keep = (row < bond) & (lane < bond)
    pieces = []
    for k in range(site):
        tile, offset = divmod(k * bond, LANES)
        piece = ref[:, tile * LANES : (tile + 1) * LANES].astype(F32)
        if offset:
            piece = pltpu.roll(piece, LANES - offset, 1)
        if offset + bond > LANES:
            more = ref[:, (tile + 1) * LANES : (tile + 2) * LANES].astype(F32)
            piece = jnp.where(lane < LANES - offset, piece, pltpu.roll(more, LANES - offset, 1))
        pieces.append(jnp.where(keep, piece, 0.0).astype(BF16))
    return pieces


def gather_dense(tiles, ref, bond):
    lane = index_of((LANES, LANES), 1)
    total = len(tiles) * bond
    for tile in range(-(-total // LANES)):
        begin = tile * LANES
        value = None
        for k in range(begin // bond, min(len(tiles) - 1, (begin + LANES - 1) // bond) + 1):
            shift = k * bond - begin
            piece = pltpu.roll(tiles[k], shift % LANES, 1) if shift % LANES else tiles[k]
            value = piece if value is None else jnp.where(lane >= shift, piece, value)
        ref[:, begin : begin + LANES] = value.astype(ref.dtype)


def pack(tiles, ref, bond):
    quarter = bond // QUARTERS
    lane = index_of((LANES, LANES), 1)
    for group in range(len(tiles) // (QUARTERS + 1)):
        first = group * (QUARTERS + 1)
        for m in range(QUARTERS):
            piece = pltpu.roll(tiles[first + QUARTERS], bond - m * quarter, 1)
            slot = group * QUARTERS + m
            value = jnp.where(lane < bond, tiles[first + m], piece)
            ref[:, slot * LANES : (slot + 1) * LANES] = value.astype(ref.dtype)


def unpack(ref, bond, site):
    quarter = bond // QUARTERS
    shape = (LANES, LANES)
    row, lane = index_of(shape, 0), index_of(shape, 1)
    keep = (row < bond) & (lane < bond)
    tiles = []
    for group in range(site // (QUARTERS + 1)):
        last = None
        for m in range(QUARTERS):
            slot = group * QUARTERS + m
            value = ref[:, slot * LANES : (slot + 1) * LANES].astype(F32)
            tiles.append(jnp.where(keep, value, 0.0).astype(BF16))
            piece = pltpu.roll(value, LANES - bond + m * quarter, 1)
            last = piece if last is None else jnp.where(lane >= m * quarter, piece, last)
        tiles.append(jnp.where(keep, last, 0.0).astype(BF16))
    return tiles


def sketched(stack, sketch):
    return product(jnp.concatenate([stack, stack], 1), jnp.concatenate(halves(sketch), 0))


def inverse_factors(grams, bond):
    count = -(-bond // ROWS) * ROWS
    shape = (count, LANES)
    row, lane = index_of(shape, 0), index_of(shape, 1)
    inside = (row < bond) & (lane < bond)
    eye = jnp.where(row == lane, 1.0, 0.0)
    work = [jnp.where(inside, gram[:count], eye) for gram in grams]
    done = [[] for _ in grams]
    for first in range(0, count, ROWS):
        height = count - first
        row, lane = index_of((height, LANES), 0), index_of((height, LANES), 1)
        block = (lane >= first) & (lane < first + ROWS)
        start = jnp.where(row == lane - first, 1.0, 0.0)
        small_row, small_lane = index_of((ROWS, LANES), 0), index_of((ROWS, LANES), 1)
        columns = []
        for n, matrix in enumerate(work):
            columns.append(
                [
                    jnp.broadcast_to(matrix[:, first + j : first + j + 1], (height, LANES))
                    for j in range(ROWS)
                ]
            )
            work[n] = jnp.where(block, start, matrix)
        pivots = [jnp.ones((ROWS, LANES), F32) for _ in work]
        for j in range(ROWS):
            for n in range(len(work)):
                column = columns[n]
                pivot = column[j][j : j + 1, :]
                factor = jnp.where(row > j, column[j] * (1.0 / pivot), 0.0)
                work[n] = work[n] - factor * work[n][j : j + 1, :]
                for later in range(j + 1, ROWS):
                    column[later] = column[later] - factor * column[later][j : j + 1, :]
                pivots[n] = jnp.where(small_row == j, pivot, pivots[n])
        for n in range(len(work)):
            scaled = work[n][:ROWS] * lax.rsqrt(pivots[n])
            done[n].append(jnp.where(small_lane <= small_row + first, scaled, 0.0))
            work[n] = work[n][ROWS:]
    tail = jnp.zeros((LANES - count, LANES), F32)
    keep = (index_of((LANES, LANES), 0) < bond) & (index_of((LANES, LANES), 1) < bond)
    return [jnp.where(keep, jnp.concatenate(parts + [tail], 0), 0.0) for parts in done]


def gram_of(values):
    high, low = halves(values)
    both = product(high, jnp.concatenate([high, low], 1), TN)
    mixed = both[:, LANES:]
    return both[:, :LANES] + mixed + mixed.T


def scaled_corner(values, bond):
    mean = jnp.sum(values * values) / (bond * bond)
    return (values / jnp.sqrt(mean + 1e-06)).astype(BF16)


def half_tiles(corner, pieces):
    return [product(corner, piece) for piece in pieces]


def fill(stack, tiles):
    for k, tile in enumerate(tiles):
        stack[k * LANES : (k + 1) * LANES, :] = tile.astype(stack.dtype)


def store_frame_rows(inverse, sketched_ref, rows_ref, spare_ref, plain, moved, site):
    plain[...] = jnp.zeros_like(plain)
    moved[...] = jnp.zeros_like(moved)
    bond_rows = plain.shape[0] // SLOT
    for k in range(site):
        tile = product_split(inverse, sketched_ref[k * LANES : (k + 1) * LANES, :], NT)
        place = ROWS * (k // (ROWS - 1)) + 1 + k % (ROWS - 1)
        plain[pl.ds(k, bond_rows, stride=SLOT), :] = tile[:bond_rows]
        moved[pl.ds(place, bond_rows, stride=SLOT), :] = tile[:bond_rows]
    rows_ref[...] = plain[...].astype(BF16)
    spare_ref[...] = moved[...].astype(BF16)


def halves_kernel(bond, site, c1, t1, c4, t3, upper_packed, lower_packed, upper, lower):
    for corner, edge, packed, stack in ((c1, t1, upper_packed, upper), (c4, t3, lower_packed, lower)):
        tiles = half_tiles(square_of(corner, bond).astype(BF16), spread(edge, bond, site))
        fill(stack, tiles)
        pack(tiles, packed, bond)


def prepare_kernel(
    bond, site, c2, t2, t4, above, below, right, upper, lower,
    t4_wide, upper_sketch, lower_sketch, side_packed, side, side_sketch,
):
    for k, piece in enumerate(spread(t4, bond, site)):
        t4_wide[:, k * LANES : (k + 1) * LANES] = piece
    tiles = half_tiles(square_of(c2, bond).astype(BF16), spread(t2, bond, site))
    fill(side, tiles)
    pack(tiles, side_packed, bond)
    upper_sketch[...] = sketched(upper[...], square_of(above, bond))
    lower_sketch[...] = sketched(lower[...], square_of(below, bond))
    side_sketch[...] = sketched(side[...], square_of(right, bond))


def vertical_kernel(
    bond, site, upper_packed, lower_packed, above, below, upper, upper_sketch, lower, lower_sketch,
    t1, side_packed, rows_ref, spare_ref, frame_out, corner_top, corner_bottom, t1_out, side_out,
    stack, over, under, plain, moved,
):
    t1_out[...] = t1[...]
    side_out[...] = side_packed[...]
    fill(stack, unpack(upper_packed, bond, site))
    under[...] = lower_sketch[...] + sketched(stack[...], square_of(above, bond))
    fill(stack, unpack(lower_packed, bond, site))
    over[...] = upper_sketch[...] + sketched(stack[...], square_of(below, bond))
    grams = [gram_of(over[...]), gram_of(under[...])]
    inverse_over, inverse_under = inverse_factors(grams, bond)
    store_frame_rows(inverse_over, over, rows_ref, spare_ref, plain, moved, site)
    frame_out[...] = product_split(under[...], inverse_under, NT).astype(BF16)
    corner_top[...] = scaled_corner(frame_rows_times(plain, upper, site), bond)
    corner_bottom[...] = scaled_corner(product(frame_out[...], lower[...], TN), bond)


def frame_rows_times(plain, stack, site):
    bond_rows = plain.shape[0] // SLOT
    total = jnp.zeros((bond_rows, LANES), F32)
    for k in range(site):
        piece = plain[pl.ds(k, bond_rows, stride=SLOT), :].astype(BF16)
        total = total + product(piece, stack[k * LANES : (k + 1) * LANES, :])
    return jnp.concatenate([total, jnp.zeros((LANES - bond_rows, LANES), F32)], 0)


def horizontal_kernel(
    bond, site, c1, edge, left, side, side_sketch, inverse_ref, frame_out, half, total
):
    corner = square_of(c1, bond).T.astype(BF16)
    for k in range(site):
        half[k * LANES : (k + 1) * LANES, :] = product(corner, edge[:, k * LANES : (k + 1) * LANES])
    total[...] = side_sketch[...] + product_split(half[...], square_of(left, bond))
    (inverse,) = inverse_factors([gram_of(total[...])], bond)
    inverse_ref[...] = inverse
    frame = product_split(total[...], inverse, NT).astype(BF16)
    tall = site * LANES
    frame_out[:tall, :] = frame
    frame_out[tall:, :] = scaled_corner(product(frame, side[...], TN), bond)


def arrive_kernel(
    bond, site, payload, side_packed, left, right, inverse_ref, t1,
    rows_ref, spare_ref, corner_left, t1_wide, half, total, stack, plain, moved,
):
    for k, piece in enumerate(spread(t1, bond, site)):
        t1_wide[:, k * LANES : (k + 1) * LANES] = piece
    fill(stack, unpack(side_packed, bond, site))
    total[...] = sketched(stack[...], square_of(right, bond))
    start = payload.shape[1] - LANES
    corner = square_of(payload.at[:, start:], bond).T.astype(BF16)
    fill(half, half_tiles(corner, spread(payload, bond, site)))
    total[...] = total[...] + product_split(half[...], square_of(left, bond))
    store_frame_rows(inverse_ref[...], total, rows_ref, spare_ref, plain, moved, site)
    fill(stack, [half[k * LANES : (k + 1) * LANES, :] for k in range(site)])
    corner_left[...] = scaled_corner(frame_rows_times(plain, stack, site).T, bond)


def finish_kernel(bond, payload, bottom, frame, left_corner, left_edge, left_bottom, top_right):
    start = payload.shape[1] - LANES
    left_edge[...] = payload[:, :start]
    left_corner[...] = payload[:, start:]
    left_bottom[...] = bottom[...]
    top_right[...] = frame[frame.shape[0] - LANES :, :]


def absorb_kernel(bond, site, first, rows_ref, spare_ref, edge, tensor, frame_out, *refs):
    mixed, pushed, last, result = refs[-4:]
    if first:
        corner, dense, wide = refs[:3]
    else:
        dense = refs[0]
    main = site - 1
    tall = site * LANES
    last[...] = jnp.zeros_like(last)
    result[bond * main :, :] = jnp.zeros((result.shape[0] - bond * main, LANES), F32)

    def step(group, carry):
        begin = pl.multiple_of(group * (GROUP * SLOT), GROUP * SLOT)
        frame = rows_ref[pl.ds(begin, GROUP * SLOT), :]
        spare = product(
            spare_ref[pl.ds(begin, GROUP * SLOT), :], edge[:, main * LANES : site * LANES]
        )
        for pair in range(main // 2):
            both = product(frame, edge[:, 2 * pair * LANES : (2 * pair + 2) * LANES])
            for side in range(2):
                j = 2 * pair + side
                for p in range(GROUP):
                    tile = both[p * SLOT : (p + 1) * SLOT, side * LANES : (side + 1) * LANES]
                    if j * (ROWS - 1) < site:
                        extra = spare[p * SLOT + j * ROWS : p * SLOT + (j + 1) * ROWS, :]
                        tile = jnp.concatenate([tile[: SLOT - ROWS], tile[SLOT - ROWS :] + extra], 0)
                    mixed[j * SLOT : (j + 1) * SLOT, p * LANES : (p + 1) * LANES] = tile.astype(BF16)
        for pair in range(GROUP // 2):
            out = product(tensor[...], mixed[:, 2 * pair * LANES : (2 * pair + 2) * LANES])
            for k in range(site):
                parts = [
                    out[k * main : (k + 1) * main, side * LANES : (side + 1) * LANES]
                    for side in range(2)
                ]
                pushed[2 * pair * main : (2 * pair + 2) * main, k * LANES : (k + 1) * LANES] = (
                    jnp.concatenate(parts, 0).astype(BF16)
                )
            for side in range(2):
                place = group * GROUP + 2 * pair + side
                last[pl.ds(place, site, stride=LANES), :] = out[
                    site * main : site * main + site, side * LANES : (side + 1) * LANES
                ]
        place = pl.multiple_of(group * (GROUP * main), GROUP * main)
        result[pl.ds(place, GROUP * main), :] = product(pushed[...], frame_out[:tall, :])
        return carry

    lax.fori_loop(0, bond // GROUP, step, 0)
    tiles = [result[pl.ds(k, LANES, stride=main), :] for k in range(main)]
    joined = jnp.concatenate(
        [last[k * LANES : (k + 1) * LANES, :].astype(BF16) for k in range(site)], 1
    )
    tiles.append(product(joined, frame_out[:tall, :]))
    squares = tiles[0] * tiles[0]
    for tile in tiles[1:]:
        squares = squares + tile * tile
    scale = 1.0 / jnp.sqrt(jnp.sum(squares) / (bond * bond * site) + 1e-06)
    tiles = [tile * scale for tile in tiles]
    gather_dense(tiles, dense, bond)
    if first:
        for k, tile in enumerate(tiles):
            wide[:, k * LANES : (k + 1) * LANES] = tile.astype(BF16)
        dense[:, dense.shape[1] - LANES :] = square_of(corner, bond).astype(BF16)


def arrange_kernel(pattern, tensors, rows, columns, out, tensor, semaphore):
    copy = pltpu.make_async_copy(tensors.at[pattern[0]], tensor, semaphore)
    copy.start()
    square = tensor.shape[0]
    pick_rows = jnp.where(index_of((rows.shape[0], square), 1) == rows[...], 1.0, 0.0).astype(BF16)
    pick_columns = jnp.where(index_of((square, columns.shape[1]), 0) == columns[...], 1.0, 0.0)
    copy.wait()
    turned = product(pick_rows, tensor[...], NT).astype(BF16)
    out[...] = product(turned, pick_columns.astype(BF16)).astype(BF16)


def places(site):
    main = site - 1
    height = -(-site * site // 16) * 16
    rows = np.full((2, height), -1, np.int32)
    columns = np.full((2, main * SLOT), -1, np.int32)
    for summed in range(site):
        for kept in range(site):
            at = summed * main + kept if kept < main else site * main + summed
            rows[0, at] = summed * site + kept
            rows[1, at] = kept * site + summed
    for edge in range(site):
        for frame in range(site):
            if edge < main:
                at = edge * SLOT + frame
            else:
                slot, offset = divmod(frame, ROWS - 1)
                at = slot * SLOT + SLOT - ROWS + 1 + offset
            columns[0, at] = frame * site + edge
            columns[1, at] = edge * site + frame
    return rows, columns


def block_of(shape):
    if shape[0] % 16 == 0 and shape[1] % LANES == 0:
        return pl.BlockSpec(memory_space=pltpu.VMEM)
    return pl.BlockSpec(tuple(-(-size // LANES) * LANES for size in shape), lambda i: (0, 0))


def call(kernel, args, outs, scratch, limit):
    return pl.pallas_call(
        kernel,
        grid=(1,),
        in_specs=[block_of(arg.shape) for arg in args],
        out_specs=[block_of(out.shape) for out in outs],
        out_shape=outs,
        scratch_shapes=scratch,
        compiler_params=pltpu.CompilerParams(vmem_limit_bytes=limit * MIB),
    )(*args)


def shape_of(shape, dtype=BF16):
    return jax.ShapeDtypeStruct(shape, dtype)


def shift(value, axis, steps):
    count = lax.axis_size(axis)
    pairs = [(source, (source + steps) % count) for source in range(count)]
    return lax.ppermute(value, axis, pairs)


def shift_both(value, steps_col, steps_row):
    columns, rows = lax.axis_size("col"), lax.axis_size("row")
    pairs = []
    for x in range(columns):
        for y in range(rows):
            target = (x + steps_col) % columns * rows + (y + steps_row) % rows
            pairs.append((x * rows + y, target))
    return lax.ppermute(value, ("col", "row"), pairs)


def body(c1, c2, c4, t1, t2, t3, t4, tensors, pattern, below, above, right, left):
    bond = c1.shape[0]
    site = t1.shape[1] // bond
    square = site * site
    tall = site * LANES
    bond_rows = -(-bond // ROWS) * ROWS
    frame_rows = shape_of((bond_rows * SLOT, LANES))
    packed = shape_of((bond, site // (QUARTERS + 1) * QUARTERS * LANES))
    dense = shape_of((bond, site * bond))
    wide = shape_of((LANES, tall))
    stack = shape_of((tall, LANES))
    stack_f32 = shape_of((tall, LANES), F32)
    corner = shape_of((bond, bond))
    payload = shape_of((bond, -(-site * bond // LANES) * LANES + LANES))
    half = pltpu.VMEM((tall, LANES), F32)
    half_bf16 = pltpu.VMEM((tall, LANES), BF16)
    frame_scratch = pltpu.VMEM(frame_rows.shape, F32)
    rows, columns = places(site)

    def arrange(which, index):
        height, depth = rows.shape[1], columns.shape[1]
        vmem = pl.BlockSpec(memory_space=pltpu.VMEM)
        return pl.pallas_call(
            arrange_kernel,
            in_specs=[
                pl.BlockSpec(memory_space=pltpu.SMEM),
                pl.BlockSpec(memory_space=pltpu.HBM),
                vmem,
                vmem,
            ],
            out_specs=vmem,
            out_shape=shape_of((height, depth)),
            scratch_shapes=[pltpu.VMEM((square, square), BF16), pltpu.SemaphoreType.DMA],
            compiler_params=pltpu.CompilerParams(vmem_limit_bytes=16 * MIB),
        )(
            index.reshape(1),
            tensors,
            rows[which].reshape(height, 1),
            columns[which].reshape(1, depth),
        )

    def absorb(first, rows_in, spare_in, edge, tensor, frame_out, *more):
        main = site - 1
        return call(
            functools.partial(absorb_kernel, bond, site, first),
            (rows_in, spare_in, edge, tensor, frame_out) + more,
            [payload, wide] if first else [dense],
            [
                pltpu.VMEM((main * SLOT, GROUP * LANES), BF16),
                pltpu.VMEM((GROUP * main, tall), BF16),
                pltpu.VMEM((tall, LANES), F32),
                pltpu.VMEM((LANES * main, LANES), F32),
            ],
            36,
        )

    upper_packed, lower_packed, upper, lower = call(
        functools.partial(halves_kernel, bond, site),
        (c1, t1, c4, t3),
        [packed, packed, stack, stack],
        [],
        24,
    )
    upper_next = shift(upper_packed, "row", -1)
    lower_back = shift(lower_packed, "row", 1)
    pattern_back = shift(pattern, "row", 1)
    tensor_left = arrange(0, pattern)
    t4_wide, upper_sketch, lower_sketch, side_packed, side, side_sketch = call(
        functools.partial(prepare_kernel, bond, site),
        (c2, t2, t4, above, below, right, upper, lower),
        [wide, stack_f32, stack_f32, packed, stack, stack_f32],
        [],
        24,
    )
    rows_left, spare_left, frame_below, corner_top, corner_bottom, t1_held, side_held = call(
        functools.partial(vertical_kernel, bond, site),
        (upper_next, lower_back, above, below, upper, upper_sketch, lower, lower_sketch, t1, side_packed),
        [frame_rows, frame_rows, stack, corner, corner, dense, packed],
        [half_bf16, half, half, frame_scratch, frame_scratch],
        32,
    )
    t1_back = shift(t1_held, "row", 1)
    side_back = shift_both(side_held, 1, 1)
    left_new, edge_wide = absorb(
        True, rows_left, spare_left, t4_wide, tensor_left, frame_below, corner_top
    )
    left_back = shift_both(left_new, 1, 1)
    inverse, frame_right = call(
        functools.partial(horizontal_kernel, bond, site),
        (corner_top, edge_wide, left, side, side_sketch),
        [shape_of((LANES, LANES), F32), shape_of((tall + LANES, LANES))],
        [half, half],
        32,
    )
    inverse_back = shift_both(inverse, 1, 1)
    frame_back = shift(frame_right, "row", 1)
    left_here = shift(left_new, "col", 1)
    bottom_here = shift(corner_bottom, "col", 1)
    tensor_top = arrange(1, pattern_back)
    rows_top, spare_top, top_left, t1_wide = call(
        functools.partial(arrive_kernel, bond, site),
        (left_back, side_back, left, right, inverse_back, t1_back),
        [frame_rows, frame_rows, corner, wide],
        [half, half, half_bf16, frame_scratch, frame_scratch],
        32,
    )
    (top_edge,) = absorb(False, rows_top, spare_top, t1_wide, tensor_top, frame_back)
    left_corner, left_edge, left_bottom, top_right = call(
        functools.partial(finish_kernel, bond),
        (left_here, bottom_here, frame_back),
        [corner, dense, corner, corner],
        [],
        16,
    )
    return (left_corner, left_edge, left_bottom, top_left, top_edge, top_right)


def solution(mesh):
    block, whole = P("col", "row"), P()
    in_specs = (block,) * 7 + (whole, block) + (whole,) * 4
    return jax.shard_map(
        body, mesh=mesh, in_specs=in_specs, out_specs=(block,) * 6, check_vma=False
    )
```

```python
import functools

import jax
import jax.numpy as jnp
import numpy as np
from jax import lax
from jax.experimental import pallas as pl
from jax.experimental.pallas import tpu as pltpu
from jax.sharding import PartitionSpec as P

LANES = 128
ROWS = 8
SLOT = 32
GROUP = 50
PAIRS = 5
STEPS = 5
QUARTERS = 4
MIB = 1 << 20
F32 = jnp.float32
BF16 = jnp.bfloat16

NN = (((1,), (0,)), ((), ()))
NT = (((1,), (1,)), ((), ()))
TN = (((0,), (0,)), ((), ()))


def product(left, right, dims=NN):
    return lax.dot_general(left, right, dims, preferred_element_type=F32)


def halves(values):
    high = values.astype(BF16)
    return high, (values - high.astype(F32)).astype(BF16)


def product_split(left, right, dims=NN):
    left_high, left_low = halves(left)
    right_high, right_low = halves(right)
    axis_left, axis_right = dims[0][0][0], dims[0][1][0]
    both = jnp.concatenate([left_high, left_low], axis_left)
    twice = jnp.concatenate([right_high, right_high], axis_right)
    return product(both, twice, dims) + product(left_high, right_low, dims)


def index_of(shape, axis):
    return lax.broadcasted_iota(jnp.int32, shape, axis)


def square_of(ref, bond):
    shape = (LANES, LANES)
    keep = (index_of(shape, 0) < bond) & (index_of(shape, 1) < bond)
    return jnp.where(keep, ref[...].astype(F32), 0.0)


def spread(ref, bond, site):
    shape = (LANES, LANES)
    row, lane = index_of(shape, 0), index_of(shape, 1)
    keep = (row < bond) & (lane < bond)
    pieces = []
    for k in range(site):
        tile, offset = divmod(k * bond, LANES)
        piece = ref[:, tile * LANES : (tile + 1) * LANES].astype(F32)
        if offset:
            piece = pltpu.roll(piece, LANES - offset, 1)
        if offset + bond > LANES:
            more = ref[:, (tile + 1) * LANES : (tile + 2) * LANES].astype(F32)
            piece = jnp.where(lane < LANES - offset, piece, pltpu.roll(more, LANES - offset, 1))
        pieces.append(jnp.where(keep, piece, 0.0).astype(BF16))
    return pieces


def gather_dense(tiles, ref, bond):
    lane = index_of((LANES, LANES), 1)
    total = len(tiles) * bond
    for tile in range(-(-total // LANES)):
        begin = tile * LANES
        value = None
        for k in range(begin // bond, min(len(tiles) - 1, (begin + LANES - 1) // bond) + 1):
            shift = k * bond - begin
            piece = pltpu.roll(tiles[k], shift % LANES, 1) if shift % LANES else tiles[k]
            value = piece if value is None else jnp.where(lane >= shift, piece, value)
        ref[:, begin : begin + LANES] = value.astype(ref.dtype)


def pack(tiles, ref, bond):
    quarter = bond // QUARTERS
    lane = index_of((LANES, LANES), 1)
    for group in range(len(tiles) // (QUARTERS + 1)):
        first = group * (QUARTERS + 1)
        for m in range(QUARTERS):
            piece = pltpu.roll(tiles[first + QUARTERS], bond - m * quarter, 1)
            slot = group * QUARTERS + m
            value = jnp.where(lane < bond, tiles[first + m], piece)
            ref[:, slot * LANES : (slot + 1) * LANES] = value.astype(ref.dtype)


def unpack(ref, bond, site):
    quarter = bond // QUARTERS
    shape = (LANES, LANES)
    row, lane = index_of(shape, 0), index_of(shape, 1)
    keep = (row < bond) & (lane < bond)
    tiles = []
    for group in range(site // (QUARTERS + 1)):
        last = None
        for m in range(QUARTERS):
            slot = group * QUARTERS + m
            value = ref[:, slot * LANES : (slot + 1) * LANES].astype(F32)
            tiles.append(jnp.where(keep, value, 0.0).astype(BF16))
            piece = pltpu.roll(value, LANES - bond + m * quarter, 1)
            last = piece if last is None else jnp.where(lane >= m * quarter, piece, last)
        tiles.append(jnp.where(keep, last, 0.0).astype(BF16))
    return tiles


def sketched(stack, sketch):
    return product(jnp.concatenate([stack, stack], 1), jnp.concatenate(halves(sketch), 0))


def inverse_factors(grams, bond):
    count = -(-bond // ROWS) * ROWS
    shape = (count, LANES)
    row, lane = index_of(shape, 0), index_of(shape, 1)
    inside = (row < bond) & (lane < bond)
    eye = jnp.where(row == lane, 1.0, 0.0)
    work = [jnp.where(inside, gram[:count], eye) for gram in grams]
    done = [[] for _ in grams]
    for first in range(0, count, ROWS):
        height = count - first
        row, lane = index_of((height, LANES), 0), index_of((height, LANES), 1)
        block = (lane >= first) & (lane < first + ROWS)
        start = jnp.where(row == lane - first, 1.0, 0.0)
        small_row, small_lane = index_of((ROWS, LANES), 0), index_of((ROWS, LANES), 1)
        columns = []
        for n, matrix in enumerate(work):
            columns.append(
                [
                    jnp.broadcast_to(matrix[:, first + j : first + j + 1], (height, LANES))
                    for j in range(ROWS)
                ]
            )
            work[n] = jnp.where(block, start, matrix)
        pivots = [jnp.ones((ROWS, LANES), F32) for _ in work]
        for j in range(ROWS):
            for n in range(len(work)):
                column = columns[n]
                pivot = column[j][j : j + 1, :]
                factor = jnp.where(row > j, column[j] * (1.0 / pivot), 0.0)
                work[n] = work[n] - factor * work[n][j : j + 1, :]
                for later in range(j + 1, ROWS):
                    column[later] = column[later] - factor * column[later][j : j + 1, :]
                pivots[n] = jnp.where(small_row == j, pivot, pivots[n])
        for n in range(len(work)):
            scaled = work[n][:ROWS] * lax.rsqrt(pivots[n])
            done[n].append(jnp.where(small_lane <= small_row + first, scaled, 0.0))
            work[n] = work[n][ROWS:]
    tail = jnp.zeros((LANES - count, LANES), F32)
    keep = (index_of((LANES, LANES), 0) < bond) & (index_of((LANES, LANES), 1) < bond)
    return [jnp.where(keep, jnp.concatenate(parts + [tail], 0), 0.0) for parts in done]


def gram_of(values):
    high, low = halves(values)
    both = product(high, jnp.concatenate([high, low], 1), TN)
    mixed = both[:, LANES:]
    return both[:, :LANES] + mixed + mixed.T


def scaled_corner(values, bond):
    mean = jnp.sum(values * values) / (bond * bond)
    return (values / jnp.sqrt(mean + 1e-06)).astype(BF16)


def half_tiles(corner, pieces):
    return [product(corner, piece) for piece in pieces]


def fill(stack, tiles):
    for k, tile in enumerate(tiles):
        stack[k * LANES : (k + 1) * LANES, :] = tile.astype(stack.dtype)


def store_frame_rows(inverse, sketched_ref, rows_ref, spare_ref, plain, moved, site):
    plain[...] = jnp.zeros_like(plain)
    moved[...] = jnp.zeros_like(moved)
    bond_rows = plain.shape[0] // SLOT
    for k in range(site):
        tile = product_split(inverse, sketched_ref[k * LANES : (k + 1) * LANES, :], NT)
        place = ROWS * (k // (ROWS - 1)) + 1 + k % (ROWS - 1)
        plain[pl.ds(k, bond_rows, stride=SLOT), :] = tile[:bond_rows]
        moved[pl.ds(place, bond_rows, stride=SLOT), :] = tile[:bond_rows]
    rows_ref[...] = plain[...].astype(BF16)
    spare_ref[...] = moved[...].astype(BF16)


def halves_kernel(bond, site, c1, t1, c4, t3, upper_packed, lower_packed, upper, lower):
    for corner, edge, packed, stack in ((c1, t1, upper_packed, upper), (c4, t3, lower_packed, lower)):
        tiles = half_tiles(square_of(corner, bond).astype(BF16), spread(edge, bond, site))
        fill(stack, tiles)
        pack(tiles, packed, bond)


def prepare_kernel(
    bond, site, c2, t2, t4, above, below, right, upper, lower,
    t4_wide, upper_sketch, lower_sketch, side_packed, side, side_sketch,
):
    for k, piece in enumerate(spread(t4, bond, site)):
        t4_wide[:, k * LANES : (k + 1) * LANES] = piece
    tiles = half_tiles(square_of(c2, bond).astype(BF16), spread(t2, bond, site))
    fill(side, tiles)
    pack(tiles, side_packed, bond)
    upper_sketch[...] = sketched(upper[...], square_of(above, bond))
    lower_sketch[...] = sketched(lower[...], square_of(below, bond))
    side_sketch[...] = sketched(side[...], square_of(right, bond))


def vertical_kernel(
    bond, site, upper_packed, lower_packed, above, below, upper, upper_sketch, lower, lower_sketch,
    t1, side_packed, pattern, rows_ref, spare_ref, frame_out, corner_top, corner_bottom, t1_out,
    side_out, pattern_out, stack, over, under, plain, moved,
):
    t1_out[...] = t1[...]
    pattern_out[0] = pattern[0]
    side_out[...] = side_packed[...]
    fill(stack, unpack(upper_packed, bond, site))
    under[...] = lower_sketch[...] + sketched(stack[...], square_of(above, bond))
    fill(stack, unpack(lower_packed, bond, site))
    over[...] = upper_sketch[...] + sketched(stack[...], square_of(below, bond))
    grams = [gram_of(over[...]), gram_of(under[...])]
    inverse_over, inverse_under = inverse_factors(grams, bond)
    store_frame_rows(inverse_over, over, rows_ref, spare_ref, plain, moved, site)
    frame_out[...] = product_split(under[...], inverse_under, NT).astype(BF16)
    corner_top[...] = scaled_corner(frame_rows_times(plain, upper, site), bond)
    corner_bottom[...] = scaled_corner(product(frame_out[...], lower[...], TN), bond)


def frame_rows_times(plain, stack, site):
    bond_rows = plain.shape[0] // SLOT
    total = jnp.zeros((bond_rows, LANES), F32)
    for k in range(site):
        piece = plain[pl.ds(k, bond_rows, stride=SLOT), :].astype(BF16)
        total = total + product(piece, stack[k * LANES : (k + 1) * LANES, :])
    return jnp.concatenate([total, jnp.zeros((LANES - bond_rows, LANES), F32)], 0)


def horizontal_kernel(
    bond, site, c1, edge, left, side, side_sketch, inverse_ref, frame_out, half, total
):
    corner = square_of(c1, bond).T.astype(BF16)
    for k in range(site):
        half[k * LANES : (k + 1) * LANES, :] = product(corner, edge[:, k * LANES : (k + 1) * LANES])
    total[...] = side_sketch[...] + product_split(half[...], square_of(left, bond))
    (inverse,) = inverse_factors([gram_of(total[...])], bond)
    inverse_ref[...] = inverse
    frame = product_split(total[...], inverse, NT)
    pack([frame[k * LANES : (k + 1) * LANES, :] for k in range(site)], frame_out, bond)
    corner_right = scaled_corner(product(frame.astype(BF16), side[...], TN), bond)
    frame_out[:, frame_out.shape[1] - LANES :] = corner_right


def early_kernel(bond, site, side_packed, right, t1, after, side_sketch, t1_wide, stack):
    for k, piece in enumerate(spread(t1, bond, site)):
        t1_wide[:, k * LANES : (k + 1) * LANES] = piece
    fill(stack, unpack(side_packed, bond, site))
    side_sketch[...] = sketched(stack[...], square_of(right, bond))


def arrive_kernel(
    bond, site, payload, side_sketch, left, inverse_ref,
    rows_ref, spare_ref, corner_left, half, total, stack, plain, moved,
):
    start = payload.shape[1] - LANES
    corner = square_of(payload.at[:, start:], bond).T.astype(BF16)
    fill(half, half_tiles(corner, spread(payload, bond, site)))
    total[...] = side_sketch[...] + product_split(half[...], square_of(left, bond))
    store_frame_rows(inverse_ref[...], total, rows_ref, spare_ref, plain, moved, site)
    fill(stack, [half[k * LANES : (k + 1) * LANES, :] for k in range(site)])
    corner_left[...] = scaled_corner(frame_rows_times(plain, stack, site).T, bond)


def finish_kernel(bond, payload, bottom, frame, left_corner, left_edge, left_bottom, top_right):
    start = payload.shape[1] - LANES
    left_edge[...] = payload[:, :start]
    left_corner[...] = payload[:, start:]
    left_bottom[...] = bottom[...]
    top_right[...] = frame[:, frame.shape[1] - LANES :]


def absorb_kernel(bond, site, first, rows_ref, spare_ref, edge, tensor, frame, *refs):
    mixed, pushed, last, result = refs[-4:]
    if first:
        corner, dense, wide = refs[:3]
        frame_out = frame
    else:
        dense, frame_out = refs[0], refs[1]
        fill(frame_out, unpack(frame, bond, site))
    main = site - 1
    depth = site * LANES // STEPS
    last[...] = jnp.zeros_like(last)
    result[bond * main :, :] = jnp.zeros((result.shape[0] - bond * main, LANES), F32)

    def mix(begin, j, spare):
        columns = pl.ds(pl.multiple_of(j * LANES, 2 * LANES), 2 * LANES)
        both = product(rows_ref[pl.ds(begin, GROUP * SLOT), :], edge[:, columns])
        for side in range(2):
            rows = pl.ds(pl.multiple_of((j + side) * SLOT, SLOT), SLOT)
            for p in range(GROUP):
                tile = both[p * SLOT : (p + 1) * SLOT, side * LANES : (side + 1) * LANES]
                if spare is not None:
                    at = p * SLOT + (j + side) * ROWS
                    extra = spare[at : at + ROWS, :]
                    tile = jnp.concatenate([tile[: SLOT - ROWS], tile[SLOT - ROWS :] + extra], 0)
                mixed[rows, p * LANES : (p + 1) * LANES] = tile.astype(BF16)

    def push(group, pair):
        columns = pl.ds(pl.multiple_of(pair * 2 * LANES, 2 * LANES), 2 * LANES)
        out = product(tensor[...], mixed[:, columns])
        rows = pl.ds(pl.multiple_of(pair * 2 * main, 2 * main), 2 * main)
        for k in range(site):
            parts = [
                out[k * main : (k + 1) * main, side * LANES : (side + 1) * LANES]
                for side in range(2)
            ]
            pushed[rows, k * LANES : (k + 1) * LANES] = jnp.concatenate(parts, 0).astype(BF16)
        for side in range(2):
            place = group * GROUP + 2 * pair + side
            last[pl.ds(place, site, stride=LANES), :] = out[
                site * main : site * main + site, side * LANES : (side + 1) * LANES
            ]

    def group_step(group, carry):
        begin = pl.multiple_of(group * (GROUP * SLOT), GROUP * SLOT)
        spare = product(
            spare_ref[pl.ds(begin, GROUP * SLOT), :], edge[:, main * LANES : site * LANES]
        )
        for j in range(0, QUARTERS, 2):
            mix(begin, j, spare)

        def mix_step(step, carry):
            mix(begin, step * 4, None)
            mix(begin, step * 4 + 2, None)
            return carry

        lax.fori_loop(1, main // 4, mix_step, 0)

        def push_step(step, carry):
            for pair in range(PAIRS):
                push(group, step * PAIRS + pair)
            return carry

        lax.fori_loop(0, GROUP // (2 * PAIRS), push_step, 0)
        place = pl.ds(pl.multiple_of(group * (GROUP * main), GROUP * main), GROUP * main)
        result[place, :] = product(pushed[:, :depth], frame_out[:depth, :])

        def sum_step(step, carry):
            part = pl.ds(pl.multiple_of(step * depth, depth), depth)
            result[place, :] = result[place, :] + product(pushed[:, part], frame_out[part, :])
            return carry

        lax.fori_loop(1, STEPS, sum_step, 0)
        return carry

    lax.fori_loop(0, bond // GROUP, group_step, 0)
    tiles = [result[pl.ds(k, LANES, stride=main), :] for k in range(main)]
    total = jnp.zeros((LANES, LANES), F32)
    for k in range(site):
        rows = pl.ds(k * LANES, LANES)
        total = total + product(last[rows, :].astype(BF16), frame_out[rows, :])
    tiles.append(total)
    squares = tiles[0] * tiles[0]
    for tile in tiles[1:]:
        squares = squares + tile * tile
    scale = 1.0 / jnp.sqrt(jnp.sum(squares) / (bond * bond * site) + 1e-06)
    tiles = [tile * scale for tile in tiles]
    gather_dense(tiles, dense, bond)
    if first:
        for k, tile in enumerate(tiles):
            wide[:, k * LANES : (k + 1) * LANES] = tile.astype(BF16)
        dense[:, dense.shape[1] - LANES :] = square_of(corner, bond).astype(BF16)


def arrange_kernel(pattern, tensors, rows, columns, after, out, tensor, semaphore):
    copy = pltpu.make_async_copy(tensors.at[pattern[0]], tensor, semaphore)
    copy.start()
    square = tensor.shape[0]
    pick_rows = jnp.where(index_of((rows.shape[0], square), 1) == rows[...], 1.0, 0.0).astype(BF16)
    pick_columns = jnp.where(index_of((square, columns.shape[1]), 0) == columns[...], 1.0, 0.0)
    copy.wait()
    turned = product(pick_rows, tensor[...], NT).astype(BF16)
    out[...] = product(turned, pick_columns.astype(BF16)).astype(BF16)


def places(site):
    main = site - 1
    height = -(-site * site // 16) * 16
    rows = np.full((2, height), -1, np.int32)
    columns = np.full((2, main * SLOT), -1, np.int32)
    for summed in range(site):
        for kept in range(site):
            at = summed * main + kept if kept < main else site * main + summed
            rows[0, at] = summed * site + kept
            rows[1, at] = kept * site + summed
    for edge in range(site):
        for frame in range(site):
            if edge < main:
                at = edge * SLOT + frame
            else:
                slot, offset = divmod(frame, ROWS - 1)
                at = slot * SLOT + SLOT - ROWS + 1 + offset
            columns[0, at] = frame * site + edge
            columns[1, at] = edge * site + frame
    return rows, columns


def block_of(arg):
    shape = arg.shape
    if len(shape) == 1:
        return pl.BlockSpec(memory_space=pltpu.SMEM)
    if shape[0] % 16 == 0 and shape[1] % LANES == 0:
        return pl.BlockSpec(memory_space=pltpu.VMEM)
    return pl.BlockSpec(tuple(-(-size // LANES) * LANES for size in shape), lambda i: (0, 0))


def cost(microseconds):
    return pl.CostEstimate(
        flops=microseconds * 1_000_000_000, bytes_accessed=microseconds * 1_000_000, transcendentals=0
    )


def call(kernel, args, outs, scratch, limit, microseconds, unread=0):
    specs = [block_of(arg) for arg in args]
    if unread:
        specs[-unread:] = [pl.BlockSpec(memory_space=pl.ANY)] * unread
    return pl.pallas_call(
        kernel,
        grid=(1,),
        in_specs=specs,
        out_specs=[block_of(out) for out in outs],
        out_shape=outs,
        scratch_shapes=scratch,
        compiler_params=pltpu.CompilerParams(vmem_limit_bytes=limit * MIB),
        cost_estimate=cost(microseconds),
    )(*args)


def shape_of(shape, dtype=BF16):
    return jax.ShapeDtypeStruct(shape, dtype)


def shift(value, axis, steps):
    count = lax.axis_size(axis)
    pairs = [(source, (source + steps) % count) for source in range(count)]
    return lax.ppermute(value, axis, pairs)


def shift_both(value, steps_col, steps_row):
    columns, rows = lax.axis_size("col"), lax.axis_size("row")
    pairs = []
    for x in range(columns):
        for y in range(rows):
            target = (x + steps_col) % columns * rows + (y + steps_row) % rows
            pairs.append((x * rows + y, target))
    return lax.ppermute(value, ("col", "row"), pairs)


def body(c1, c2, c4, t1, t2, t3, t4, tensors, pattern, below, above, right, left):
    bond = c1.shape[0]
    site = t1.shape[1] // bond
    square = site * site
    tall = site * LANES
    bond_rows = -(-bond // ROWS) * ROWS
    frame_rows = shape_of((bond_rows * SLOT, LANES))
    packed = shape_of((bond, site // (QUARTERS + 1) * QUARTERS * LANES))
    dense = shape_of((bond, site * bond))
    wide = shape_of((LANES, tall))
    stack = shape_of((tall, LANES))
    stack_f32 = shape_of((tall, LANES), F32)
    corner = shape_of((bond, bond))
    payload = shape_of((bond, -(-site * bond // LANES) * LANES + LANES))
    half = pltpu.VMEM((tall, LANES), F32)
    half_bf16 = pltpu.VMEM((tall, LANES), BF16)
    frame_scratch = pltpu.VMEM(frame_rows.shape, F32)
    rows, columns = places(site)

    def arrange(which, index, after):
        height, depth = rows.shape[1], columns.shape[1]
        vmem = pl.BlockSpec(memory_space=pltpu.VMEM)
        return pl.pallas_call(
            arrange_kernel,
            in_specs=[
                pl.BlockSpec(memory_space=pltpu.SMEM),
                pl.BlockSpec(memory_space=pltpu.HBM),
                vmem,
                vmem,
                pl.BlockSpec(memory_space=pl.ANY),
            ],
            out_specs=vmem,
            out_shape=shape_of((height, depth)),
            scratch_shapes=[pltpu.VMEM((square, square), BF16), pltpu.SemaphoreType.DMA],
            compiler_params=pltpu.CompilerParams(vmem_limit_bytes=16 * MIB),
            cost_estimate=cost(3),
        )(
            index,
            tensors,
            rows[which].reshape(height, 1),
            columns[which].reshape(1, depth),
            after,
        )

    def absorb(first, rows_in, spare_in, edge, tensor, frame, *more):
        main = site - 1
        return call(
            functools.partial(absorb_kernel, bond, site, first),
            (rows_in, spare_in, edge, tensor, frame) + more,
            [payload, wide] if first else [dense],
            ([] if first else [half_bf16])
            + [
                pltpu.VMEM((main * SLOT, GROUP * LANES), BF16),
                pltpu.VMEM((GROUP * main, tall), BF16),
                pltpu.VMEM((tall, LANES), F32),
                pltpu.VMEM((LANES * main, LANES), F32),
            ],
            36,
            28,
        )

    upper_packed, lower_packed, upper, lower = call(
        functools.partial(halves_kernel, bond, site),
        (c1, t1, c4, t3),
        [packed, packed, stack, stack],
        [],
        60,
        2,
    )
    upper_next = shift(upper_packed, "row", -1)
    lower_back = shift(lower_packed, "row", 1)
    pattern = pattern.reshape(1)
    pattern_back = shift(pattern, "row", 1)
    tensor_left = arrange(0, pattern, lower)
    t4_wide, upper_sketch, lower_sketch, side_packed, side, side_sketch = call(
        functools.partial(prepare_kernel, bond, site),
        (c2, t2, t4, above, below, right, upper, lower),
        [wide, stack_f32, stack_f32, packed, stack, stack_f32],
        [],
        24,
        2,
    )
    rows_left, spare_left, frame_below, corner_top, corner_bottom, t1_held, side_held, pattern_held = call(
        functools.partial(vertical_kernel, bond, site),
        (upper_next, lower_back, above, below, upper, upper_sketch, lower, lower_sketch)
        + (t1, side_packed, pattern_back),
        [frame_rows, frame_rows, stack, corner, corner, dense, packed, shape_of((1,), jnp.int32)],
        [half_bf16, half, half, frame_scratch, frame_scratch],
        32,
        10,
    )
    t1_back = shift(t1_held, "row", 1)
    side_back = shift_both(side_held, 1, 1)
    left_new, edge_wide = absorb(
        True, rows_left, spare_left, t4_wide, tensor_left, frame_below, corner_top
    )
    left_back = shift_both(left_new, 1, 1)
    inverse, frame_right = call(
        functools.partial(horizontal_kernel, bond, site),
        (corner_top, edge_wide, left, side, side_sketch),
        [shape_of((LANES, LANES), F32), shape_of((bond, packed.shape[1] + LANES))],
        [half, half],
        32,
        6,
    )
    inverse_back = shift_both(inverse, 1, 1)
    frame_back = shift(frame_right, "row", 1)
    bottom_here = shift(corner_bottom, "col", 1)
    tensor_top = arrange(1, pattern_held, inverse)
    early_sketch, t1_wide = call(
        functools.partial(early_kernel, bond, site),
        (side_back, right, t1_back, inverse),
        [stack_f32, wide],
        [half_bf16],
        24,
        2,
        1,
    )
    rows_top, spare_top, top_left = call(
        functools.partial(arrive_kernel, bond, site),
        (left_back, early_sketch, left, inverse_back),
        [frame_rows, frame_rows, corner],
        [half, half, half_bf16, frame_scratch, frame_scratch],
        32,
        4,
    )
    left_here = shift(left_back, "row", -1)
    (top_edge,) = absorb(False, rows_top, spare_top, t1_wide, tensor_top, frame_back)
    left_corner, left_edge, left_bottom, top_right = call(
        functools.partial(finish_kernel, bond),
        (left_here, bottom_here, frame_back),
        [corner, dense, corner, corner],
        [],
        16,
        1,
    )
    return (left_corner, left_edge, left_bottom, top_left, top_edge, top_right)


def solution(mesh):
    block, whole = P("col", "row"), P()
    in_specs = (block,) * 7 + (whole, block) + (whole,) * 4
    return jax.shard_map(
        body, mesh=mesh, in_specs=in_specs, out_specs=(block,) * 6, check_vma=False
    )
```

```python
import functools

import jax
import jax.numpy as jnp
import numpy as np
from jax import lax
from jax.experimental import pallas as pl
from jax.experimental.pallas import tpu as pltpu
from jax.sharding import PartitionSpec as P

LANES = 128
ROWS = 8
SLOT = 32
GROUP = 10
CUTS = 4
QUARTERS = 4
MIB = 1 << 20
F32 = jnp.float32
BF16 = jnp.bfloat16

NN = (((1,), (0,)), ((), ()))
NT = (((1,), (1,)), ((), ()))
TN = (((0,), (0,)), ((), ()))


def product(left, right, dims=NN):
    return lax.dot_general(left, right, dims, preferred_element_type=F32)


def halves(values):
    high = values.astype(BF16)
    return high, (values - high.astype(F32)).astype(BF16)


def product_split(left, right, dims=NN):
    left_high, left_low = halves(left)
    right_high, right_low = halves(right)
    axis_left, axis_right = dims[0][0][0], dims[0][1][0]
    both = jnp.concatenate([left_high, left_low], axis_left)
    twice = jnp.concatenate([right_high, right_high], axis_right)
    return product(both, twice, dims) + product(left_high, right_low, dims)


def index_of(shape, axis):
    return lax.broadcasted_iota(jnp.int32, shape, axis)


def square_of(ref, bond):
    shape = (LANES, LANES)
    keep = (index_of(shape, 0) < bond) & (index_of(shape, 1) < bond)
    return jnp.where(keep, ref[...].astype(F32), 0.0)


def spread(ref, bond, site):
    shape = (LANES, LANES)
    row, lane = index_of(shape, 0), index_of(shape, 1)
    keep = (row < bond) & (lane < bond)
    pieces = []
    for k in range(site):
        tile, offset = divmod(k * bond, LANES)
        piece = ref[:, tile * LANES : (tile + 1) * LANES].astype(F32)
        if offset:
            piece = pltpu.roll(piece, LANES - offset, 1)
        if offset + bond > LANES:
            more = ref[:, (tile + 1) * LANES : (tile + 2) * LANES].astype(F32)
            piece = jnp.where(lane < LANES - offset, piece, pltpu.roll(more, LANES - offset, 1))
        pieces.append(jnp.where(keep, piece, 0.0).astype(BF16))
    return pieces


def gather_dense(tiles, ref, bond):
    lane = index_of((LANES, LANES), 1)
    total = len(tiles) * bond
    for tile in range(-(-total // LANES)):
        begin = tile * LANES
        value = None
        for k in range(begin // bond, min(len(tiles) - 1, (begin + LANES - 1) // bond) + 1):
            shift = k * bond - begin
            piece = pltpu.roll(tiles[k], shift % LANES, 1) if shift % LANES else tiles[k]
            value = piece if value is None else jnp.where(lane >= shift, piece, value)
        ref[:, begin : begin + LANES] = value.astype(ref.dtype)


def pack(tiles, ref, bond):
    quarter = bond // QUARTERS
    lane = index_of((LANES, LANES), 1)
    for group in range(len(tiles) // (QUARTERS + 1)):
        first = group * (QUARTERS + 1)
        for m in range(QUARTERS):
            piece = pltpu.roll(tiles[first + QUARTERS], bond - m * quarter, 1)
            slot = group * QUARTERS + m
            value = jnp.where(lane < bond, tiles[first + m], piece)
            ref[:, slot * LANES : (slot + 1) * LANES] = value.astype(ref.dtype)


def unpack(ref, bond, site):
    quarter = bond // QUARTERS
    shape = (LANES, LANES)
    row, lane = index_of(shape, 0), index_of(shape, 1)
    keep = (row < bond) & (lane < bond)
    tiles = []
    for group in range(site // (QUARTERS + 1)):
        last = None
        for m in range(QUARTERS):
            slot = group * QUARTERS + m
            value = ref[:, slot * LANES : (slot + 1) * LANES].astype(F32)
            tiles.append(jnp.where(keep, value, 0.0).astype(BF16))
            piece = pltpu.roll(value, LANES - bond + m * quarter, 1)
            last = piece if last is None else jnp.where(lane >= m * quarter, piece, last)
        tiles.append(jnp.where(keep, last, 0.0).astype(BF16))
    return tiles


def sketched(stack, sketch):
    return product(jnp.concatenate([stack, stack], 1), jnp.concatenate(halves(sketch), 0))


def inverse_factors(grams, bond):
    count = -(-bond // ROWS) * ROWS
    shape = (count, LANES)
    row, lane = index_of(shape, 0), index_of(shape, 1)
    inside = (row < bond) & (lane < bond)
    eye = jnp.where(row == lane, 1.0, 0.0)
    work = [jnp.where(inside, gram[:count], eye) for gram in grams]
    done = [[] for _ in grams]
    for first in range(0, count, ROWS):
        height = count - first
        row, lane = index_of((height, LANES), 0), index_of((height, LANES), 1)
        block = (lane >= first) & (lane < first + ROWS)
        start = jnp.where(row == lane - first, 1.0, 0.0)
        small_row, small_lane = index_of((ROWS, LANES), 0), index_of((ROWS, LANES), 1)
        columns = []
        for n, matrix in enumerate(work):
            columns.append(
                [
                    jnp.broadcast_to(matrix[:, first + j : first + j + 1], (height, LANES))
                    for j in range(ROWS)
                ]
            )
            work[n] = jnp.where(block, start, matrix)
        pivots = [jnp.ones((ROWS, LANES), F32) for _ in work]
        for j in range(ROWS):
            for n in range(len(work)):
                column = columns[n]
                pivot = column[j][j : j + 1, :]
                factor = jnp.where(row > j, column[j] * (1.0 / pivot), 0.0)
                work[n] = work[n] - factor * work[n][j : j + 1, :]
                for later in range(j + 1, ROWS):
                    column[later] = column[later] - factor * column[later][j : j + 1, :]
                pivots[n] = jnp.where(small_row == j, pivot, pivots[n])
        for n in range(len(work)):
            scaled = work[n][:ROWS] * lax.rsqrt(pivots[n])
            done[n].append(jnp.where(small_lane <= small_row + first, scaled, 0.0))
            work[n] = work[n][ROWS:]
    tail = jnp.zeros((LANES - count, LANES), F32)
    keep = (index_of((LANES, LANES), 0) < bond) & (index_of((LANES, LANES), 1) < bond)
    return [jnp.where(keep, jnp.concatenate(parts + [tail], 0), 0.0) for parts in done]


def gram_of(values):
    high, low = halves(values)
    both = product(high, jnp.concatenate([high, low], 1), TN)
    mixed = both[:, LANES:]
    return both[:, :LANES] + mixed + mixed.T


def scaled_corner(values, bond):
    mean = jnp.sum(values * values) / (bond * bond)
    return (values / jnp.sqrt(mean + 1e-06)).astype(BF16)


def half_tiles(corner, pieces):
    return [product(corner, piece) for piece in pieces]


def fill(stack, tiles):
    for k, tile in enumerate(tiles):
        stack[k * LANES : (k + 1) * LANES, :] = tile.astype(stack.dtype)


def store_frame_rows(frame, rows_ref, spare_ref, plain, moved, site):
    bond_rows = plain.shape[0] // SLOT
    zero = jnp.zeros((bond_rows, LANES), F32)
    moves = [ROWS * (k // (ROWS - 1)) + 1 + k % (ROWS - 1) for k in range(site)]
    for k in range(SLOT):
        if k >= site:
            plain[pl.ds(k, bond_rows, stride=SLOT), :] = zero
        if k not in moves:
            moved[pl.ds(k, bond_rows, stride=SLOT), :] = zero
    for k in range(site):
        tile = frame[k * LANES : (k + 1) * LANES, :].T.astype(F32)[:bond_rows]
        plain[pl.ds(k, bond_rows, stride=SLOT), :] = tile
        moved[pl.ds(moves[k], bond_rows, stride=SLOT), :] = tile
    rows_ref[...] = plain[...].astype(BF16)
    spare_ref[...] = moved[...].astype(BF16)


def halves_kernel(bond, site, c1, t1, c4, t3, upper_packed, lower_packed, upper, lower):
    for corner, edge, packed, stack in ((c1, t1, upper_packed, upper), (c4, t3, lower_packed, lower)):
        tiles = half_tiles(square_of(corner, bond).astype(BF16), spread(edge, bond, site))
        fill(stack, tiles)
        pack(tiles, packed, bond)


def prepare_kernel(
    bond, site, c2, t2, t4, t1, above, below, right, upper, lower,
    t4_wide, t1_out, upper_sketch, lower_sketch, side_packed, side, side_sketch,
):
    t1_out[...] = t1[...]
    for k, piece in enumerate(spread(t4, bond, site)):
        t4_wide[:, k * LANES : (k + 1) * LANES] = piece
    tiles = half_tiles(square_of(c2, bond).astype(BF16), spread(t2, bond, site))
    fill(side, tiles)
    pack(tiles, side_packed, bond)
    upper_sketch[...] = sketched(upper[...], square_of(above, bond))
    lower_sketch[...] = sketched(lower[...], square_of(below, bond))
    side_sketch[...] = sketched(side[...], square_of(right, bond))


def vertical_kernel(
    bond, site, upper_packed, lower_packed, above, below, upper, upper_sketch, lower, lower_sketch,
    pattern, rows_ref, spare_ref, frame_out, corner_top, corner_bottom, pattern_out, stack, over, under, plain, moved,
):
    pattern_out[0] = pattern[0]
    fill(stack, unpack(upper_packed, bond, site))
    under[...] = lower_sketch[...] + sketched(stack[...], square_of(above, bond))
    fill(stack, unpack(lower_packed, bond, site))
    over[...] = upper_sketch[...] + sketched(stack[...], square_of(below, bond))
    grams = [gram_of(over[...]), gram_of(under[...])]
    inverse_over, inverse_under = inverse_factors(grams, bond)
    frame_in = product_split(over[...], inverse_over, NT).astype(BF16)
    store_frame_rows(frame_in, rows_ref, spare_ref, plain, moved, site)
    frame_out[...] = product_split(under[...], inverse_under, NT).astype(BF16)
    corner_top[...] = scaled_corner(product(frame_in, upper[...], TN), bond)
    corner_bottom[...] = scaled_corner(product(frame_out[...], lower[...], TN), bond)


def horizontal_kernel(
    bond, site, c1, c4, edge, left, side, side_sketch, inverse_ref, frame_out, half, total
):
    corner = square_of(c1, bond).T.astype(BF16)
    for k in range(site):
        half[k * LANES : (k + 1) * LANES, :] = product(corner, edge[:, k * LANES : (k + 1) * LANES])
    total[...] = side_sketch[...] + product_split(half[...], square_of(left, bond))
    (inverse,) = inverse_factors([gram_of(total[...])], bond)
    inverse_ref[:, :LANES] = inverse
    inverse_ref[:, LANES:] = square_of(c4, bond)
    frame = product_split(total[...], inverse, NT)
    pack([frame[k * LANES : (k + 1) * LANES, :] for k in range(site)], frame_out, bond)
    corner_right = scaled_corner(product(frame.astype(BF16), side[...], TN), bond)
    frame_out[:, frame_out.shape[1] - LANES :] = corner_right


def early_kernel(bond, site, side_packed, right, t1, after, side_sketch, t1_wide, stack):
    for k, piece in enumerate(spread(t1, bond, site)):
        t1_wide[:, k * LANES : (k + 1) * LANES] = piece
    fill(stack, unpack(side_packed, bond, site))
    side_sketch[...] = sketched(stack[...], square_of(right, bond))


def arrive_kernel(
    bond, site, payload, side_sketch, left, inverse_ref,
    rows_ref, spare_ref, corner_left, forward, half, total, plain, moved,
):
    start = payload.shape[1] - LANES
    corner = square_of(payload.at[:, start:], bond).T.astype(BF16)
    fill(half, half_tiles(corner, spread(payload, bond, site)))
    total[...] = side_sketch[...] + product_split(half[...], square_of(left, bond))
    frame_in = product_split(total[...], inverse_ref[:, :LANES], NT).astype(BF16)
    store_frame_rows(frame_in, rows_ref, spare_ref, plain, moved, site)
    corner_left[...] = scaled_corner(product(half[...].astype(BF16), frame_in, TN), bond)
    forward[:, : payload.shape[1]] = payload[...]
    forward[:, payload.shape[1] :] = inverse_ref[:, LANES:].astype(BF16)


def finish_kernel(bond, payload, frame, left_corner, left_edge, left_bottom, top_right):
    start = payload.shape[1] - 2 * LANES
    left_edge[...] = payload[:, :start]
    left_corner[...] = payload[:, start : start + LANES]
    left_bottom[...] = payload[:, start + LANES :]
    top_right[...] = frame[:, frame.shape[1] - LANES :]


def absorb_kernel(bond, site, first, rows_ref, spare_ref, edge, tensor, frame, *refs):
    mixed_even, mixed_odd, pushed_even, pushed_odd, last, result = refs[-6:]
    if first:
        corner, dense, wide = refs[:3]
        frame_out = frame
    else:
        dense, frame_out = refs[0], refs[1]
        fill(frame_out, unpack(frame, bond, site))
    main = site - 1
    groups = bond // GROUP
    tall = GROUP * main
    tiles = GROUP * SLOT
    last[...] = jnp.zeros_like(last)
    ahead = tall + bond * main
    result[ahead:, :] = jnp.zeros((result.shape[0] - ahead, LANES), F32)

    def frames_of(ref, group):
        return ref[pl.ds(pl.multiple_of(group * tiles, tiles), tiles), :]

    def spare_of(group):
        return product(frames_of(spare_ref, group), edge[:, main * LANES : site * LANES])

    def mix(group, mixed, j, spare):
        both = product(frames_of(rows_ref, group), edge[:, j * LANES : (j + 2) * LANES])
        for side in range(2):
            rows = slice((j + side) * SLOT, (j + side + 1) * SLOT)
            for p in range(GROUP):
                tile = both[p * SLOT : (p + 1) * SLOT, side * LANES : (side + 1) * LANES]
                if j + side < QUARTERS:
                    at = p * SLOT + (j + side) * ROWS
                    extra = spare[at : at + ROWS, :]
                    tile = jnp.concatenate([tile[: SLOT - ROWS], tile[SLOT - ROWS :] + extra], 0)
                mixed[rows, p * LANES : (p + 1) * LANES] = tile.astype(BF16)

    def push(group, mixed, pushed, pair):
        out = product(tensor[...], mixed[:, 2 * pair * LANES : (2 * pair + 2) * LANES])
        for k in range(site):
            parts = [
                out[k * main : (k + 1) * main, side * LANES : (side + 1) * LANES]
                for side in range(2)
            ]
            pushed[2 * pair * main : (2 * pair + 2) * main, k * LANES : (k + 1) * LANES] = (
                jnp.concatenate(parts, 0).astype(BF16)
            )
        for side in range(2):
            place = group * GROUP + 2 * pair + side
            last[pl.ds(place, site, stride=LANES), :] = out[
                site * main : site * main + site, side * LANES : (side + 1) * LANES
            ]

    def cuts():
        step = -(-site // CUTS) // 2 * 2
        starts = [n * step for n in range(CUTS)] + [site]
        return [slice(low * LANES, high * LANES) for low, high in zip(starts, starts[1:])]

    def close(group, total):
        result[pl.ds(pl.multiple_of((group + 1) * tall, tall), tall), :] = total

    def stage(group, mixed, pushed, mixed_next, pushed_before):
        following = jnp.minimum(group + 1, groups - 1)
        spare = spare_of(following)
        total = jnp.zeros((tall, LANES), F32)
        pairs = GROUP // 2
        parts = cuts()
        units = main // 2
        for n in range(pairs):
            push(group, mixed, pushed, n)
            for unit in range(n * units // pairs, (n + 1) * units // pairs):
                mix(following, mixed_next, 2 * unit, spare)
            if n < CUTS:
                total = total + product(pushed_before[:, parts[n]], frame_out[parts[n], :])
        close(group - 1, total)

    spare = spare_of(0)
    for unit in range(main // 2):
        mix(0, mixed_even, 2 * unit, spare)

    def step(index, carry):
        stage(2 * index, mixed_even, pushed_even, mixed_odd, pushed_odd)
        stage(2 * index + 1, mixed_odd, pushed_odd, mixed_even, pushed_even)
        return carry

    lax.fori_loop(0, groups // 2, step, 0)
    close(groups - 1, product(pushed_odd[...], frame_out[...]))
    tiles = [result[pl.ds(tall + k, LANES, stride=main), :] for k in range(main)]
    total = jnp.zeros((LANES, LANES), F32)
    for k in range(site):
        rows = pl.ds(k * LANES, LANES)
        total = total + product(last[rows, :].astype(BF16), frame_out[rows, :])
    tiles.append(total)
    squares = tiles[0] * tiles[0]
    for tile in tiles[1:]:
        squares = squares + tile * tile
    scale = 1.0 / jnp.sqrt(jnp.sum(squares) / (bond * bond * site) + 1e-06)
    tiles = [tile * scale for tile in tiles]
    gather_dense(tiles, dense, bond)
    if first:
        for k, tile in enumerate(tiles):
            wide[:, k * LANES : (k + 1) * LANES] = tile.astype(BF16)
        dense[:, dense.shape[1] - LANES :] = square_of(corner, bond).astype(BF16)


def arrange_kernel(pattern, tensors, rows, columns, after, out, tensor, semaphore):
    copy = pltpu.make_async_copy(tensors.at[pattern[0]], tensor, semaphore)
    copy.start()
    square = tensor.shape[0]
    pick_rows = jnp.where(index_of((rows.shape[0], square), 1) == rows[...], 1.0, 0.0).astype(BF16)
    pick_columns = jnp.where(index_of((square, columns.shape[1]), 0) == columns[...], 1.0, 0.0)
    copy.wait()
    turned = product(pick_rows, tensor[...], NT).astype(BF16)
    out[...] = product(turned, pick_columns.astype(BF16)).astype(BF16)


def places(site):
    main = site - 1
    height = -(-site * site // 16) * 16
    rows = np.full((2, height), -1, np.int32)
    columns = np.full((2, main * SLOT), -1, np.int32)
    for summed in range(site):
        for kept in range(site):
            at = summed * main + kept if kept < main else site * main + summed
            rows[0, at] = summed * site + kept
            rows[1, at] = kept * site + summed
    for edge in range(site):
        for frame in range(site):
            if edge < main:
                at = edge * SLOT + frame
            else:
                slot, offset = divmod(frame, ROWS - 1)
                at = slot * SLOT + SLOT - ROWS + 1 + offset
            columns[0, at] = frame * site + edge
            columns[1, at] = edge * site + frame
    return rows, columns


def block_of(arg):
    shape = arg.shape
    if len(shape) == 1:
        return pl.BlockSpec(memory_space=pltpu.SMEM)
    if shape[0] % 16 == 0 and shape[1] % LANES == 0:
        return pl.BlockSpec(memory_space=pltpu.VMEM)
    return pl.BlockSpec(tuple(-(-size // LANES) * LANES for size in shape), lambda i: (0, 0))


def cost(microseconds):
    return pl.CostEstimate(
        flops=microseconds * 1_000_000_000, bytes_accessed=microseconds * 1_000_000, transcendentals=0
    )


def call(kernel, args, outs, scratch, limit, microseconds, unread=0):
    specs = [block_of(arg) for arg in args]
    if unread:
        specs[-unread:] = [pl.BlockSpec(memory_space=pl.ANY)] * unread
    return pl.pallas_call(
        kernel,
        grid=(1,),
        in_specs=specs,
        out_specs=[block_of(out) for out in outs],
        out_shape=outs,
        scratch_shapes=scratch,
        compiler_params=pltpu.CompilerParams(vmem_limit_bytes=limit * MIB),
        cost_estimate=cost(microseconds),
    )(*args)


def shape_of(shape, dtype=BF16):
    return jax.ShapeDtypeStruct(shape, dtype)


def shift(value, axis, steps):
    count = lax.axis_size(axis)
    pairs = [(source, (source + steps) % count) for source in range(count)]
    return lax.ppermute(value, axis, pairs)


def shift_both(value, steps_col, steps_row):
    columns, rows = lax.axis_size("col"), lax.axis_size("row")
    pairs = []
    for x in range(columns):
        for y in range(rows):
            target = (x + steps_col) % columns * rows + (y + steps_row) % rows
            pairs.append((x * rows + y, target))
    return lax.ppermute(value, ("col", "row"), pairs)


def body(c1, c2, c4, t1, t2, t3, t4, tensors, pattern, below, above, right, left):
    bond = c1.shape[0]
    site = t1.shape[1] // bond
    square = site * site
    tall = site * LANES
    bond_rows = -(-bond // ROWS) * ROWS
    frame_rows = shape_of((bond_rows * SLOT, LANES))
    packed = shape_of((bond, site // (QUARTERS + 1) * QUARTERS * LANES))
    dense = shape_of((bond, site * bond))
    wide = shape_of((LANES, tall))
    stack = shape_of((tall, LANES))
    stack_f32 = shape_of((tall, LANES), F32)
    corner = shape_of((bond, bond))
    payload = shape_of((bond, -(-site * bond // LANES) * LANES + LANES))
    half = pltpu.VMEM((tall, LANES), F32)
    half_bf16 = pltpu.VMEM((tall, LANES), BF16)
    frame_scratch = pltpu.VMEM(frame_rows.shape, F32)
    rows, columns = places(site)

    def arrange(which, index, after):
        height, depth = rows.shape[1], columns.shape[1]
        vmem = pl.BlockSpec(memory_space=pltpu.VMEM)
        return pl.pallas_call(
            arrange_kernel,
            in_specs=[
                pl.BlockSpec(memory_space=pltpu.SMEM),
                pl.BlockSpec(memory_space=pltpu.HBM),
                vmem,
                vmem,
                pl.BlockSpec(memory_space=pl.ANY),
            ],
            out_specs=vmem,
            out_shape=shape_of((height, depth)),
            scratch_shapes=[pltpu.VMEM((square, square), BF16), pltpu.SemaphoreType.DMA],
            compiler_params=pltpu.CompilerParams(vmem_limit_bytes=16 * MIB),
            cost_estimate=cost(3),
        )(
            index,
            tensors,
            rows[which].reshape(height, 1),
            columns[which].reshape(1, depth),
            after,
        )

    def absorb(first, rows_in, spare_in, edge, tensor, frame, *more):
        main = site - 1
        return call(
            functools.partial(absorb_kernel, bond, site, first),
            (rows_in, spare_in, edge, tensor, frame) + more,
            [payload, wide] if first else [dense],
            ([] if first else [half_bf16])
            + [
                pltpu.VMEM((main * SLOT, GROUP * LANES), BF16),
                pltpu.VMEM((main * SLOT, GROUP * LANES), BF16),
                pltpu.VMEM((GROUP * main, tall), BF16),
                pltpu.VMEM((GROUP * main, tall), BF16),
                pltpu.VMEM((tall, LANES), F32),
                pltpu.VMEM(((LANES + GROUP) * main, LANES), F32),
            ],
            36,
            28,
        )

    upper_packed, lower_packed, upper, lower = call(
        functools.partial(halves_kernel, bond, site),
        (c1, t1, c4, t3),
        [packed, packed, stack, stack],
        [],
        60,
        2,
    )
    upper_next = shift(upper_packed, "row", -1)
    lower_back = shift(lower_packed, "row", 1)
    pattern = pattern.reshape(1)
    pattern_back = shift(pattern, "row", 1)
    tensor_left = arrange(0, pattern, lower)
    t4_wide, t1_held, upper_sketch, lower_sketch, side_packed, side, side_sketch = call(
        functools.partial(prepare_kernel, bond, site),
        (c2, t2, t4, t1, above, below, right, upper, lower),
        [wide, dense, stack_f32, stack_f32, packed, stack, stack_f32],
        [],
        24,
        2,
    )
    t1_back = shift(t1_held, "row", 1)
    side_back = shift_both(side_packed, 1, 1)
    rows_left, spare_left, frame_below, corner_top, corner_bottom, pattern_held = call(
        functools.partial(vertical_kernel, bond, site),
        (upper_next, lower_back, above, below, upper, upper_sketch, lower, lower_sketch)
        + (pattern_back,),
        [frame_rows, frame_rows, stack, corner, corner, shape_of((1,), jnp.int32)],
        [half_bf16, half, half, frame_scratch, frame_scratch],
        32,
        10,
    )
    left_new, edge_wide = absorb(
        True, rows_left, spare_left, t4_wide, tensor_left, frame_below, corner_top
    )
    left_back = shift_both(left_new, 1, 1)
    inverse, frame_right = call(
        functools.partial(horizontal_kernel, bond, site),
        (corner_top, corner_bottom, edge_wide, left, side, side_sketch),
        [shape_of((LANES, 2 * LANES), F32), shape_of((bond, packed.shape[1] + LANES))],
        [half, half],
        32,
        6,
    )
    inverse_back = shift_both(inverse, 1, 1)
    frame_back = shift(frame_right, "row", 1)
    tensor_top = arrange(1, pattern_held, inverse)
    early_sketch, t1_wide = call(
        functools.partial(early_kernel, bond, site),
        (side_back, right, t1_back, inverse),
        [stack_f32, wide],
        [half_bf16],
        24,
        2,
        1,
    )
    rows_top, spare_top, top_left, forward = call(
        functools.partial(arrive_kernel, bond, site),
        (left_back, early_sketch, left, inverse_back),
        [frame_rows, frame_rows, corner, shape_of((bond, payload.shape[1] + LANES))],
        [half, half, frame_scratch, frame_scratch],
        32,
        4,
    )
    left_here = shift(forward, "row", -1)
    (top_edge,) = absorb(False, rows_top, spare_top, t1_wide, tensor_top, frame_back)
    left_corner, left_edge, left_bottom, top_right = call(
        functools.partial(finish_kernel, bond),
        (left_here, frame_back),
        [corner, dense, corner, corner],
        [],
        16,
        1,
    )
    return (left_corner, left_edge, left_bottom, top_left, top_edge, top_right)


def solution(mesh):
    block, whole = P("col", "row"), P()
    in_specs = (block,) * 7 + (whole, block) + (whole,) * 4
    return jax.shard_map(
        body, mesh=mesh, in_specs=in_specs, out_specs=(block,) * 6, check_vma=False
    )
```

```python
import functools

import jax
import jax.numpy as jnp
import numpy as np
from jax import lax
from jax.experimental import pallas as pl
from jax.experimental.pallas import tpu as pltpu
from jax.sharding import PartitionSpec as P

LANES = 128
ROWS = 8
HALF_TILE = 16
GROUP = 10
CUTS = 4
QUARTERS = 4
MIB = 1 << 20
F32 = jnp.float32
BF16 = jnp.bfloat16

NN = (((1,), (0,)), ((), ()))
NT = (((1,), (1,)), ((), ()))
TN = (((0,), (0,)), ((), ()))


def product(left, right, dims=NN):
    return lax.dot_general(left, right, dims, preferred_element_type=F32)


def halves(values):
    high = values.astype(BF16)
    return high, (values - high.astype(F32)).astype(BF16)


def product_split(left, right, dims=NN):
    left_high, left_low = halves(left)
    right_high, right_low = halves(right)
    axis_left, axis_right = dims[0][0][0], dims[0][1][0]
    both = jnp.concatenate([left_high, left_low], axis_left)
    twice = jnp.concatenate([right_high, right_high], axis_right)
    return product(both, twice, dims) + product(left_high, right_low, dims)


def index_of(shape, axis):
    return lax.broadcasted_iota(jnp.int32, shape, axis)


def square_of(ref, bond):
    shape = (LANES, LANES)
    keep = (index_of(shape, 0) < bond) & (index_of(shape, 1) < bond)
    return jnp.where(keep, ref[...].astype(F32), 0.0)


def spread(ref, bond, site):
    shape = (LANES, LANES)
    row, lane = index_of(shape, 0), index_of(shape, 1)
    keep = (row < bond) & (lane < bond)
    pieces = []
    for k in range(site):
        tile, offset = divmod(k * bond, LANES)
        piece = ref[:, tile * LANES : (tile + 1) * LANES].astype(F32)
        if offset:
            piece = pltpu.roll(piece, LANES - offset, 1)
        if offset + bond > LANES:
            more = ref[:, (tile + 1) * LANES : (tile + 2) * LANES].astype(F32)
            piece = jnp.where(lane < LANES - offset, piece, pltpu.roll(more, LANES - offset, 1))
        pieces.append(jnp.where(keep, piece, 0.0).astype(BF16))
    return pieces


def gather_dense(tiles, ref, bond):
    lane = index_of((LANES, LANES), 1)
    total = len(tiles) * bond
    for tile in range(-(-total // LANES)):
        begin = tile * LANES
        value = None
        for k in range(begin // bond, min(len(tiles) - 1, (begin + LANES - 1) // bond) + 1):
            shift = k * bond - begin
            piece = pltpu.roll(tiles[k], shift % LANES, 1) if shift % LANES else tiles[k]
            value = piece if value is None else jnp.where(lane >= shift, piece, value)
        ref[:, begin : begin + LANES] = value.astype(ref.dtype)


def pack(tiles, ref, bond):
    quarter = bond // QUARTERS
    lane = index_of((LANES, LANES), 1)
    for group in range(len(tiles) // (QUARTERS + 1)):
        first = group * (QUARTERS + 1)
        for m in range(QUARTERS):
            piece = pltpu.roll(tiles[first + QUARTERS], bond - m * quarter, 1)
            slot = group * QUARTERS + m
            value = jnp.where(lane < bond, tiles[first + m], piece)
            ref[:, slot * LANES : (slot + 1) * LANES] = value.astype(ref.dtype)


def unpack(ref, bond, site):
    quarter = bond // QUARTERS
    shape = (LANES, LANES)
    row, lane = index_of(shape, 0), index_of(shape, 1)
    keep = (row < bond) & (lane < bond)
    tiles = []
    for group in range(site // (QUARTERS + 1)):
        last = None
        for m in range(QUARTERS):
            slot = group * QUARTERS + m
            value = ref[:, slot * LANES : (slot + 1) * LANES].astype(F32)
            tiles.append(jnp.where(keep, value, 0.0).astype(BF16))
            piece = pltpu.roll(value, LANES - bond + m * quarter, 1)
            last = piece if last is None else jnp.where(lane >= m * quarter, piece, last)
        tiles.append(jnp.where(keep, last, 0.0).astype(BF16))
    return tiles


def sketched(stack, sketch):
    return product(jnp.concatenate([stack, stack], 1), jnp.concatenate(halves(sketch), 0))


def inverse_factors(grams, bond):
    count = -(-bond // ROWS) * ROWS
    shape = (count, LANES)
    row, lane = index_of(shape, 0), index_of(shape, 1)
    inside = (row < bond) & (lane < bond)
    eye = jnp.where(row == lane, 1.0, 0.0)
    work = [jnp.where(inside, gram[:count], eye) for gram in grams]
    done = [[] for _ in grams]
    for first in range(0, count, ROWS):
        height = count - first
        row, lane = index_of((height, LANES), 0), index_of((height, LANES), 1)
        block = (lane >= first) & (lane < first + ROWS)
        start = jnp.where(row == lane - first, 1.0, 0.0)
        small_row, small_lane = index_of((ROWS, LANES), 0), index_of((ROWS, LANES), 1)
        columns = []
        for n, matrix in enumerate(work):
            columns.append(
                [
                    jnp.broadcast_to(matrix[:, first + j : first + j + 1], (height, LANES))
                    for j in range(ROWS)
                ]
            )
            work[n] = jnp.where(block, start, matrix)
        pivots = [jnp.ones((ROWS, LANES), F32) for _ in work]
        for j in range(ROWS):
            for n in range(len(work)):
                column = columns[n]
                pivot = column[j][j : j + 1, :]
                factor = jnp.where(row > j, column[j] * (1.0 / pivot), 0.0)
                work[n] = work[n] - factor * work[n][j : j + 1, :]
                for later in range(j + 1, ROWS):
                    column[later] = column[later] - factor * column[later][j : j + 1, :]
                pivots[n] = jnp.where(small_row == j, pivot, pivots[n])
        for n in range(len(work)):
            scaled = work[n][:ROWS] * lax.rsqrt(pivots[n])
            done[n].append(jnp.where(small_lane <= small_row + first, scaled, 0.0))
            work[n] = work[n][ROWS:]
    tail = jnp.zeros((LANES - count, LANES), F32)
    keep = (index_of((LANES, LANES), 0) < bond) & (index_of((LANES, LANES), 1) < bond)
    return [jnp.where(keep, jnp.concatenate(parts + [tail], 0), 0.0) for parts in done]


def gram_and(values, other):
    both = product(values, jnp.concatenate([values, other], 1), TN)
    return both[:, :LANES], both[:, LANES:]


def frame_from(values, inverse):
    high, low = halves(inverse)
    both = jnp.concatenate([values, values], 1)
    return product(both, jnp.concatenate([high, low], 1), NT)


def scaled_corner(values, bond):
    mean = jnp.sum(values * values) / (bond * bond)
    return (values / jnp.sqrt(mean + 1e-06)).astype(BF16)


def half_tiles(corner, pieces):
    return [product(corner, piece) for piece in pieces]


def fill(stack, tiles):
    for k, tile in enumerate(tiles):
        stack[k * LANES : (k + 1) * LANES, :] = tile.astype(stack.dtype)


def store_frame_rows(sketch, inverse, rows_ref, plain, tail, site):
    main = site - 1
    bond_rows = plain.shape[0] // main
    both = jnp.concatenate(halves(inverse), 1)[:bond_rows]
    for k in range(site):
        piece = sketch[k * LANES : (k + 1) * LANES, :]
        tile = product(both, jnp.concatenate([piece, piece], 1), NT)
        if k < main:
            plain[pl.ds(k, bond_rows, stride=main), :] = tile
        else:
            for group in range(tail.shape[0] // HALF_TILE):
                begin = group * HALF_TILE
                tail[begin : begin + GROUP, :] = tile[group * GROUP : (group + 1) * GROUP]
    rows_ref[: plain.shape[0], :] = plain[...].astype(BF16)
    rows_ref[plain.shape[0] :, :] = tail[...].astype(BF16)


def halves_kernel(bond, site, c1, t1, c4, t3, upper_packed, lower_packed):
    for corner, edge, packed in ((c1, t1, upper_packed), (c4, t3, lower_packed)):
        pack(half_tiles(square_of(corner, bond).astype(BF16), spread(edge, bond, site)), packed, bond)


def prepare_kernel(
    bond, site, c2, t2, t4, t1, above, below, right, upper_packed, lower_packed,
    t4_wide, t1_out, upper, upper_sketch, lower, lower_sketch, side_packed, side, side_sketch,
):
    t1_out[...] = t1[...]
    tiles = half_tiles(square_of(c2, bond).astype(BF16), spread(t2, bond, site))
    fill(side, tiles)
    pack(tiles, side_packed, bond)
    fill(upper, unpack(upper_packed, bond, site))
    fill(lower, unpack(lower_packed, bond, site))
    upper_sketch[...] = sketched(upper[...], square_of(above, bond))
    lower_sketch[...] = sketched(lower[...], square_of(below, bond))
    side_sketch[...] = sketched(side[...], square_of(right, bond))
    for k, piece in enumerate(spread(t4, bond, site)):
        t4_wide[:, k * LANES : (k + 1) * LANES] = piece


def vertical_kernel(
    bond, site, upper_packed, lower_packed, above, below, upper, upper_sketch, lower, lower_sketch,
    pattern, rows_ref, frame_out, corner_top, corner_bottom, pattern_out, stack, over, under, plain, tail,
):
    pattern_out[0] = pattern[0]
    fill(stack, unpack(upper_packed, bond, site))
    under[...] = (lower_sketch[...] + sketched(stack[...], square_of(above, bond))).astype(BF16)
    fill(stack, unpack(lower_packed, bond, site))
    over[...] = (upper_sketch[...] + sketched(stack[...], square_of(below, bond))).astype(BF16)
    gram_over, mixed_over = gram_and(over[...], upper[...])
    gram_under, mixed_under = gram_and(under[...], lower[...])
    inverse_over, inverse_under = inverse_factors([gram_over, gram_under], bond)
    store_frame_rows(over, inverse_over, rows_ref, plain, tail, site)
    frame_out[...] = frame_from(under[...], inverse_under).astype(BF16)
    corner_top[...] = scaled_corner(product_split(inverse_over, mixed_over), bond)
    corner_bottom[...] = scaled_corner(product_split(inverse_under, mixed_under), bond)


def horizontal_kernel(
    bond, site, c1, c4, edge, left, side, side_sketch, inverse_ref, frame_out, half, total
):
    corner = square_of(c1, bond).T.astype(BF16)
    fill(half, half_tiles(corner, [edge[:, k * LANES : (k + 1) * LANES] for k in range(site)]))
    total[...] = (side_sketch[...] + sketched(half[...], square_of(left, bond))).astype(BF16)
    gram, mixed = gram_and(total[...], side[...])
    (inverse,) = inverse_factors([gram], bond)
    inverse_ref[:, :LANES] = inverse
    inverse_ref[:, LANES:] = square_of(c4, bond)
    frame = frame_from(total[...], inverse)
    pack([frame[k * LANES : (k + 1) * LANES, :] for k in range(site)], frame_out, bond)
    corner_right = scaled_corner(product_split(inverse, mixed), bond)
    frame_out[:, frame_out.shape[1] - LANES :] = corner_right


def early_kernel(bond, site, side_packed, right, t1, after, side_sketch, t1_wide, stack):
    for k, piece in enumerate(spread(t1, bond, site)):
        t1_wide[:, k * LANES : (k + 1) * LANES] = piece
    fill(stack, unpack(side_packed, bond, site))
    side_sketch[...] = sketched(stack[...], square_of(right, bond))


def arrive_kernel(
    bond, site, payload, side_sketch, left, inverse_ref,
    rows_ref, corner_left, forward, half, total, plain, tail,
):
    start = payload.shape[1] - LANES
    corner = square_of(payload.at[:, start:], bond).T.astype(BF16)
    fill(half, half_tiles(corner, spread(payload, bond, site)))
    total[...] = (side_sketch[...] + sketched(half[...], square_of(left, bond))).astype(BF16)
    inverse = inverse_ref[:, :LANES]
    store_frame_rows(total, inverse, rows_ref, plain, tail, site)
    mixed = product(half[...], total[...], TN)
    corner_left[...] = scaled_corner(product_split(mixed, inverse, NT), bond)
    forward[:, : payload.shape[1]] = payload[...]
    forward[:, payload.shape[1] :] = inverse_ref[:, LANES:].astype(BF16)


def finish_kernel(bond, payload, frame, left_corner, left_edge, left_bottom, top_right):
    start = payload.shape[1] - 2 * LANES
    left_edge[...] = payload[:, :start]
    left_corner[...] = payload[:, start : start + LANES]
    left_bottom[...] = payload[:, start + LANES :]
    top_right[...] = frame[:, frame.shape[1] - LANES :]


def absorb_kernel(bond, site, first, rows_ref, edge, tensor, frame, *refs):
    mixed_even, mixed_odd, spare_even, spare_odd, pushed_even, pushed_odd, last, result = refs[-8:]
    if first:
        corner, dense, wide = refs[:3]
        frame_out = frame
    else:
        dense, frame_out = refs[0], refs[1]
        fill(frame_out, unpack(frame, bond, site))
    main = site - 1
    groups = bond // GROUP
    tall = GROUP * main
    slot = spare_even.shape[0] // HALF_TILE
    spare_even[...] = jnp.zeros_like(spare_even)
    spare_odd[...] = jnp.zeros_like(spare_odd)
    ahead = tall + bond * main
    result[ahead:, :] = jnp.zeros((result.shape[0] - ahead, LANES), F32)

    def frames_of(group):
        body = rows_ref[pl.ds(pl.multiple_of(group * tall, tall), tall), :]
        begin = rows_ref.shape[0] - groups * HALF_TILE + group * HALF_TILE
        tail = rows_ref[pl.ds(pl.multiple_of(begin, HALF_TILE), HALF_TILE), :]
        return jnp.concatenate([body, tail], 0)

    def mix(frames, mixed, spare, unit):
        j = 2 * unit
        sides = min(2, site - j)
        both = product(frames, edge[:, j * LANES : (j + sides) * LANES])
        for side in range(sides):
            lanes = slice(side * LANES, (side + 1) * LANES)
            spare[pl.ds(j + side, HALF_TILE, stride=slot), :] = both[tall:, lanes]
        for p in range(GROUP):
            parts = [
                both[p * main : (p + 1) * main, side * LANES : (side + 1) * LANES]
                for side in range(sides)
            ]
            end = (j + sides) * main
            if sides == 1:
                end = mixed.shape[0]
                parts.append(spare[p * slot : (p + 1) * slot, :])
                parts.append(jnp.zeros((end - j * main - main - slot, LANES), F32))
            mixed[j * main : end, p * LANES : (p + 1) * LANES] = (
                jnp.concatenate(parts, 0).astype(BF16)
            )

    def push(group, mixed, pushed, pair):
        out = product(tensor[...], mixed[:, 2 * pair * LANES : (2 * pair + 2) * LANES])
        for k in range(site):
            parts = [
                out[k * main : (k + 1) * main, side * LANES : (side + 1) * LANES]
                for side in range(2)
            ]
            pushed[2 * pair * main : (2 * pair + 2) * main, k * LANES : (k + 1) * LANES] = (
                jnp.concatenate(parts, 0).astype(BF16)
            )
        for side in range(2):
            place = group * GROUP + 2 * pair + side
            last[pl.ds(place, site, stride=LANES), :] = out[
                site * main : site * main + site, side * LANES : (side + 1) * LANES
            ]

    def cuts():
        step = -(-site // CUTS) // 2 * 2
        starts = [n * step for n in range(CUTS)] + [site]
        return [slice(low * LANES, high * LANES) for low, high in zip(starts, starts[1:])]

    def close(group, total):
        result[pl.ds(pl.multiple_of((group + 1) * tall, tall), tall), :] = total

    units = (site + 1) // 2

    def stage(group, mixed, pushed, mixed_next, spare_next, pushed_before):
        frames = frames_of(jnp.minimum(group + 1, groups - 1))
        total = jnp.zeros((tall, LANES), F32)
        pairs = GROUP // 2
        parts = cuts()
        for n in range(pairs):
            push(group, mixed, pushed, n)
            for unit in range(n * units // pairs, (n + 1) * units // pairs):
                mix(frames, mixed_next, spare_next, unit)
            if n < CUTS:
                total = total + product(pushed_before[:, parts[n]], frame_out[parts[n], :])
        close(group - 1, total)

    frames = frames_of(0)
    for unit in range(units):
        mix(frames, mixed_even, spare_even, unit)

    def step(index, carry):
        stage(2 * index, mixed_even, pushed_even, mixed_odd, spare_odd, pushed_odd)
        stage(2 * index + 1, mixed_odd, pushed_odd, mixed_even, spare_even, pushed_even)
        return carry

    lax.fori_loop(0, groups // 2, step, 0)
    close(groups - 1, product(pushed_odd[...], frame_out[...]))
    tiles = [result[pl.ds(tall + k, LANES, stride=main), :] for k in range(main)]
    total = jnp.zeros((LANES, LANES), F32)
    for k in range(site):
        rows = pl.ds(k * LANES, LANES)
        total = total + product(last[rows, :].astype(BF16), frame_out[rows, :])
    tiles.append(jnp.where(index_of(total.shape, 0) < bond, total, 0.0))
    squares = tiles[0] * tiles[0]
    for tile in tiles[1:]:
        squares = squares + tile * tile
    scale = 1.0 / jnp.sqrt(jnp.sum(squares) / (bond * bond * site) + 1e-06)
    tiles = [tile * scale for tile in tiles]
    gather_dense(tiles, dense, bond)
    if first:
        for k, tile in enumerate(tiles):
            wide[:, k * LANES : (k + 1) * LANES] = tile.astype(BF16)
        dense[:, dense.shape[1] - LANES :] = square_of(corner, bond).astype(BF16)


def arrange_kernel(pattern, tensors, rows, columns, after, out, tensor, semaphore):
    copy = pltpu.make_async_copy(tensors.at[pattern[0]], tensor, semaphore)
    copy.start()
    square = tensor.shape[0]
    pick_rows = jnp.where(index_of((rows.shape[0], square), 1) == rows[...], 1.0, 0.0).astype(BF16)
    pick_columns = jnp.where(index_of((square, columns.shape[1]), 0) == columns[...], 1.0, 0.0)
    copy.wait()
    turned = product(pick_rows, tensor[...], NT).astype(BF16)
    out[...] = product(turned, pick_columns.astype(BF16)).astype(BF16)


def places(site):
    main = site - 1
    size = -(-site * site // LANES) * LANES
    rows = np.full((2, size), -1, np.int32)
    columns = np.full((2, size), -1, np.int32)
    for other in range(site):
        for inner in range(site):
            at = other * main + inner if inner < main else site * main + other
            rows[0, at] = other * site + inner
            rows[1, at] = inner * site + other
            columns[0, at] = inner * site + other
            columns[1, at] = other * site + inner
    return rows, columns


def block_of(arg):
    shape = arg.shape
    if len(shape) == 1:
        return pl.BlockSpec(memory_space=pltpu.SMEM)
    if shape[0] % 16 == 0 and shape[1] % LANES == 0:
        return pl.BlockSpec(memory_space=pltpu.VMEM)
    return pl.BlockSpec(tuple(-(-size // LANES) * LANES for size in shape), lambda i: (0, 0))


def cost(microseconds):
    return pl.CostEstimate(
        flops=microseconds * 1_000_000_000, bytes_accessed=microseconds * 1_000_000, transcendentals=0
    )


def call(kernel, args, outs, scratch, limit, microseconds, unread=0):
    specs = [block_of(arg) for arg in args]
    if unread:
        specs[-unread:] = [pl.BlockSpec(memory_space=pl.ANY)] * unread
    return pl.pallas_call(
        kernel,
        grid=(1,),
        in_specs=specs,
        out_specs=[block_of(out) for out in outs],
        out_shape=outs,
        scratch_shapes=scratch,
        compiler_params=pltpu.CompilerParams(vmem_limit_bytes=limit * MIB),
        cost_estimate=cost(microseconds),
    )(*args)


def shape_of(shape, dtype=BF16):
    return jax.ShapeDtypeStruct(shape, dtype)


def shift(value, axis, steps):
    count = lax.axis_size(axis)
    pairs = [(source, (source + steps) % count) for source in range(count)]
    return lax.ppermute(value, axis, pairs)


def shift_both(value, steps_col, steps_row):
    columns, rows = lax.axis_size("col"), lax.axis_size("row")
    pairs = []
    for x in range(columns):
        for y in range(rows):
            target = (x + steps_col) % columns * rows + (y + steps_row) % rows
            pairs.append((x * rows + y, target))
    return lax.ppermute(value, ("col", "row"), pairs)


def body(c1, c2, c4, t1, t2, t3, t4, tensors, pattern, below, above, right, left):
    bond = c1.shape[0]
    site = t1.shape[1] // bond
    square = site * site
    tall = site * LANES
    bond_rows = -(-bond // ROWS) * ROWS
    body_rows = bond_rows * (site - 1)
    tail_rows = bond // GROUP * HALF_TILE
    frame_rows = shape_of((body_rows + tail_rows, LANES))
    packed = shape_of((bond, site // (QUARTERS + 1) * QUARTERS * LANES))
    dense = shape_of((bond, site * bond))
    wide = shape_of((LANES, tall))
    stack = shape_of((tall, LANES))
    stack_f32 = shape_of((tall, LANES), F32)
    corner = shape_of((bond, bond))
    payload = shape_of((bond, -(-site * bond // LANES) * LANES + LANES))
    half_bf16 = pltpu.VMEM((tall, LANES), BF16)
    frame_scratch = [pltpu.VMEM((body_rows, LANES), F32), pltpu.VMEM((tail_rows, LANES), F32)]
    rows, columns = places(site)

    def arrange(which, index, after):
        height, depth = rows.shape[1], columns.shape[1]
        vmem = pl.BlockSpec(memory_space=pltpu.VMEM)
        return pl.pallas_call(
            arrange_kernel,
            in_specs=[
                pl.BlockSpec(memory_space=pltpu.SMEM),
                pl.BlockSpec(memory_space=pltpu.HBM),
                vmem,
                vmem,
                pl.BlockSpec(memory_space=pl.ANY),
            ],
            out_specs=vmem,
            out_shape=shape_of((height, depth)),
            scratch_shapes=[pltpu.VMEM((square, square), BF16), pltpu.SemaphoreType.DMA],
            compiler_params=pltpu.CompilerParams(vmem_limit_bytes=16 * MIB),
            cost_estimate=cost(3),
        )(
            index,
            tensors,
            rows[which].reshape(height, 1),
            columns[which].reshape(1, depth),
            after,
        )

    def absorb(first, rows_in, edge, tensor, frame, *more):
        main = site - 1
        mixed = pltpu.VMEM((tensor.shape[1], GROUP * LANES), BF16)
        spare = pltpu.VMEM((HALF_TILE * (-(-site // ROWS) * ROWS), LANES), F32)
        pushed = pltpu.VMEM((GROUP * main, tall), BF16)
        return call(
            functools.partial(absorb_kernel, bond, site, first),
            (rows_in, edge, tensor, frame) + more,
            [payload, wide] if first else [dense],
            ([] if first else [half_bf16])
            + [mixed, mixed, spare, spare, pushed, pushed]
            + [pltpu.VMEM((tall, LANES), F32), pltpu.VMEM(((LANES + GROUP) * main, LANES), F32)],
            28,
            25,
        )

    upper_packed, lower_packed = call(
        functools.partial(halves_kernel, bond, site),
        (c1, t1, c4, t3),
        [packed, packed],
        [],
        60,
        2,
    )
    upper_next = shift(upper_packed, "row", -1)
    lower_back = shift(lower_packed, "row", 1)
    pattern = pattern.reshape(1)
    pattern_back = shift(pattern, "row", 1)
    tensor_left = arrange(0, pattern, upper_packed)
    prepared = call(
        functools.partial(prepare_kernel, bond, site),
        (c2, t2, t4, t1, above, below, right, upper_packed, lower_packed),
        [wide, dense, stack, stack_f32, stack, stack_f32, packed, stack, stack_f32],
        [],
        16,
        2,
    )
    t4_wide, t1_held, upper, upper_sketch, lower, lower_sketch, side_packed, side, side_sketch = prepared
    t1_back = shift(t1_held, "row", 1)
    side_back = shift_both(side_packed, 1, 1)
    rows_left, frame_below, corner_top, corner_bottom, pattern_held = call(
        functools.partial(vertical_kernel, bond, site),
        (upper_next, lower_back, above, below, upper, upper_sketch, lower, lower_sketch)
        + (pattern_back,),
        [frame_rows, stack, corner, corner, shape_of((1,), jnp.int32)],
        [half_bf16, half_bf16, half_bf16] + frame_scratch,
        20,
        8,
    )
    left_new, edge_wide = absorb(True, rows_left, t4_wide, tensor_left, frame_below, corner_top)
    left_back = shift_both(left_new, 1, 1)
    inverse, frame_right = call(
        functools.partial(horizontal_kernel, bond, site),
        (corner_top, corner_bottom, edge_wide, left, side, side_sketch),
        [shape_of((LANES, 2 * LANES), F32), shape_of((bond, packed.shape[1] + LANES))],
        [half_bf16, half_bf16],
        16,
        5,
    )
    inverse_back = shift_both(inverse, 1, 1)
    frame_back = shift(frame_right, "row", 1)
    tensor_top = arrange(1, pattern_held, inverse)
    early_sketch, t1_wide = call(
        functools.partial(early_kernel, bond, site),
        (side_back, right, t1_back, inverse),
        [stack_f32, wide],
        [half_bf16],
        16,
        2,
        1,
    )
    rows_top, top_left, forward = call(
        functools.partial(arrive_kernel, bond, site),
        (left_back, early_sketch, left, inverse_back),
        [frame_rows, corner, shape_of((bond, payload.shape[1] + LANES))],
        [half_bf16, half_bf16] + frame_scratch,
        16,
        4,
    )
    left_here = shift(forward, "row", -1)
    (top_edge,) = absorb(False, rows_top, t1_wide, tensor_top, frame_back)
    left_corner, left_edge, left_bottom, top_right = call(
        functools.partial(finish_kernel, bond),
        (left_here, frame_back),
        [corner, dense, corner, corner],
        [],
        8,
        1,
    )
    return (left_corner, left_edge, left_bottom, top_left, top_edge, top_right)


def solution(mesh):
    block, whole = P("col", "row"), P()
    in_specs = (block,) * 7 + (whole, block) + (whole,) * 4
    return jax.shard_map(
        body, mesh=mesh, in_specs=in_specs, out_specs=(block,) * 6, check_vma=False
    )
```

```python
import functools

import jax
import jax.numpy as jnp
import numpy as np
from jax import lax
from jax.experimental import pallas as pl
from jax.experimental.pallas import tpu as pltpu
from jax.sharding import PartitionSpec as P

LANES = 128
ROWS = 8
HALF_TILE = 16
GROUP = 10
CUTS = 4
QUARTERS = 4
MIB = 1 << 20
F32 = jnp.float32
BF16 = jnp.bfloat16

NN = (((1,), (0,)), ((), ()))
NT = (((1,), (1,)), ((), ()))
TN = (((0,), (0,)), ((), ()))


def product(left, right, dims=NN):
    return lax.dot_general(left, right, dims, preferred_element_type=F32)


def halves(values):
    high = values.astype(BF16)
    return high, (values - high.astype(F32)).astype(BF16)


def product_split(left, right, dims=NN):
    left_high, left_low = halves(left)
    right_high, right_low = halves(right)
    axis_left, axis_right = dims[0][0][0], dims[0][1][0]
    both = jnp.concatenate([left_high, left_low], axis_left)
    twice = jnp.concatenate([right_high, right_high], axis_right)
    return product(both, twice, dims) + product(left_high, right_low, dims)


def index_of(shape, axis):
    return lax.broadcasted_iota(jnp.int32, shape, axis)


def square_of(ref, bond):
    shape = (LANES, LANES)
    keep = (index_of(shape, 0) < bond) & (index_of(shape, 1) < bond)
    return jnp.where(keep, ref[...].astype(F32), 0.0)


def spread(ref, bond, site):
    shape = (LANES, LANES)
    row, lane = index_of(shape, 0), index_of(shape, 1)
    keep = (row < bond) & (lane < bond)
    pieces = []
    for k in range(site):
        tile, offset = divmod(k * bond, LANES)
        piece = ref[:, tile * LANES : (tile + 1) * LANES].astype(F32)
        if offset:
            piece = pltpu.roll(piece, LANES - offset, 1)
        if offset + bond > LANES:
            more = ref[:, (tile + 1) * LANES : (tile + 2) * LANES].astype(F32)
            piece = jnp.where(lane < LANES - offset, piece, pltpu.roll(more, LANES - offset, 1))
        pieces.append(jnp.where(keep, piece, 0.0).astype(BF16))
    return pieces


def gather_dense(tiles, ref, bond):
    lane = index_of((LANES, LANES), 1)
    total = len(tiles) * bond
    for tile in range(-(-total // LANES)):
        begin = tile * LANES
        value = None
        for k in range(begin // bond, min(len(tiles) - 1, (begin + LANES - 1) // bond) + 1):
            shift = k * bond - begin
            piece = pltpu.roll(tiles[k], shift % LANES, 1) if shift % LANES else tiles[k]
            value = piece if value is None else jnp.where(lane >= shift, piece, value)
        ref[:, begin : begin + LANES] = value.astype(ref.dtype)


def pack(tiles, ref, bond):
    quarter = bond // QUARTERS
    lane = index_of((LANES, LANES), 1)
    for group in range(len(tiles) // (QUARTERS + 1)):
        first = group * (QUARTERS + 1)
        for m in range(QUARTERS):
            piece = pltpu.roll(tiles[first + QUARTERS], bond - m * quarter, 1)
            slot = group * QUARTERS + m
            value = jnp.where(lane < bond, tiles[first + m], piece)
            ref[:, slot * LANES : (slot + 1) * LANES] = value.astype(ref.dtype)


def unpack(ref, bond, site):
    quarter = bond // QUARTERS
    shape = (LANES, LANES)
    row, lane = index_of(shape, 0), index_of(shape, 1)
    keep = (row < bond) & (lane < bond)
    tiles = []
    for group in range(site // (QUARTERS + 1)):
        last = None
        for m in range(QUARTERS):
            slot = group * QUARTERS + m
            value = ref[:, slot * LANES : (slot + 1) * LANES].astype(F32)
            tiles.append(jnp.where(keep, value, 0.0).astype(BF16))
            piece = pltpu.roll(value, LANES - bond + m * quarter, 1)
            last = piece if last is None else jnp.where(lane >= m * quarter, piece, last)
        tiles.append(jnp.where(keep, last, 0.0).astype(BF16))
    return tiles


def sketched(stack, sketch):
    return product(jnp.concatenate([stack, stack], 1), jnp.concatenate(halves(sketch), 0))


def inverse_factors(grams, bond):
    count = -(-bond // ROWS) * ROWS
    shape = (count, LANES)
    row, lane = index_of(shape, 0), index_of(shape, 1)
    inside = (row < bond) & (lane < bond)
    eye = jnp.where(row == lane, 1.0, 0.0)
    work = [jnp.where(inside, gram[:count], eye) for gram in grams]
    done = [[] for _ in grams]
    for first in range(0, count, ROWS):
        height = count - first
        row, lane = index_of((height, LANES), 0), index_of((height, LANES), 1)
        block = (lane >= first) & (lane < first + ROWS)
        start = jnp.where(row == lane - first, 1.0, 0.0)
        small_row, small_lane = index_of((ROWS, LANES), 0), index_of((ROWS, LANES), 1)
        columns = []
        for n, matrix in enumerate(work):
            columns.append(
                [
                    jnp.broadcast_to(matrix[:, first + j : first + j + 1], (height, LANES))
                    for j in range(ROWS)
                ]
            )
            work[n] = jnp.where(block, start, matrix)
        pivots = [jnp.ones((ROWS, LANES), F32) for _ in work]
        for j in range(ROWS):
            for n in range(len(work)):
                column = columns[n]
                pivot = column[j][j : j + 1, :]
                factor = jnp.where(row > j, column[j] * (1.0 / pivot), 0.0)
                work[n] = work[n] - factor * work[n][j : j + 1, :]
                for later in range(j + 1, ROWS):
                    column[later] = column[later] - factor * column[later][j : j + 1, :]
                pivots[n] = jnp.where(small_row == j, pivot, pivots[n])
        for n in range(len(work)):
            scaled = work[n][:ROWS] * lax.rsqrt(pivots[n])
            done[n].append(jnp.where(small_lane <= small_row + first, scaled, 0.0))
            work[n] = work[n][ROWS:]
    tail = jnp.zeros((LANES - count, LANES), F32)
    keep = (index_of((LANES, LANES), 0) < bond) & (index_of((LANES, LANES), 1) < bond)
    return [jnp.where(keep, jnp.concatenate(parts + [tail], 0), 0.0) for parts in done]


def store_halves(values, high, low):
    high[...], low[...] = halves(values)


def gram_of(high, low):
    both = product(high[...], jnp.concatenate([high[...], low[...]], 1), TN)
    mixed = both[:, LANES:]
    return both[:, :LANES] + mixed + mixed.T


def overlap(other, high, low):
    both = product(other, jnp.concatenate([high[...], low[...]], 1), TN)
    return both[:, :LANES] + both[:, LANES:]


def frame_from(high, low, inverse):
    inverse_high, inverse_low = halves(inverse)
    left = jnp.concatenate([high[...], low[...], high[...]], 1)
    return product(left, jnp.concatenate([inverse_high, inverse_high, inverse_low], 1), NT)


def scaled_corner(values, bond):
    mean = jnp.sum(values * values) / (bond * bond)
    return (values / jnp.sqrt(mean + 1e-06)).astype(BF16)


def half_tiles(corner, pieces):
    return [product(corner, piece) for piece in pieces]


def fill(stack, tiles):
    for k, tile in enumerate(tiles):
        stack[k * LANES : (k + 1) * LANES, :] = tile.astype(stack.dtype)


def store_frame_rows(high, low, inverse, rows_ref, plain, tail, site):
    main = site - 1
    bond_rows = plain.shape[0] // main
    inverse_high, inverse_low = halves(inverse)
    left = jnp.concatenate([inverse_high, inverse_high, inverse_low], 1)[:bond_rows]
    for k in range(site):
        rows = slice(k * LANES, (k + 1) * LANES)
        tile = product(left, jnp.concatenate([high[rows, :], low[rows, :], high[rows, :]], 1), NT)
        if k < main:
            plain[pl.ds(k, bond_rows, stride=main), :] = tile
        else:
            for group in range(tail.shape[0] // HALF_TILE):
                begin = group * HALF_TILE
                tail[begin : begin + GROUP, :] = tile[group * GROUP : (group + 1) * GROUP]
    rows_ref[: plain.shape[0], :] = plain[...].astype(BF16)
    rows_ref[plain.shape[0] :, :] = tail[...].astype(BF16)


def halves_kernel(bond, site, c1, t1, c4, t3, upper_packed, lower_packed):
    for corner, edge, packed in ((c1, t1, upper_packed), (c4, t3, lower_packed)):
        pack(half_tiles(square_of(corner, bond).astype(BF16), spread(edge, bond, site)), packed, bond)


def prepare_kernel(
    bond, site, c2, t2, t4, t1, above, below, right, upper_packed, lower_packed,
    t4_wide, t1_out, upper, upper_sketch, lower, lower_sketch, side_packed, side, side_sketch,
):
    t1_out[...] = t1[...]
    tiles = half_tiles(square_of(c2, bond).astype(BF16), spread(t2, bond, site))
    fill(side, tiles)
    pack(tiles, side_packed, bond)
    fill(upper, unpack(upper_packed, bond, site))
    fill(lower, unpack(lower_packed, bond, site))
    upper_sketch[...] = sketched(upper[...], square_of(above, bond))
    lower_sketch[...] = sketched(lower[...], square_of(below, bond))
    side_sketch[...] = sketched(side[...], square_of(right, bond))
    for k, piece in enumerate(spread(t4, bond, site)):
        t4_wide[:, k * LANES : (k + 1) * LANES] = piece


def vertical_kernel(
    bond, site, upper_packed, lower_packed, above, below, upper, upper_sketch, lower, lower_sketch,
    rows_ref, frame_out, corner_top, corner_bottom, stack, over, over_low, under, under_low, plain, tail,
):
    fill(stack, unpack(upper_packed, bond, site))
    store_halves(lower_sketch[...] + sketched(stack[...], square_of(above, bond)), under, under_low)
    fill(stack, unpack(lower_packed, bond, site))
    store_halves(upper_sketch[...] + sketched(stack[...], square_of(below, bond)), over, over_low)
    grams = [gram_of(over, over_low), gram_of(under, under_low)]
    mixed_over = overlap(upper[...], over, over_low)
    mixed_under = overlap(lower[...], under, under_low)
    inverse_over, inverse_under = inverse_factors(grams, bond)
    store_frame_rows(over, over_low, inverse_over, rows_ref, plain, tail, site)
    frame_out[...] = frame_from(under, under_low, inverse_under).astype(BF16)
    corner_top[...] = scaled_corner(product_split(inverse_over, mixed_over, NT), bond)
    corner_bottom[...] = scaled_corner(product_split(inverse_under, mixed_under, NT), bond)


def horizontal_kernel(
    bond, site, c1, edge, left, side, side_sketch, inverse_ref, frame_out, half, total, total_low
):
    corner = square_of(c1, bond).T.astype(BF16)
    fill(half, half_tiles(corner, [edge[:, k * LANES : (k + 1) * LANES] for k in range(site)]))
    store_halves(side_sketch[...] + sketched(half[...], square_of(left, bond)), total, total_low)
    mixed = overlap(side[...], total, total_low)
    (inverse,) = inverse_factors([gram_of(total, total_low)], bond)
    inverse_ref[...] = inverse[: inverse_ref.shape[0]]
    frame = frame_from(total, total_low, inverse)
    pack([frame[k * LANES : (k + 1) * LANES, :] for k in range(site)], frame_out, bond)
    corner_right = scaled_corner(product_split(inverse, mixed, NT), bond)
    frame_out[:, frame_out.shape[1] - LANES :] = corner_right


def early_kernel(bond, site, side_packed, right, t1, after, side_sketch, t1_wide, stack):
    for k, piece in enumerate(spread(t1, bond, site)):
        t1_wide[:, k * LANES : (k + 1) * LANES] = piece
    fill(stack, unpack(side_packed, bond, site))
    side_sketch[...] = sketched(stack[...], square_of(right, bond))


def arrive_kernel(
    bond, site, payload, side_sketch, left, inverse_ref,
    rows_ref, corner_left, forward, half, total, total_low, plain, tail,
):
    start = payload.shape[1] - 2 * LANES
    corner = square_of(payload.at[:, start : start + LANES], bond).T.astype(BF16)
    fill(half, half_tiles(corner, spread(payload, bond, site)))
    store_halves(side_sketch[...] + sketched(half[...], square_of(left, bond)), total, total_low)
    rest = jnp.zeros((LANES - inverse_ref.shape[0], LANES), F32)
    inverse = jnp.concatenate([inverse_ref[...], rest], 0)
    store_frame_rows(total, total_low, inverse, rows_ref, plain, tail, site)
    mixed = overlap(half[...], total, total_low)
    corner_left[...] = scaled_corner(product_split(mixed, inverse, NT), bond)
    forward[...] = payload[...]


def finish_kernel(bond, payload, frame, left_corner, left_edge, left_bottom, top_right):
    start = payload.shape[1] - 2 * LANES
    left_edge[...] = payload[:, :start]
    left_corner[...] = payload[:, start : start + LANES]
    left_bottom[...] = payload[:, start + LANES :]
    top_right[...] = frame[:, frame.shape[1] - LANES :]


def absorb_kernel(bond, site, first, rows_ref, edge, tensor, frame, *refs):
    mixed_even, mixed_odd, spare_even, spare_odd, pushed_even, pushed_odd, last, result = refs[-8:]
    if first:
        corner, bottom, dense, wide = refs[:4]
        frame_out = frame
    else:
        dense, frame_out = refs[0], refs[1]
        fill(frame_out, unpack(frame, bond, site))
    main = site - 1
    groups = bond // GROUP
    tall = GROUP * main
    slot = spare_even.shape[0] // HALF_TILE
    spare_even[...] = jnp.zeros_like(spare_even)
    spare_odd[...] = jnp.zeros_like(spare_odd)
    ahead = tall + bond * main
    result[ahead:, :] = jnp.zeros((result.shape[0] - ahead, LANES), F32)

    def frames_of(group):
        body = rows_ref[pl.ds(pl.multiple_of(group * tall, tall), tall), :]
        begin = rows_ref.shape[0] - groups * HALF_TILE + group * HALF_TILE
        tail = rows_ref[pl.ds(pl.multiple_of(begin, HALF_TILE), HALF_TILE), :]
        return jnp.concatenate([body, tail], 0)

    def mix(frames, mixed, spare, unit):
        j = 2 * unit
        sides = min(2, site - j)
        both = product(frames, edge[:, j * LANES : (j + sides) * LANES])
        for side in range(sides):
            lanes = slice(side * LANES, (side + 1) * LANES)
            spare[pl.ds(j + side, HALF_TILE, stride=slot), :] = both[tall:, lanes]
        for p in range(GROUP):
            parts = [
                both[p * main : (p + 1) * main, side * LANES : (side + 1) * LANES]
                for side in range(sides)
            ]
            end = (j + sides) * main
            if sides == 1:
                end = mixed.shape[0]
                parts.append(spare[p * slot : (p + 1) * slot, :])
                parts.append(jnp.zeros((end - j * main - main - slot, LANES), F32))
            mixed[j * main : end, p * LANES : (p + 1) * LANES] = (
                jnp.concatenate(parts, 0).astype(BF16)
            )

    def push(group, mixed, pushed, pair):
        out = product(tensor[...], mixed[:, 2 * pair * LANES : (2 * pair + 2) * LANES])
        for k in range(site):
            parts = [
                out[k * main : (k + 1) * main, side * LANES : (side + 1) * LANES]
                for side in range(2)
            ]
            pushed[2 * pair * main : (2 * pair + 2) * main, k * LANES : (k + 1) * LANES] = (
                jnp.concatenate(parts, 0).astype(BF16)
            )
        for side in range(2):
            place = group * GROUP + 2 * pair + side
            last[pl.ds(place, site, stride=LANES), :] = out[
                site * main : site * main + site, side * LANES : (side + 1) * LANES
            ]

    def cuts():
        step = -(-site // CUTS) // 2 * 2
        starts = [n * step for n in range(CUTS)] + [site]
        return [slice(low * LANES, high * LANES) for low, high in zip(starts, starts[1:])]

    def close(group, total):
        result[pl.ds(pl.multiple_of((group + 1) * tall, tall), tall), :] = total

    units = (site + 1) // 2

    def stage(group, mixed, pushed, mixed_next, spare_next, pushed_before):
        frames = frames_of(jnp.minimum(group + 1, groups - 1))
        total = jnp.zeros((tall, LANES), F32)
        pairs = GROUP // 2
        parts = cuts()
        for n in range(pairs):
            push(group, mixed, pushed, n)
            for unit in range(n * units // pairs, (n + 1) * units // pairs):
                mix(frames, mixed_next, spare_next, unit)
            if n < CUTS:
                total = total + product(pushed_before[:, parts[n]], frame_out[parts[n], :])
        close(group - 1, total)

    frames = frames_of(0)
    for unit in range(units):
        mix(frames, mixed_even, spare_even, unit)

    def step(index, carry):
        stage(2 * index, mixed_even, pushed_even, mixed_odd, spare_odd, pushed_odd)
        stage(2 * index + 1, mixed_odd, pushed_odd, mixed_even, spare_even, pushed_even)
        return carry

    lax.fori_loop(0, groups // 2, step, 0)
    close(groups - 1, product(pushed_odd[...], frame_out[...]))
    tiles = [result[pl.ds(tall + k, LANES, stride=main), :] for k in range(main)]
    total = jnp.zeros((LANES, LANES), F32)
    for k in range(site):
        rows = pl.ds(k * LANES, LANES)
        total = total + product(last[rows, :].astype(BF16), frame_out[rows, :])
    tiles.append(jnp.where(index_of(total.shape, 0) < bond, total, 0.0))
    squares = tiles[0] * tiles[0]
    for tile in tiles[1:]:
        squares = squares + tile * tile
    scale = 1.0 / jnp.sqrt(jnp.sum(squares) / (bond * bond * site) + 1e-06)
    tiles = [tile * scale for tile in tiles]
    gather_dense(tiles, dense, bond)
    if first:
        for k, tile in enumerate(tiles):
            wide[:, k * LANES : (k + 1) * LANES] = tile.astype(BF16)
        start = dense.shape[1] - 2 * LANES
        dense[:, start : start + LANES] = square_of(corner, bond).astype(BF16)
        dense[:, start + LANES :] = square_of(bottom, bond).astype(BF16)


def pick_kernel(pattern, tensors, out, *tiles):
    height, count, width = tensors.shape
    values = tensors[...].astype(F32).reshape(height * count, width)
    for n, tile in enumerate(tiles):
        end = min(width, (n + 1) * LANES)
        tile[:, : end - n * LANES] = values[:, n * LANES : end]
        rows = tile[pl.ds(pattern[0], height, stride=count), :]
        out[:, n * LANES : end] = rows[:, : end - n * LANES].astype(BF16)


def arrange_kernel(tensor, rows, columns, after, out):
    square = tensor.shape[0]
    pick_rows = jnp.where(index_of((rows.shape[0], square), 1) == rows[...], 1.0, 0.0).astype(BF16)
    pick_columns = jnp.where(index_of((square, columns.shape[1]), 0) == columns[...], 1.0, 0.0)
    turned = product(pick_rows, tensor[...], NT).astype(BF16)
    out[...] = product(turned, pick_columns.astype(BF16)).astype(BF16)


def places(site):
    main = site - 1
    size = -(-site * site // LANES) * LANES
    rows = np.full((2, size), -1, np.int32)
    columns = np.full((2, size), -1, np.int32)
    for other in range(site):
        for inner in range(site):
            at = other * main + inner if inner < main else site * main + other
            rows[0, at] = other * site + inner
            rows[1, at] = inner * site + other
            columns[0, at] = inner * site + other
            columns[1, at] = other * site + inner
    return rows, columns


def block_of(arg):
    shape = arg.shape
    if len(shape) == 1:
        return pl.BlockSpec(memory_space=pltpu.SMEM)
    if shape[0] % 16 == 0 and shape[1] % LANES == 0:
        return pl.BlockSpec(memory_space=pltpu.VMEM)
    return pl.BlockSpec(tuple(-(-size // LANES) * LANES for size in shape), lambda i: (0, 0))


def cost(microseconds):
    return pl.CostEstimate(
        flops=microseconds * 1_000_000_000, bytes_accessed=microseconds * 1_000_000, transcendentals=0
    )


def call(kernel, args, outs, scratch, limit, microseconds, unread=0):
    specs = [block_of(arg) for arg in args]
    if unread:
        specs[-unread:] = [pl.BlockSpec(memory_space=pl.ANY)] * unread
    return pl.pallas_call(
        kernel,
        grid=(1,),
        in_specs=specs,
        out_specs=[block_of(out) for out in outs],
        out_shape=outs,
        scratch_shapes=scratch,
        compiler_params=pltpu.CompilerParams(vmem_limit_bytes=limit * MIB),
        cost_estimate=cost(microseconds),
    )(*args)


def shape_of(shape, dtype=BF16):
    return jax.ShapeDtypeStruct(shape, dtype)


def shift(value, axis, steps):
    count = lax.axis_size(axis)
    pairs = [(source, (source + steps) % count) for source in range(count)]
    return lax.ppermute(value, axis, pairs)


def shift_both(value, steps_col, steps_row):
    columns, rows = lax.axis_size("col"), lax.axis_size("row")
    pairs = []
    for x in range(columns):
        for y in range(rows):
            target = (x + steps_col) % columns * rows + (y + steps_row) % rows
            pairs.append((x * rows + y, target))
    return lax.ppermute(value, ("col", "row"), pairs)


def body(c1, c2, c4, t1, t2, t3, t4, tensors, pattern, below, above, right, left):
    bond = c1.shape[0]
    site = t1.shape[1] // bond
    square = site * site
    tall = site * LANES
    bond_rows = -(-bond // ROWS) * ROWS
    body_rows = bond_rows * (site - 1)
    tail_rows = bond // GROUP * HALF_TILE
    frame_rows = shape_of((body_rows + tail_rows, LANES))
    packed = shape_of((bond, site // (QUARTERS + 1) * QUARTERS * LANES))
    dense = shape_of((bond, site * bond))
    wide = shape_of((LANES, tall))
    stack = shape_of((tall, LANES))
    stack_f32 = shape_of((tall, LANES), F32)
    corner = shape_of((bond, bond))
    payload = shape_of((bond, -(-site * bond // LANES) * LANES + 2 * LANES))
    half_bf16 = pltpu.VMEM((tall, LANES), BF16)
    frame_scratch = [pltpu.VMEM((body_rows, LANES), F32), pltpu.VMEM((tail_rows, LANES), F32)]
    rows, columns = places(site)

    def pick(index):
        count = tensors.shape[0]
        return pl.pallas_call(
            pick_kernel,
            grid=(-(-square // LANES),),
            in_specs=[
                pl.BlockSpec(memory_space=pltpu.SMEM),
                pl.BlockSpec((LANES, count, square), lambda i: (i, 0, 0)),
            ],
            out_specs=pl.BlockSpec((LANES, square), lambda i: (i, 0)),
            out_shape=shape_of((square, square)),
            scratch_shapes=[pltpu.VMEM((LANES * count, LANES), F32)] * -(-square // LANES),
            compiler_params=pltpu.CompilerParams(vmem_limit_bytes=16 * MIB),
            cost_estimate=cost(2),
        )(index, tensors.transpose(1, 0, 2))

    def arrange(which, tensor, after):
        height, depth = rows.shape[1], columns.shape[1]
        vmem = pl.BlockSpec(memory_space=pltpu.VMEM)
        return pl.pallas_call(
            arrange_kernel,
            in_specs=[vmem, vmem, vmem, pl.BlockSpec(memory_space=pl.ANY)],
            out_specs=vmem,
            out_shape=shape_of((height, depth)),
            compiler_params=pltpu.CompilerParams(vmem_limit_bytes=16 * MIB),
            cost_estimate=cost(2),
        )(
            tensor,
            rows[which].reshape(height, 1),
            columns[which].reshape(1, depth),
            after,
        )

    def absorb(first, rows_in, edge, tensor, frame, *more):
        main = site - 1
        mixed = pltpu.VMEM((tensor.shape[1], GROUP * LANES), BF16)
        spare = pltpu.VMEM((HALF_TILE * (-(-site // ROWS) * ROWS), LANES), F32)
        pushed = pltpu.VMEM((GROUP * main, tall), BF16)
        return call(
            functools.partial(absorb_kernel, bond, site, first),
            (rows_in, edge, tensor, frame) + more,
            [payload, wide] if first else [dense],
            ([] if first else [half_bf16])
            + [mixed, mixed, spare, spare, pushed, pushed]
            + [pltpu.VMEM((tall, LANES), F32), pltpu.VMEM(((LANES + GROUP) * main, LANES), F32)],
            28,
            25,
        )

    upper_packed, lower_packed = call(
        functools.partial(halves_kernel, bond, site),
        (c1, t1, c4, t3),
        [packed, packed],
        [],
        60,
        2,
    )
    upper_next = shift(upper_packed, "row", -1)
    lower_back = shift(lower_packed, "row", 1)
    tensor = pick(pattern.reshape(1))
    tensor_left = arrange(0, tensor, upper_packed)
    prepared = call(
        functools.partial(prepare_kernel, bond, site),
        (c2, t2, t4, t1, above, below, right, upper_packed, lower_packed),
        [wide, dense, stack, stack_f32, stack, stack_f32, packed, stack, stack_f32],
        [],
        16,
        2,
    )
    t4_wide, t1_held, upper, upper_sketch, lower, lower_sketch, side_packed, side, side_sketch = prepared
    t1_back = shift(t1_held, "row", 1)
    side_back = shift_both(side_packed, 1, 1)
    tensor_back = shift(tensor, "row", 1)
    rows_left, frame_below, corner_top, corner_bottom = call(
        functools.partial(vertical_kernel, bond, site),
        (upper_next, lower_back, above, below, upper, upper_sketch, lower, lower_sketch),
        [frame_rows, stack, corner, corner],
        [half_bf16] * 5 + frame_scratch,
        20,
        8,
    )
    left_new, edge_wide = absorb(True, rows_left, t4_wide, tensor_left, frame_below, corner_top, corner_bottom)
    left_back = shift_both(left_new, 1, 1)
    inverse, frame_right = call(
        functools.partial(horizontal_kernel, bond, site),
        (corner_top, edge_wide, left, side, side_sketch),
        [shape_of((-(-bond // HALF_TILE) * HALF_TILE, LANES), F32), shape_of((bond, packed.shape[1] + LANES))],
        [half_bf16] * 3,
        16,
        5,
    )
    inverse_back = shift_both(inverse, 1, 1)
    frame_back = shift(frame_right, "row", 1)
    tensor_top = arrange(1, tensor_back, inverse)
    early_sketch, t1_wide = call(
        functools.partial(early_kernel, bond, site),
        (side_back, right, t1_back, inverse),
        [stack_f32, wide],
        [half_bf16],
        16,
        2,
        1,
    )
    rows_top, top_left, forward = call(
        functools.partial(arrive_kernel, bond, site),
        (left_back, early_sketch, left, inverse_back),
        [frame_rows, corner, payload],
        [half_bf16] * 3 + frame_scratch,
        16,
        4,
    )
    left_here = shift(forward, "row", -1)
    (top_edge,) = absorb(False, rows_top, t1_wide, tensor_top, frame_back)
    left_corner, left_edge, left_bottom, top_right = call(
        functools.partial(finish_kernel, bond),
        (left_here, frame_back),
        [corner, dense, corner, corner],
        [],
        8,
        1,
    )
    return (left_corner, left_edge, left_bottom, top_left, top_edge, top_right)


def solution(mesh):
    block, whole = P("col", "row"), P()
    in_specs = (block,) * 7 + (whole, block) + (whole,) * 4
    return jax.shard_map(
        body, mesh=mesh, in_specs=in_specs, out_specs=(block,) * 6, check_vma=False
    )
```

```python
import functools

import jax
import jax.numpy as jnp
import numpy as np
from jax import lax
from jax.experimental import pallas as pl
from jax.experimental.pallas import tpu as pltpu
from jax.sharding import PartitionSpec as P

LANES = 128
ROWS = 8
HALF_TILE = 16
GROUP = 10
CUTS = 4
QUARTERS = 4
MIB = 1 << 20
F32 = jnp.float32
BF16 = jnp.bfloat16

NN = (((1,), (0,)), ((), ()))
NT = (((1,), (1,)), ((), ()))
TN = (((0,), (0,)), ((), ()))


def product(left, right, dims=NN):
    return lax.dot_general(left, right, dims, preferred_element_type=F32)


def halves(values):
    high = values.astype(BF16)
    return high, (values - high.astype(F32)).astype(BF16)


def product_split(left, right, dims=NN):
    left_high, left_low = halves(left)
    right_high, right_low = halves(right)
    axis_left, axis_right = dims[0][0][0], dims[0][1][0]
    both = jnp.concatenate([left_high, left_low], axis_left)
    twice = jnp.concatenate([right_high, right_high], axis_right)
    return product(both, twice, dims) + product(left_high, right_low, dims)


def index_of(shape, axis):
    return lax.broadcasted_iota(jnp.int32, shape, axis)


def square_of(ref, bond):
    shape = (LANES, LANES)
    keep = (index_of(shape, 0) < bond) & (index_of(shape, 1) < bond)
    return jnp.where(keep, ref[...].astype(F32), 0.0)


def spread(ref, bond, site):
    shape = (LANES, LANES)
    row, lane = index_of(shape, 0), index_of(shape, 1)
    keep = (row < bond) & (lane < bond)
    zero = jnp.zeros(shape, BF16)
    pieces = []
    for k in range(site):
        tile, offset = divmod(k * bond, LANES)
        piece = ref[:, tile * LANES : (tile + 1) * LANES]
        if offset:
            piece = pltpu.roll(piece, LANES - offset, 1)
        if offset + bond > LANES:
            more = ref[:, (tile + 1) * LANES : (tile + 2) * LANES]
            piece = jnp.where(lane < LANES - offset, piece, pltpu.roll(more, LANES - offset, 1))
        pieces.append(jnp.where(keep, piece, zero))
    return pieces


def gather_dense(tiles, ref, bond):
    lane = index_of((LANES, LANES), 1)
    total = len(tiles) * bond
    for tile in range(-(-total // LANES)):
        begin = tile * LANES
        value = None
        for k in range(begin // bond, min(len(tiles) - 1, (begin + LANES - 1) // bond) + 1):
            shift = k * bond - begin
            piece = pltpu.roll(tiles[k], shift % LANES, 1) if shift % LANES else tiles[k]
            value = piece if value is None else jnp.where(lane >= shift, piece, value)
        ref[:, begin : begin + LANES] = value


def pack(tiles, ref, bond):
    quarter = bond // QUARTERS
    lane = index_of((LANES, LANES), 1)
    tiles = [tile.astype(BF16) for tile in tiles]
    for group in range(len(tiles) // (QUARTERS + 1)):
        first = group * (QUARTERS + 1)
        for m in range(QUARTERS):
            piece = pltpu.roll(tiles[first + QUARTERS], bond - m * quarter, 1)
            slot = group * QUARTERS + m
            value = jnp.where(lane < bond, tiles[first + m], piece)
            ref[:, slot * LANES : (slot + 1) * LANES] = value


def unpack(ref, bond, site):
    quarter = bond // QUARTERS
    shape = (LANES, LANES)
    row, lane = index_of(shape, 0), index_of(shape, 1)
    keep = (row < bond) & (lane < bond)
    zero = jnp.zeros(shape, BF16)
    tiles = []
    for group in range(site // (QUARTERS + 1)):
        last = None
        for m in range(QUARTERS):
            slot = group * QUARTERS + m
            value = ref[:, slot * LANES : (slot + 1) * LANES]
            tiles.append(jnp.where(keep, value, zero))
            piece = pltpu.roll(value, LANES - bond + m * quarter, 1)
            last = piece if last is None else jnp.where(lane >= m * quarter, piece, last)
        tiles.append(jnp.where(keep, last, zero))
    return tiles


def sketched(stack, sketch):
    return product(jnp.concatenate([stack, stack], 1), jnp.concatenate(halves(sketch), 0))


def inverse_factors(grams, bond):
    count = -(-bond // ROWS) * ROWS
    shape = (count, LANES)
    row, lane = index_of(shape, 0), index_of(shape, 1)
    inside = (row < bond) & (lane < bond)
    eye = jnp.where(row == lane, 1.0, 0.0)
    work = [jnp.where(inside, gram[:count], eye) for gram in grams]
    done = [[] for _ in grams]
    for first in range(0, count, ROWS):
        height = count - first
        row, lane = index_of((height, LANES), 0), index_of((height, LANES), 1)
        block = (lane >= first) & (lane < first + ROWS)
        start = jnp.where(row == lane - first, 1.0, 0.0)
        small_row, small_lane = index_of((ROWS, LANES), 0), index_of((ROWS, LANES), 1)
        columns = []
        for n, matrix in enumerate(work):
            columns.append(
                [
                    jnp.broadcast_to(matrix[:, first + j : first + j + 1], (height, LANES))
                    for j in range(ROWS)
                ]
            )
            work[n] = jnp.where(block, start, matrix)
        pivots = [jnp.ones((ROWS, LANES), F32) for _ in work]
        pivot = [column[0][:1, :] for column in columns]
        for j in range(ROWS):
            for n in range(len(work)):
                column = columns[n]
                inverse = 1.0 / pivot[n]
                pivots[n] = jnp.where(small_row == j, pivot[n], pivots[n])
                if j + 1 < ROWS:
                    at = slice(j + 1, j + 2)
                    cross = column[j][at, :] * column[j + 1][j : j + 1, :]
                    pivot[n] = column[j + 1][at, :] - cross * inverse
                factor = jnp.where(row > j, column[j], 0.0) * inverse
                for later in range(j + 1, ROWS):
                    column[later] = column[later] - factor * column[later][j : j + 1, :]
                work[n] = work[n] - factor * work[n][j : j + 1, :]
        for n in range(len(work)):
            scaled = work[n][:ROWS] * lax.rsqrt(pivots[n])
            done[n].append(jnp.where(small_lane <= small_row + first, scaled, 0.0))
            work[n] = work[n][ROWS:]
    tail = jnp.zeros((LANES - count, LANES), F32)
    keep = (index_of((LANES, LANES), 0) < bond) & (index_of((LANES, LANES), 1) < bond)
    return [jnp.where(keep, jnp.concatenate(parts + [tail], 0), 0.0) for parts in done]


def store_halves(values, high, low):
    high[...], low[...] = halves(values)


def gram_of(high, low):
    both = product(high[...], jnp.concatenate([high[...], low[...]], 1), TN)
    mixed = both[:, LANES:]
    return both[:, :LANES] + mixed + mixed.T


def overlap(other, high, low):
    both = product(other, jnp.concatenate([high[...], low[...]], 1), TN)
    return both[:, :LANES] + both[:, LANES:]


def frame_from(high, low, inverse):
    inverse_high, inverse_low = halves(inverse)
    left = jnp.concatenate([high[...], low[...], high[...]], 1)
    return product(left, jnp.concatenate([inverse_high, inverse_high, inverse_low], 1), NT)


def scaled_corner(values, bond):
    mean = jnp.sum(values * values) / (bond * bond)
    return (values / jnp.sqrt(mean + 1e-06)).astype(BF16)


def half_tiles(corner, pieces):
    return [product(corner, piece) for piece in pieces]


def fill(stack, tiles):
    for k, tile in enumerate(tiles):
        stack[k * LANES : (k + 1) * LANES, :] = tile.astype(stack.dtype)


def store_frame_rows(high, low, inverse, rows_ref, plain, tail, site):
    main = site - 1
    bond_rows = plain.shape[0] // main
    inverse_high, inverse_low = halves(inverse)
    left = jnp.concatenate([inverse_high, inverse_high, inverse_low], 1)[:bond_rows]
    for k in range(site):
        rows = slice(k * LANES, (k + 1) * LANES)
        tile = product(left, jnp.concatenate([high[rows, :], low[rows, :], high[rows, :]], 1), NT)
        if k < main:
            plain[pl.ds(k, bond_rows, stride=main), :] = tile
        else:
            for group in range(tail.shape[0] // HALF_TILE):
                begin = group * HALF_TILE
                tail[begin : begin + GROUP, :] = tile[group * GROUP : (group + 1) * GROUP]
    rows_ref[: plain.shape[0], :] = plain[...].astype(BF16)
    rows_ref[plain.shape[0] :, :] = tail[...].astype(BF16)


def halves_kernel(bond, site, c1, t1, c4, t3, upper_packed, lower_packed):
    for corner, edge, packed in ((c1, t1, upper_packed), (c4, t3, lower_packed)):
        pack(half_tiles(square_of(corner, bond).astype(BF16), spread(edge, bond, site)), packed, bond)


def prepare_kernel(
    bond, site, c2, t2, t4, above, below, right, upper_packed, lower_packed,
    t4_wide, upper, upper_sketch, lower, lower_sketch, side_packed, side, side_sketch,
):
    tiles = half_tiles(square_of(c2, bond).astype(BF16), spread(t2, bond, site))
    fill(side, tiles)
    pack(tiles, side_packed, bond)
    fill(upper, unpack(upper_packed, bond, site))
    fill(lower, unpack(lower_packed, bond, site))
    upper_sketch[...] = sketched(upper[...], square_of(above, bond))
    lower_sketch[...] = sketched(lower[...], square_of(below, bond))
    side_sketch[...] = sketched(side[...], square_of(right, bond))
    for k, piece in enumerate(spread(t4, bond, site)):
        t4_wide[:, k * LANES : (k + 1) * LANES] = piece


def vertical_kernel(
    bond, site, upper_packed, lower_packed, above, below, upper, upper_sketch, lower, lower_sketch,
    rows_ref, frame_out, corner_top, corner_bottom, stack, over, over_low, under, under_low, plain, tail,
):
    fill(stack, unpack(upper_packed, bond, site))
    store_halves(lower_sketch[...] + sketched(stack[...], square_of(above, bond)), under, under_low)
    fill(stack, unpack(lower_packed, bond, site))
    store_halves(upper_sketch[...] + sketched(stack[...], square_of(below, bond)), over, over_low)
    grams = [gram_of(over, over_low), gram_of(under, under_low)]
    mixed_over = overlap(upper[...], over, over_low)
    mixed_under = overlap(lower[...], under, under_low)
    inverse_over, inverse_under = inverse_factors(grams, bond)
    store_frame_rows(over, over_low, inverse_over, rows_ref, plain, tail, site)
    frame_out[...] = frame_from(under, under_low, inverse_under).astype(BF16)
    corner_top[...] = scaled_corner(product_split(inverse_over, mixed_over, NT), bond)
    corner_bottom[...] = scaled_corner(product_split(inverse_under, mixed_under, NT), bond)


def horizontal_kernel(
    bond, site, c1, edge, left, side, side_sketch, inverse_ref, frame_out, half, total, total_low
):
    corner = square_of(c1, bond).T.astype(BF16)
    fill(half, half_tiles(corner, [edge[:, k * LANES : (k + 1) * LANES] for k in range(site)]))
    store_halves(side_sketch[...] + sketched(half[...], square_of(left, bond)), total, total_low)
    mixed = overlap(side[...], total, total_low)
    (inverse,) = inverse_factors([gram_of(total, total_low)], bond)
    inverse_ref[...] = inverse[: inverse_ref.shape[0]]
    frame = frame_from(total, total_low, inverse)
    pack([frame[k * LANES : (k + 1) * LANES, :] for k in range(site)], frame_out, bond)
    corner_right = scaled_corner(product_split(inverse, mixed, NT), bond)
    frame_out[:, frame_out.shape[1] - LANES :] = corner_right


def early_kernel(bond, site, side_packed, right, t1, after, side_sketch, t1_wide, stack):
    for k, piece in enumerate(spread(t1, bond, site)):
        t1_wide[:, k * LANES : (k + 1) * LANES] = piece
    fill(stack, unpack(side_packed, bond, site))
    side_sketch[...] = sketched(stack[...], square_of(right, bond))


def arrive_kernel(
    bond, site, payload, side_sketch, left, inverse_ref,
    rows_ref, corner_left, forward, half, total, total_low, plain, tail,
):
    start = payload.shape[1] - 2 * LANES
    corner = square_of(payload.at[:, start : start + LANES], bond).T.astype(BF16)
    fill(half, half_tiles(corner, spread(payload, bond, site)))
    store_halves(side_sketch[...] + sketched(half[...], square_of(left, bond)), total, total_low)
    rest = jnp.zeros((LANES - inverse_ref.shape[0], LANES), F32)
    inverse = jnp.concatenate([inverse_ref[...], rest], 0)
    store_frame_rows(total, total_low, inverse, rows_ref, plain, tail, site)
    mixed = overlap(half[...], total, total_low)
    corner_left[...] = scaled_corner(product_split(mixed, inverse, NT), bond)
    forward[...] = payload[...]


def finish_kernel(bond, payload, frame, left_corner, left_edge, left_bottom, top_right):
    start = payload.shape[1] - 2 * LANES
    left_edge[...] = payload[:, :start]
    left_corner[...] = payload[:, start : start + LANES]
    left_bottom[...] = payload[:, start + LANES :]
    top_right[...] = frame[:, frame.shape[1] - LANES :]


def absorb_kernel(bond, site, first, rows_ref, edge, tensor, frame, *refs):
    mixed_even, mixed_odd, spare_even, spare_odd, pushed_even, pushed_odd, last, result = refs[-8:]
    if first:
        corner, bottom, dense, wide = refs[:4]
        frame_out = frame
    else:
        dense, frame_out = refs[0], refs[1]
        fill(frame_out, unpack(frame, bond, site))
    main = site - 1
    groups = bond // GROUP
    tall = GROUP * main
    slot = spare_even.shape[0] // HALF_TILE
    spare_even[...] = jnp.zeros_like(spare_even)
    spare_odd[...] = jnp.zeros_like(spare_odd)
    ahead = tall + bond * main
    result[ahead:, :] = jnp.zeros((result.shape[0] - ahead, LANES), F32)

    def frames_of(group):
        body = rows_ref[pl.ds(pl.multiple_of(group * tall, tall), tall), :]
        begin = rows_ref.shape[0] - groups * HALF_TILE + group * HALF_TILE
        tail = rows_ref[pl.ds(pl.multiple_of(begin, HALF_TILE), HALF_TILE), :]
        return jnp.concatenate([body, tail], 0)

    def mix(frames, mixed, spare, unit):
        j = 2 * unit
        sides = min(2, site - j)
        both = product(frames, edge[:, j * LANES : (j + sides) * LANES])
        for side in range(sides):
            lanes = slice(side * LANES, (side + 1) * LANES)
            spare[pl.ds(j + side, HALF_TILE, stride=slot), :] = both[tall:, lanes]
        for p in range(GROUP):
            parts = [
                both[p * main : (p + 1) * main, side * LANES : (side + 1) * LANES]
                for side in range(sides)
            ]
            end = (j + sides) * main
            if sides == 1:
                end = mixed.shape[0]
                parts.append(spare[p * slot : (p + 1) * slot, :])
                parts.append(jnp.zeros((end - j * main - main - slot, LANES), F32))
            mixed[j * main : end, p * LANES : (p + 1) * LANES] = (
                jnp.concatenate(parts, 0).astype(BF16)
            )

    def push(group, mixed, pushed, pair):
        out = product(tensor[...], mixed[:, 2 * pair * LANES : (2 * pair + 2) * LANES])
        for k in range(site):
            parts = [
                out[k * main : (k + 1) * main, side * LANES : (side + 1) * LANES]
                for side in range(2)
            ]
            pushed[2 * pair * main : (2 * pair + 2) * main, k * LANES : (k + 1) * LANES] = (
                jnp.concatenate(parts, 0).astype(BF16)
            )
        for side in range(2):
            place = group * GROUP + 2 * pair + side
            last[pl.ds(place, site, stride=LANES), :] = out[
                site * main : site * main + site, side * LANES : (side + 1) * LANES
            ]

    def cuts():
        step = -(-site // CUTS) // 2 * 2
        starts = [n * step for n in range(CUTS)] + [site]
        return [slice(low * LANES, high * LANES) for low, high in zip(starts, starts[1:])]

    def close(group, total):
        result[pl.ds(pl.multiple_of((group + 1) * tall, tall), tall), :] = total

    units = (site + 1) // 2

    def stage(group, mixed, pushed, mixed_next, spare_next, pushed_before):
        frames = frames_of(jnp.minimum(group + 1, groups - 1))
        total = jnp.zeros((tall, LANES), F32)
        pairs = GROUP // 2
        parts = cuts()
        for n in range(pairs):
            push(group, mixed, pushed, n)
            for unit in range(n * units // pairs, (n + 1) * units // pairs):
                mix(frames, mixed_next, spare_next, unit)
            if n < CUTS:
                total = total + product(pushed_before[:, parts[n]], frame_out[parts[n], :])
        close(group - 1, total)

    frames = frames_of(0)
    for unit in range(units):
        mix(frames, mixed_even, spare_even, unit)

    def step(index, carry):
        stage(2 * index, mixed_even, pushed_even, mixed_odd, spare_odd, pushed_odd)
        stage(2 * index + 1, mixed_odd, pushed_odd, mixed_even, spare_even, pushed_even)
        return carry

    lax.fori_loop(0, groups // 2, step, 0)
    close(groups - 1, product(pushed_odd[...], frame_out[...]))
    tiles = [result[pl.ds(tall + k, LANES, stride=main), :] for k in range(main)]
    total = jnp.zeros((LANES, LANES), F32)
    for k in range(site):
        rows = pl.ds(k * LANES, LANES)
        total = total + product(last[rows, :].astype(BF16), frame_out[rows, :])
    tiles.append(jnp.where(index_of(total.shape, 0) < bond, total, 0.0))
    squares = tiles[0] * tiles[0]
    for tile in tiles[1:]:
        squares = squares + tile * tile
    scale = 1.0 / jnp.sqrt(jnp.sum(squares) / (bond * bond * site) + 1e-06)
    tiles = [(tile * scale).astype(BF16) for tile in tiles]
    gather_dense(tiles, dense, bond)
    if first:
        for k, tile in enumerate(tiles):
            wide[:, k * LANES : (k + 1) * LANES] = tile
        start = dense.shape[1] - 2 * LANES
        dense[:, start : start + LANES] = square_of(corner, bond).astype(BF16)
        dense[:, start + LANES :] = square_of(bottom, bond).astype(BF16)


def pick_kernel(pattern, tensors, after, out, *tiles):
    height, count, width = tensors.shape
    values = tensors[...].astype(F32).reshape(height * count, width)
    for n, tile in enumerate(tiles):
        end = min(width, (n + 1) * LANES)
        tile[:, : end - n * LANES] = values[:, n * LANES : end]
        rows = tile[pl.ds(pattern[0], height, stride=count), :]
        out[:, n * LANES : end] = rows[:, : end - n * LANES].astype(BF16)


def arrange_kernel(count, tensor, rows, columns, *refs):
    held, out, copies = refs[:count], refs[-count - 1], refs[len(refs) - count :]
    for source, target in zip(held, copies):
        target[...] = source[...]
    square = tensor.shape[0]
    pick_rows = jnp.where(index_of((rows.shape[0], square), 1) == rows[...], 1.0, 0.0).astype(BF16)
    pick_columns = jnp.where(index_of((square, columns.shape[1]), 0) == columns[...], 1.0, 0.0)
    turned = product(pick_rows, tensor[...], NT).astype(BF16)
    out[...] = product(turned, pick_columns.astype(BF16)).astype(BF16)


def places(site):
    main = site - 1
    size = -(-site * site // LANES) * LANES
    rows = np.full((2, size), -1, np.int32)
    columns = np.full((2, size), -1, np.int32)
    for other in range(site):
        for inner in range(site):
            at = other * main + inner if inner < main else site * main + other
            rows[0, at] = other * site + inner
            rows[1, at] = inner * site + other
            columns[0, at] = inner * site + other
            columns[1, at] = other * site + inner
    return rows, columns


def block_of(arg):
    shape = arg.shape
    if len(shape) == 1:
        return pl.BlockSpec(memory_space=pltpu.SMEM)
    if shape[0] % 16 == 0 and shape[1] % LANES == 0:
        return pl.BlockSpec(memory_space=pltpu.VMEM)
    return pl.BlockSpec(tuple(-(-size // LANES) * LANES for size in shape), lambda i: (0, 0))


def cost(microseconds):
    return pl.CostEstimate(
        flops=microseconds * 1_000_000_000, bytes_accessed=microseconds * 1_000_000, transcendentals=0
    )


def call(kernel, args, outs, scratch, limit, microseconds, unread=0):
    specs = [block_of(arg) for arg in args]
    if unread:
        specs[-unread:] = [pl.BlockSpec(memory_space=pl.ANY)] * unread
    return pl.pallas_call(
        kernel,
        grid=(1,),
        in_specs=specs,
        out_specs=[block_of(out) for out in outs],
        out_shape=outs,
        scratch_shapes=scratch,
        compiler_params=pltpu.CompilerParams(vmem_limit_bytes=limit * MIB),
        cost_estimate=cost(microseconds),
    )(*args)


def shape_of(shape, dtype=BF16):
    return jax.ShapeDtypeStruct(shape, dtype)


def shift(value, axis, steps):
    count = lax.axis_size(axis)
    pairs = [(source, (source + steps) % count) for source in range(count)]
    return lax.ppermute(value, axis, pairs)


def shift_both(value, steps_col, steps_row):
    columns, rows = lax.axis_size("col"), lax.axis_size("row")
    pairs = []
    for x in range(columns):
        for y in range(rows):
            target = (x + steps_col) % columns * rows + (y + steps_row) % rows
            pairs.append((x * rows + y, target))
    return lax.ppermute(value, ("col", "row"), pairs)


def body(c1, c2, c4, t1, t2, t3, t4, tensors, pattern, below, above, right, left):
    bond = c1.shape[0]
    site = t1.shape[1] // bond
    square = site * site
    tall = site * LANES
    bond_rows = -(-bond // ROWS) * ROWS
    body_rows = bond_rows * (site - 1)
    tail_rows = bond // GROUP * HALF_TILE
    frame_rows = shape_of((body_rows + tail_rows, LANES))
    packed = shape_of((bond, site // (QUARTERS + 1) * QUARTERS * LANES))
    dense = shape_of((bond, site * bond))
    wide = shape_of((LANES, tall))
    stack = shape_of((tall, LANES))
    stack_f32 = shape_of((tall, LANES), F32)
    corner = shape_of((bond, bond))
    payload = shape_of((bond, -(-site * bond // LANES) * LANES + 2 * LANES))
    half_bf16 = pltpu.VMEM((tall, LANES), BF16)
    frame_scratch = [pltpu.VMEM((body_rows, LANES), F32), pltpu.VMEM((tail_rows, LANES), F32)]
    rows, columns = places(site)

    def pick(index, after):
        count = tensors.shape[0]
        return pl.pallas_call(
            pick_kernel,
            grid=(-(-square // LANES),),
            in_specs=[
                pl.BlockSpec(memory_space=pltpu.SMEM),
                pl.BlockSpec((LANES, count, square), lambda i: (i, 0, 0)),
                pl.BlockSpec(memory_space=pl.ANY),
            ],
            out_specs=pl.BlockSpec((LANES, square), lambda i: (i, 0)),
            out_shape=shape_of((square, square)),
            scratch_shapes=[pltpu.VMEM((LANES * count, LANES), F32)] * -(-square // LANES),
            compiler_params=pltpu.CompilerParams(vmem_limit_bytes=16 * MIB),
            cost_estimate=cost(2),
        )(index, tensors.transpose(1, 0, 2), after)

    def arrange(which, tensor, held, after):
        height, depth = rows.shape[1], columns.shape[1]
        vmem = pl.BlockSpec(memory_space=pltpu.VMEM)
        return pl.pallas_call(
            functools.partial(arrange_kernel, len(held)),
            grid=(1,),
            in_specs=[vmem, vmem, vmem]
            + [block_of(array) for array in held]
            + [pl.BlockSpec(memory_space=pl.ANY)],
            out_specs=[vmem] + [block_of(array) for array in held],
            out_shape=[shape_of((height, depth))] + [shape_of(array.shape) for array in held],
            compiler_params=pltpu.CompilerParams(vmem_limit_bytes=16 * MIB),
            cost_estimate=cost(2),
        )(
            tensor,
            rows[which].reshape(height, 1),
            columns[which].reshape(1, depth),
            *held,
            after,
        )

    def absorb(first, rows_in, edge, tensor, frame, *more):
        main = site - 1
        mixed = pltpu.VMEM((tensor.shape[1], GROUP * LANES), BF16)
        spare = pltpu.VMEM((HALF_TILE * (-(-site // ROWS) * ROWS), LANES), F32)
        pushed = pltpu.VMEM((GROUP * main, tall), BF16)
        return call(
            functools.partial(absorb_kernel, bond, site, first),
            (rows_in, edge, tensor, frame) + more,
            [payload, wide] if first else [dense],
            ([] if first else [half_bf16])
            + [mixed, mixed, spare, spare, pushed, pushed]
            + [pltpu.VMEM((tall, LANES), F32), pltpu.VMEM(((LANES + GROUP) * main, LANES), F32)],
            28,
            25,
        )

    upper_packed, lower_packed = call(
        functools.partial(halves_kernel, bond, site),
        (c1, t1, c4, t3),
        [packed, packed],
        [],
        60,
        2,
    )
    upper_next = shift(upper_packed, "row", -1)
    lower_back = shift(lower_packed, "row", 1)
    prepared = call(
        functools.partial(prepare_kernel, bond, site),
        (c2, t2, t4, above, below, right, upper_packed, lower_packed),
        [wide, stack, stack_f32, stack, stack_f32, packed, stack, stack_f32],
        [],
        16,
        2,
    )
    t4_wide, upper, upper_sketch, lower, lower_sketch, side_packed, side, side_sketch = prepared
    tensor = pick(pattern.reshape(1), side)
    tensor_left, t1_held, side_held, tensor_held = arrange(0, tensor, [t1, side_packed, tensor], side)
    t1_back = shift(t1_held, "row", 1)
    side_back = shift_both(side_held, 1, 1)
    tensor_back = shift(tensor_held, "row", 1)
    rows_left, frame_below, corner_top, corner_bottom = call(
        functools.partial(vertical_kernel, bond, site),
        (upper_next, lower_back, above, below, upper, upper_sketch, lower, lower_sketch),
        [frame_rows, stack, corner, corner],
        [half_bf16] * 5 + frame_scratch,
        20,
        8,
    )
    left_new, edge_wide = absorb(True, rows_left, t4_wide, tensor_left, frame_below, corner_top, corner_bottom)
    left_back = shift_both(left_new, 1, 1)
    inverse, frame_right = call(
        functools.partial(horizontal_kernel, bond, site),
        (corner_top, edge_wide, left, side, side_sketch),
        [shape_of((-(-bond // HALF_TILE) * HALF_TILE, LANES), F32), shape_of((bond, packed.shape[1] + LANES))],
        [half_bf16] * 3,
        16,
        5,
    )
    inverse_back = shift_both(inverse, 1, 1)
    frame_back = shift(frame_right, "row", 1)
    (tensor_top,) = arrange(1, tensor_back, [], inverse)
    early_sketch, t1_wide = call(
        functools.partial(early_kernel, bond, site),
        (side_back, right, t1_back, inverse),
        [stack_f32, wide],
        [half_bf16],
        16,
        2,
        1,
    )
    rows_top, top_left, forward = call(
        functools.partial(arrive_kernel, bond, site),
        (left_back, early_sketch, left, inverse_back),
        [frame_rows, corner, payload],
        [half_bf16] * 3 + frame_scratch,
        16,
        4,
    )
    left_here = shift(forward, "row", -1)
    (top_edge,) = absorb(False, rows_top, t1_wide, tensor_top, frame_back)
    left_corner, left_edge, left_bottom, top_right = call(
        functools.partial(finish_kernel, bond),
        (left_here, frame_back),
        [corner, dense, corner, corner],
        [],
        8,
        1,
    )
    return (left_corner, left_edge, left_bottom, top_left, top_edge, top_right)


def solution(mesh):
    block, whole = P("col", "row"), P()
    in_specs = (block,) * 7 + (whole, block) + (whole,) * 4
    return jax.shard_map(
        body, mesh=mesh, in_specs=in_specs, out_specs=(block,) * 6, check_vma=False
    )
```

```python
import functools

import jax
import jax.numpy as jnp
import numpy as np
from jax import lax
from jax.experimental import pallas as pl
from jax.experimental.pallas import tpu as pltpu
from jax.sharding import PartitionSpec as P

LANES = 128
ROWS = 8
HALF_TILE = 16
GROUP = 10
CUTS = 4
QUARTERS = 4
MIB = 1 << 20
F32 = jnp.float32
BF16 = jnp.bfloat16

NN = (((1,), (0,)), ((), ()))
NT = (((1,), (1,)), ((), ()))
TN = (((0,), (0,)), ((), ()))


def product(left, right, dims=NN):
    return lax.dot_general(left, right, dims, preferred_element_type=F32)


def halves(values):
    high = values.astype(BF16)
    return high, (values - high.astype(F32)).astype(BF16)


def product_split(left, right, dims=NN):
    left_high, left_low = halves(left)
    right_high, right_low = halves(right)
    axis_left, axis_right = dims[0][0][0], dims[0][1][0]
    both = jnp.concatenate([left_high, left_low], axis_left)
    twice = jnp.concatenate([right_high, right_high], axis_right)
    return product(both, twice, dims) + product(left_high, right_low, dims)


def index_of(shape, axis):
    return lax.broadcasted_iota(jnp.int32, shape, axis)


def square_of(ref, bond):
    shape = (LANES, LANES)
    keep = (index_of(shape, 0) < bond) & (index_of(shape, 1) < bond)
    return jnp.where(keep, ref[...].astype(F32), 0.0)


def spread(ref, bond, site):
    shape = (LANES, LANES)
    row, lane = index_of(shape, 0), index_of(shape, 1)
    keep = (row < bond) & (lane < bond)
    zero = jnp.zeros(shape, BF16)
    pieces = []
    for k in range(site):
        tile, offset = divmod(k * bond, LANES)
        piece = ref[:, tile * LANES : (tile + 1) * LANES]
        if offset:
            piece = pltpu.roll(piece, LANES - offset, 1)
        if offset + bond > LANES:
            more = ref[:, (tile + 1) * LANES : (tile + 2) * LANES]
            piece = jnp.where(lane < LANES - offset, piece, pltpu.roll(more, LANES - offset, 1))
        pieces.append(jnp.where(keep, piece, zero))
    return pieces


def gather_dense(tiles, ref, bond):
    lane = index_of((LANES, LANES), 1)
    total = len(tiles) * bond
    for tile in range(-(-total // LANES)):
        begin = tile * LANES
        value = None
        for k in range(begin // bond, min(len(tiles) - 1, (begin + LANES - 1) // bond) + 1):
            shift = k * bond - begin
            piece = pltpu.roll(tiles[k], shift % LANES, 1) if shift % LANES else tiles[k]
            value = piece if value is None else jnp.where(lane >= shift, piece, value)
        ref[:, begin : begin + LANES] = value


def pack(tiles, ref, bond):
    quarter = bond // QUARTERS
    lane = index_of((LANES, LANES), 1)
    tiles = [tile.astype(BF16) for tile in tiles]
    for group in range(len(tiles) // (QUARTERS + 1)):
        first = group * (QUARTERS + 1)
        for m in range(QUARTERS):
            piece = pltpu.roll(tiles[first + QUARTERS], bond - m * quarter, 1)
            slot = group * QUARTERS + m
            value = jnp.where(lane < bond, tiles[first + m], piece)
            ref[:, slot * LANES : (slot + 1) * LANES] = value


def unpack(ref, bond, site):
    quarter = bond // QUARTERS
    shape = (LANES, LANES)
    row, lane = index_of(shape, 0), index_of(shape, 1)
    keep = (row < bond) & (lane < bond)
    zero = jnp.zeros(shape, BF16)
    tiles = []
    for group in range(site // (QUARTERS + 1)):
        last = None
        for m in range(QUARTERS):
            slot = group * QUARTERS + m
            value = ref[:, slot * LANES : (slot + 1) * LANES]
            tiles.append(jnp.where(keep, value, zero))
            piece = pltpu.roll(value, LANES - bond + m * quarter, 1)
            last = piece if last is None else jnp.where(lane >= m * quarter, piece, last)
        tiles.append(jnp.where(keep, last, zero))
    return tiles


def sketched(stack, sketch):
    return product(jnp.concatenate([stack, stack], 1), jnp.concatenate(halves(sketch), 0))


def inverse_factors(grams, bond):
    count = -(-bond // ROWS)
    tile = (ROWS, LANES)
    small_row, small_lane = index_of(tile, 0), index_of(tile, 1)

    def splat(blocks, row):
        return jnp.broadcast_to(blocks[0, row : row + 1, :], tile)

    shape = (count * ROWS, LANES)
    row, lane = index_of(shape, 0), index_of(shape, 1)
    eye = jnp.where(row == lane, 1.0, 0.0)
    inside = (row < bond) & (lane < bond)
    work = [
        jnp.where(inside, gram[: count * ROWS], eye).reshape(count, ROWS, LANES) for gram in grams
    ]
    done = [[] for _ in grams]
    for block in range(count):
        first = block * ROWS
        height = count - block
        lane = index_of((height, ROWS, LANES), 2)
        fresh = (lane >= first) & (lane < first + ROWS)
        start = jnp.where(small_row == small_lane - first, 1.0, 0.0)
        start = jnp.concatenate(
            [start[None], jnp.zeros((height - 1, ROWS, LANES), F32)], 0
        ) if height > 1 else start[None]
        columns = []
        for n, matrix in enumerate(work):
            columns.append(
                [
                    jnp.broadcast_to(matrix[:, :, first + j : first + j + 1], matrix.shape)
                    for j in range(ROWS)
                ]
            )
            work[n] = jnp.where(fresh, start, matrix)
        pivots = [jnp.ones(tile, F32) for _ in work]
        pivot = [splat(column[0], 0) for column in columns]
        for j in range(ROWS):
            for n in range(len(work)):
                column = columns[n]
                inverse = 1.0 / pivot[n]
                pivots[n] = jnp.where(small_row == j, pivot[n], pivots[n])
                below = jnp.where(small_row > j, column[j][0], 0.0)[None]
                if height > 1:
                    below = jnp.concatenate([below, column[j][1:]], 0)
                if j + 1 < ROWS:
                    cross = splat(column[j], j + 1) * splat(column[j + 1], j)
                    pivot[n] = splat(column[j + 1], j + 1) - cross * inverse
                factor = below * inverse[None]
                for later in range(j + 1, ROWS):
                    column[later] = column[later] - factor * splat(column[later], j)[None]
                work[n] = work[n] - factor * splat(work[n], j)[None]
        for n in range(len(work)):
            scaled = work[n][0] * lax.rsqrt(pivots[n])
            done[n].append(jnp.where(small_lane <= small_row + first, scaled, 0.0))
            work[n] = work[n][1:]
    tail = jnp.zeros((LANES - count * ROWS, LANES), F32)
    keep = (index_of((LANES, LANES), 0) < bond) & (index_of((LANES, LANES), 1) < bond)
    return [jnp.where(keep, jnp.concatenate(parts + [tail], 0), 0.0) for parts in done]


def store_halves(values, high, low):
    high[...], low[...] = halves(values)


def gram_of(high, low):
    both = product(high[...], jnp.concatenate([high[...], low[...]], 1), TN)
    mixed = both[:, LANES:]
    return both[:, :LANES] + mixed + mixed.T


def overlap(other, high, low):
    both = product(other, jnp.concatenate([high[...], low[...]], 1), TN)
    return both[:, :LANES] + both[:, LANES:]


def frame_from(high, low, inverse):
    inverse_high, inverse_low = halves(inverse)
    left = jnp.concatenate([high[...], low[...], high[...]], 1)
    return product(left, jnp.concatenate([inverse_high, inverse_high, inverse_low], 1), NT)


def scaled_corner(values, bond):
    mean = jnp.sum(values * values) / (bond * bond)
    return (values / jnp.sqrt(mean + 1e-06)).astype(BF16)


def half_tiles(corner, pieces):
    return [product(corner, piece) for piece in pieces]


def fill(stack, tiles):
    for k, tile in enumerate(tiles):
        stack[k * LANES : (k + 1) * LANES, :] = tile.astype(stack.dtype)


def store_frame_rows(high, low, inverse, rows_ref, plain, tail, site):
    main = site - 1
    bond_rows = plain.shape[0] // main
    inverse_high, inverse_low = halves(inverse)
    left = jnp.concatenate([inverse_high, inverse_high, inverse_low], 1)[:bond_rows]
    for k in range(site):
        rows = slice(k * LANES, (k + 1) * LANES)
        tile = product(left, jnp.concatenate([high[rows, :], low[rows, :], high[rows, :]], 1), NT)
        if k < main:
            plain[pl.ds(k, bond_rows, stride=main), :] = tile
        else:
            for group in range(tail.shape[0] // HALF_TILE):
                begin = group * HALF_TILE
                tail[begin : begin + GROUP, :] = tile[group * GROUP : (group + 1) * GROUP]
    rows_ref[: plain.shape[0], :] = plain[...].astype(BF16)
    rows_ref[plain.shape[0] :, :] = tail[...].astype(BF16)


def halves_kernel(bond, site, c1, t1, c4, t3, upper_packed, lower_packed):
    for corner, edge, packed in ((c1, t1, upper_packed), (c4, t3, lower_packed)):
        pack(half_tiles(square_of(corner, bond).astype(BF16), spread(edge, bond, site)), packed, bond)


def prepare_kernel(
    bond, site, c2, t2, t4, above, below, right, upper_packed, lower_packed,
    t4_wide, upper, upper_sketch, lower, lower_sketch, side_packed, side, side_sketch,
):
    tiles = half_tiles(square_of(c2, bond).astype(BF16), spread(t2, bond, site))
    fill(side, tiles)
    pack(tiles, side_packed, bond)
    fill(upper, unpack(upper_packed, bond, site))
    fill(lower, unpack(lower_packed, bond, site))
    upper_sketch[...] = sketched(upper[...], square_of(above, bond))
    lower_sketch[...] = sketched(lower[...], square_of(below, bond))
    side_sketch[...] = sketched(side[...], square_of(right, bond))
    for k, piece in enumerate(spread(t4, bond, site)):
        t4_wide[:, k * LANES : (k + 1) * LANES] = piece


def vertical_kernel(
    bond, site, upper_packed, lower_packed, above, below, upper, upper_sketch, lower, lower_sketch,
    rows_ref, frame_out, corner_top, corner_bottom, stack, over, over_low, under, under_low, plain, tail,
):
    fill(stack, unpack(upper_packed, bond, site))
    store_halves(lower_sketch[...] + sketched(stack[...], square_of(above, bond)), under, under_low)
    fill(stack, unpack(lower_packed, bond, site))
    store_halves(upper_sketch[...] + sketched(stack[...], square_of(below, bond)), over, over_low)
    grams = [gram_of(over, over_low), gram_of(under, under_low)]
    mixed_over = overlap(upper[...], over, over_low)
    mixed_under = overlap(lower[...], under, under_low)
    inverse_over, inverse_under = inverse_factors(grams, bond)
    store_frame_rows(over, over_low, inverse_over, rows_ref, plain, tail, site)
    frame_out[...] = frame_from(under, under_low, inverse_under).astype(BF16)
    corner_top[...] = scaled_corner(product_split(inverse_over, mixed_over, NT), bond)
    corner_bottom[...] = scaled_corner(product_split(inverse_under, mixed_under, NT), bond)


def horizontal_kernel(
    bond, site, c1, edge, left, side, side_sketch, inverse_ref, frame_out, half, total, total_low
):
    corner = square_of(c1, bond).T.astype(BF16)
    fill(half, half_tiles(corner, [edge[:, k * LANES : (k + 1) * LANES] for k in range(site)]))
    store_halves(side_sketch[...] + sketched(half[...], square_of(left, bond)), total, total_low)
    mixed = overlap(side[...], total, total_low)
    (inverse,) = inverse_factors([gram_of(total, total_low)], bond)
    inverse_ref[...] = inverse[: inverse_ref.shape[0]]
    frame = frame_from(total, total_low, inverse)
    pack([frame[k * LANES : (k + 1) * LANES, :] for k in range(site)], frame_out, bond)
    corner_right = scaled_corner(product_split(inverse, mixed, NT), bond)
    frame_out[:, frame_out.shape[1] - LANES :] = corner_right


def early_kernel(bond, site, side_packed, right, t1, after, side_sketch, t1_wide, stack):
    for k, piece in enumerate(spread(t1, bond, site)):
        t1_wide[:, k * LANES : (k + 1) * LANES] = piece
    fill(stack, unpack(side_packed, bond, site))
    side_sketch[...] = sketched(stack[...], square_of(right, bond))


def arrive_kernel(
    bond, site, payload, side_sketch, left, inverse_ref,
    rows_ref, corner_left, forward, half, total, total_low, plain, tail,
):
    start = payload.shape[1] - 2 * LANES
    corner = square_of(payload.at[:, start : start + LANES], bond).T.astype(BF16)
    fill(half, half_tiles(corner, spread(payload, bond, site)))
    store_halves(side_sketch[...] + sketched(half[...], square_of(left, bond)), total, total_low)
    rest = jnp.zeros((LANES - inverse_ref.shape[0], LANES), F32)
    inverse = jnp.concatenate([inverse_ref[...], rest], 0)
    store_frame_rows(total, total_low, inverse, rows_ref, plain, tail, site)
    mixed = overlap(half[...], total, total_low)
    corner_left[...] = scaled_corner(product_split(mixed, inverse, NT), bond)
    forward[...] = payload[...]


def finish_kernel(bond, payload, frame, left_corner, left_edge, left_bottom, top_right):
    start = payload.shape[1] - 2 * LANES
    left_edge[...] = payload[:, :start]
    left_corner[...] = payload[:, start : start + LANES]
    left_bottom[...] = payload[:, start + LANES :]
    top_right[...] = frame[:, frame.shape[1] - LANES :]


def absorb_kernel(bond, site, first, counts, rows_ref, edge, tensor, frame, *refs):
    mixed_even, mixed_odd, spare_even, spare_odd, pushed_even, pushed_odd, last, result = refs[-8:]
    if first:
        corner, bottom, dense, wide = refs[:4]
        frame_out = frame
    else:
        dense, frame_out = refs[0], refs[1]
        fill(frame_out, unpack(frame, bond, site))
    main = site - 1
    groups = bond // GROUP
    tall = GROUP * main
    slot = spare_even.shape[0] // HALF_TILE
    spare_even[...] = jnp.zeros_like(spare_even)
    spare_odd[...] = jnp.zeros_like(spare_odd)
    ahead = tall + bond * main
    result[ahead:, :] = jnp.zeros((result.shape[0] - ahead, LANES), F32)

    def frames_of(group):
        body = rows_ref[pl.ds(pl.multiple_of(group * tall, tall), tall), :]
        begin = rows_ref.shape[0] - groups * HALF_TILE + group * HALF_TILE
        tail = rows_ref[pl.ds(pl.multiple_of(begin, HALF_TILE), HALF_TILE), :]
        return jnp.concatenate([body, tail], 0)

    def mix(frames, mixed, spare, unit):
        j = 2 * unit
        sides = min(2, site - j)
        both = product(frames, edge[:, j * LANES : (j + sides) * LANES])
        for side in range(sides):
            lanes = slice(side * LANES, (side + 1) * LANES)
            spare[pl.ds(j + side, HALF_TILE, stride=slot), :] = both[tall:, lanes]
        for p in range(GROUP):
            parts = [
                both[p * main : (p + 1) * main, side * LANES : (side + 1) * LANES]
                for side in range(sides)
            ]
            end = (j + sides) * main
            if sides == 1:
                end = mixed.shape[0]
                parts.append(spare[p * slot : (p + 1) * slot, :])
                parts.append(jnp.zeros((end - j * main - main - slot, LANES), F32))
            mixed[j * main : end, p * LANES : (p + 1) * LANES] = (
                jnp.concatenate(parts, 0).astype(BF16)
            )

    def push(group, mixed, pushed, begin, count):
        out = product(tensor[...], mixed[:, begin * LANES : (begin + count) * LANES])
        for pair in range(count // 2):
            sides = (2 * pair, 2 * pair + 1)
            rows = slice((begin + 2 * pair) * main, (begin + 2 * pair + 2) * main)
            for k in range(site):
                parts = [
                    out[k * main : (k + 1) * main, side * LANES : (side + 1) * LANES]
                    for side in sides
                ]
                pushed[rows, k * LANES : (k + 1) * LANES] = jnp.concatenate(parts, 0).astype(BF16)
            for side in sides:
                place = group * GROUP + begin + side
                last[pl.ds(place, site, stride=LANES), :] = out[
                    site * main : site * main + site, side * LANES : (side + 1) * LANES
                ]

    def cuts():
        step = -(-site // CUTS) // 2 * 2
        starts = [n * step for n in range(CUTS)] + [site]
        return [slice(low * LANES, high * LANES) for low, high in zip(starts, starts[1:])]

    def close(group, total):
        result[pl.ds(pl.multiple_of((group + 1) * tall, tall), tall), :] = total

    units = (site + 1) // 2

    def stage(group, mixed, pushed, mixed_next, spare_next, pushed_before):
        frames = frames_of(jnp.minimum(group + 1, groups - 1))
        total = jnp.zeros((tall, LANES), F32)
        parts = cuts()
        begin = 0
        for n, count in enumerate(counts):
            push(group, mixed, pushed, begin, count)
            begin += count
            for unit in range(n * units // len(counts), (n + 1) * units // len(counts)):
                mix(frames, mixed_next, spare_next, unit)
            for part in parts[n * CUTS // len(counts) : (n + 1) * CUTS // len(counts)]:
                total = total + product(pushed_before[:, part], frame_out[part, :])
        close(group - 1, total)

    frames = frames_of(0)
    for unit in range(units):
        mix(frames, mixed_even, spare_even, unit)

    def step(index, carry):
        stage(2 * index, mixed_even, pushed_even, mixed_odd, spare_odd, pushed_odd)
        stage(2 * index + 1, mixed_odd, pushed_odd, mixed_even, spare_even, pushed_even)
        return carry

    lax.fori_loop(0, groups // 2, step, 0)
    close(groups - 1, product(pushed_odd[...], frame_out[...]))
    tiles = [result[pl.ds(tall + k, LANES, stride=main), :] for k in range(main)]
    total = jnp.zeros((LANES, LANES), F32)
    for k in range(site):
        rows = pl.ds(k * LANES, LANES)
        total = total + product(last[rows, :].astype(BF16), frame_out[rows, :])
    tiles.append(jnp.where(index_of(total.shape, 0) < bond, total, 0.0))
    squares = tiles[0] * tiles[0]
    for tile in tiles[1:]:
        squares = squares + tile * tile
    scale = 1.0 / jnp.sqrt(jnp.sum(squares) / (bond * bond * site) + 1e-06)
    tiles = [(tile * scale).astype(BF16) for tile in tiles]
    gather_dense(tiles, dense, bond)
    if first:
        for k, tile in enumerate(tiles):
            wide[:, k * LANES : (k + 1) * LANES] = tile
        start = dense.shape[1] - 2 * LANES
        dense[:, start : start + LANES] = square_of(corner, bond).astype(BF16)
        dense[:, start + LANES :] = square_of(bottom, bond).astype(BF16)


def pick_kernel(pattern, tensors, after, out, *tiles):
    height, count, width = tensors.shape
    values = tensors[...].astype(F32).reshape(height * count, width)
    for n, tile in enumerate(tiles):
        end = min(width, (n + 1) * LANES)
        tile[:, : end - n * LANES] = values[:, n * LANES : end]
        rows = tile[pl.ds(pattern[0], height, stride=count), :]
        out[:, n * LANES : end] = rows[:, : end - n * LANES].astype(BF16)


def arrange_kernel(count, tensor, rows, columns, *refs):
    held, out, copies = refs[:count], refs[-count - 1], refs[len(refs) - count :]
    for source, target in zip(held, copies):
        target[...] = source[...]
    square = tensor.shape[0]
    pick_rows = jnp.where(index_of((rows.shape[0], square), 1) == rows[...], 1.0, 0.0).astype(BF16)
    pick_columns = jnp.where(index_of((square, columns.shape[1]), 0) == columns[...], 1.0, 0.0)
    turned = product(pick_rows, tensor[...], NT).astype(BF16)
    out[...] = product(turned, pick_columns.astype(BF16)).astype(BF16)


def places(site):
    main = site - 1
    size = -(-site * site // LANES) * LANES
    rows = np.full((2, size), -1, np.int32)
    columns = np.full((2, size), -1, np.int32)
    for other in range(site):
        for inner in range(site):
            at = other * main + inner if inner < main else site * main + other
            rows[0, at] = other * site + inner
            rows[1, at] = inner * site + other
            columns[0, at] = inner * site + other
            columns[1, at] = other * site + inner
    return rows, columns


def block_of(arg):
    shape = arg.shape
    if len(shape) == 1:
        return pl.BlockSpec(memory_space=pltpu.SMEM)
    if shape[0] % 16 == 0 and shape[1] % LANES == 0:
        return pl.BlockSpec(memory_space=pltpu.VMEM)
    return pl.BlockSpec(tuple(-(-size // LANES) * LANES for size in shape), lambda i: (0, 0))


def cost(microseconds):
    return pl.CostEstimate(
        flops=microseconds * 1_000_000_000, bytes_accessed=microseconds * 1_000_000, transcendentals=0
    )


def call(kernel, args, outs, scratch, limit, microseconds, unread=0):
    specs = [block_of(arg) for arg in args]
    if unread:
        specs[-unread:] = [pl.BlockSpec(memory_space=pl.ANY)] * unread
    return pl.pallas_call(
        kernel,
        grid=(1,),
        in_specs=specs,
        out_specs=[block_of(out) for out in outs],
        out_shape=outs,
        scratch_shapes=scratch,
        compiler_params=pltpu.CompilerParams(vmem_limit_bytes=limit * MIB),
        cost_estimate=cost(microseconds),
    )(*args)


def shape_of(shape, dtype=BF16):
    return jax.ShapeDtypeStruct(shape, dtype)


def shift(value, axis, steps):
    count = lax.axis_size(axis)
    pairs = [(source, (source + steps) % count) for source in range(count)]
    return lax.ppermute(value, axis, pairs)


def shift_both(value, steps_col, steps_row):
    columns, rows = lax.axis_size("col"), lax.axis_size("row")
    pairs = []
    for x in range(columns):
        for y in range(rows):
            target = (x + steps_col) % columns * rows + (y + steps_row) % rows
            pairs.append((x * rows + y, target))
    return lax.ppermute(value, ("col", "row"), pairs)


def body(c1, c2, c4, t1, t2, t3, t4, tensors, pattern, below, above, right, left):
    bond = c1.shape[0]
    site = t1.shape[1] // bond
    square = site * site
    tall = site * LANES
    bond_rows = -(-bond // ROWS) * ROWS
    body_rows = bond_rows * (site - 1)
    tail_rows = bond // GROUP * HALF_TILE
    frame_rows = shape_of((body_rows + tail_rows, LANES))
    packed = shape_of((bond, site // (QUARTERS + 1) * QUARTERS * LANES))
    dense = shape_of((bond, site * bond))
    wide = shape_of((LANES, tall))
    stack = shape_of((tall, LANES))
    stack_f32 = shape_of((tall, LANES), F32)
    corner = shape_of((bond, bond))
    payload = shape_of((bond, -(-site * bond // LANES) * LANES + 2 * LANES))
    half_bf16 = pltpu.VMEM((tall, LANES), BF16)
    frame_scratch = [pltpu.VMEM((body_rows, LANES), F32), pltpu.VMEM((tail_rows, LANES), F32)]
    rows, columns = places(site)

    def pick(index, after):
        count = tensors.shape[0]
        return pl.pallas_call(
            pick_kernel,
            grid=(-(-square // LANES),),
            in_specs=[
                pl.BlockSpec(memory_space=pltpu.SMEM),
                pl.BlockSpec((LANES, count, square), lambda i: (i, 0, 0)),
                pl.BlockSpec(memory_space=pl.ANY),
            ],
            out_specs=pl.BlockSpec((LANES, square), lambda i: (i, 0)),
            out_shape=shape_of((square, square)),
            scratch_shapes=[pltpu.VMEM((LANES * count, LANES), F32)] * -(-square // LANES),
            compiler_params=pltpu.CompilerParams(vmem_limit_bytes=16 * MIB),
            cost_estimate=cost(2),
        )(index, tensors.transpose(1, 0, 2), after)

    def arrange(which, tensor, held, after):
        height, depth = rows.shape[1], columns.shape[1]
        vmem = pl.BlockSpec(memory_space=pltpu.VMEM)
        return pl.pallas_call(
            functools.partial(arrange_kernel, len(held)),
            grid=(1,),
            in_specs=[vmem, vmem, vmem]
            + [block_of(array) for array in held]
            + [pl.BlockSpec(memory_space=pl.ANY)],
            out_specs=[vmem] + [block_of(array) for array in held],
            out_shape=[shape_of((height, depth))] + [shape_of(array.shape) for array in held],
            compiler_params=pltpu.CompilerParams(vmem_limit_bytes=16 * MIB),
            cost_estimate=cost(2),
        )(
            tensor,
            rows[which].reshape(height, 1),
            columns[which].reshape(1, depth),
            *held,
            after,
        )

    def absorb(first, rows_in, edge, tensor, frame, *more):
        main = site - 1
        mixed = pltpu.VMEM((tensor.shape[1], GROUP * LANES), BF16)
        spare = pltpu.VMEM((HALF_TILE * (-(-site // ROWS) * ROWS), LANES), F32)
        pushed = pltpu.VMEM((GROUP * main, tall), BF16)
        return call(
            functools.partial(absorb_kernel, bond, site, first, (4, 4, 2) if first else (6, 4)),
            (rows_in, edge, tensor, frame) + more,
            [payload, wide] if first else [dense],
            ([] if first else [half_bf16])
            + [mixed, mixed, spare, spare, pushed, pushed]
            + [pltpu.VMEM((tall, LANES), F32), pltpu.VMEM(((LANES + GROUP) * main, LANES), F32)],
            28,
            25,
        )

    upper_packed, lower_packed = call(
        functools.partial(halves_kernel, bond, site),
        (c1, t1, c4, t3),
        [packed, packed],
        [],
        60,
        2,
    )
    upper_next = shift(upper_packed, "row", -1)
    lower_back = shift(lower_packed, "row", 1)
    prepared = call(
        functools.partial(prepare_kernel, bond, site),
        (c2, t2, t4, above, below, right, upper_packed, lower_packed),
        [wide, stack, stack_f32, stack, stack_f32, packed, stack, stack_f32],
        [],
        16,
        2,
    )
    t4_wide, upper, upper_sketch, lower, lower_sketch, side_packed, side, side_sketch = prepared
    tensor = pick(pattern.reshape(1), side)
    tensor_left, t1_held, side_held, tensor_held = arrange(0, tensor, [t1, side_packed, tensor], side)
    t1_back = shift(t1_held, "row", 1)
    side_back = shift_both(side_held, 1, 1)
    tensor_back = shift(tensor_held, "row", 1)
    rows_left, frame_below, corner_top, corner_bottom = call(
        functools.partial(vertical_kernel, bond, site),
        (upper_next, lower_back, above, below, upper, upper_sketch, lower, lower_sketch),
        [frame_rows, stack, corner, corner],
        [half_bf16] * 5 + frame_scratch,
        20,
        8,
    )
    left_new, edge_wide = absorb(True, rows_left, t4_wide, tensor_left, frame_below, corner_top, corner_bottom)
    left_back = shift_both(left_new, 1, 1)
    inverse, frame_right = call(
        functools.partial(horizontal_kernel, bond, site),
        (corner_top, edge_wide, left, side, side_sketch),
        [shape_of((-(-bond // HALF_TILE) * HALF_TILE, LANES), F32), shape_of((bond, packed.shape[1] + LANES))],
        [half_bf16] * 3,
        16,
        5,
    )
    inverse_back = shift_both(inverse, 1, 1)
    frame_back = shift(frame_right, "row", 1)
    (tensor_top,) = arrange(1, tensor_back, [], inverse)
    early_sketch, t1_wide = call(
        functools.partial(early_kernel, bond, site),
        (side_back, right, t1_back, inverse),
        [stack_f32, wide],
        [half_bf16],
        16,
        2,
        1,
    )
    rows_top, top_left, forward = call(
        functools.partial(arrive_kernel, bond, site),
        (left_back, early_sketch, left, inverse_back),
        [frame_rows, corner, payload],
        [half_bf16] * 3 + frame_scratch,
        16,
        4,
    )
    left_here = shift(forward, "row", -1)
    (top_edge,) = absorb(False, rows_top, t1_wide, tensor_top, frame_back)
    left_corner, left_edge, left_bottom, top_right = call(
        functools.partial(finish_kernel, bond),
        (left_here, frame_back),
        [corner, dense, corner, corner],
        [],
        8,
        1,
    )
    return (left_corner, left_edge, left_bottom, top_left, top_edge, top_right)


def solution(mesh):
    block, whole = P("col", "row"), P()
    in_specs = (block,) * 7 + (whole, block) + (whole,) * 4
    return jax.shard_map(
        body, mesh=mesh, in_specs=in_specs, out_specs=(block,) * 6, check_vma=False
    )
```

```python
import functools

import jax
import jax.numpy as jnp
import numpy as np
from jax import lax
from jax.experimental import pallas as pl
from jax.experimental.pallas import tpu as pltpu
from jax.sharding import PartitionSpec as P

LANES = 128
ROWS = 8
HALF_TILE = 16
TAIL = 16
GROUP = 10
CUTS = 4
QUARTERS = 4
MIB = 1 << 20
F32 = jnp.float32
BF16 = jnp.bfloat16

NN = (((1,), (0,)), ((), ()))
NT = (((1,), (1,)), ((), ()))
TN = (((0,), (0,)), ((), ()))


def product(left, right, dims=NN):
    return lax.dot_general(left, right, dims, preferred_element_type=F32)


def halves(values):
    high = values.astype(BF16)
    return high, (values - high.astype(F32)).astype(BF16)


def product_split(left, right, dims=NN):
    left_high, left_low = halves(left)
    right_high, right_low = halves(right)
    axis_left, axis_right = dims[0][0][0], dims[0][1][0]
    both = jnp.concatenate([left_high, left_low], axis_left)
    twice = jnp.concatenate([right_high, right_high], axis_right)
    return product(both, twice, dims) + product(left_high, right_low, dims)


def index_of(shape, axis):
    return lax.broadcasted_iota(jnp.int32, shape, axis)


def square_of(ref, bond):
    shape = (LANES, LANES)
    keep = (index_of(shape, 0) < bond) & (index_of(shape, 1) < bond)
    return jnp.where(keep, ref[...].astype(F32), 0.0)


def spread(ref, bond, site):
    shape = (LANES, LANES)
    row, lane = index_of(shape, 0), index_of(shape, 1)
    keep = (row < bond) & (lane < bond)
    zero = jnp.zeros(shape, BF16)
    pieces = []
    for k in range(site):
        tile, offset = divmod(k * bond, LANES)
        piece = ref[:, tile * LANES : (tile + 1) * LANES]
        if offset:
            piece = pltpu.roll(piece, LANES - offset, 1)
        if offset + bond > LANES:
            more = ref[:, (tile + 1) * LANES : (tile + 2) * LANES]
            piece = jnp.where(lane < LANES - offset, piece, pltpu.roll(more, LANES - offset, 1))
        pieces.append(jnp.where(keep, piece, zero))
    return pieces


def gather_dense(tiles, ref, bond):
    lane = index_of((LANES, LANES), 1)
    total = len(tiles) * bond
    for tile in range(-(-total // LANES)):
        begin = tile * LANES
        value = None
        for k in range(begin // bond, min(len(tiles) - 1, (begin + LANES - 1) // bond) + 1):
            shift = k * bond - begin
            piece = pltpu.roll(tiles[k], shift % LANES, 1) if shift % LANES else tiles[k]
            value = piece if value is None else jnp.where(lane >= shift, piece, value)
        ref[:, begin : begin + LANES] = value


def pack(tiles, ref, bond):
    quarter = bond // QUARTERS
    lane = index_of((LANES, LANES), 1)
    tiles = [tile.astype(BF16) for tile in tiles]
    for group in range(len(tiles) // (QUARTERS + 1)):
        first = group * (QUARTERS + 1)
        for m in range(QUARTERS):
            piece = pltpu.roll(tiles[first + QUARTERS], bond - m * quarter, 1)
            slot = group * QUARTERS + m
            value = jnp.where(lane < bond, tiles[first + m], piece)
            ref[:, slot * LANES : (slot + 1) * LANES] = value


def unpack(ref, bond, site):
    quarter = bond // QUARTERS
    shape = (LANES, LANES)
    row, lane = index_of(shape, 0), index_of(shape, 1)
    keep = (row < bond) & (lane < bond)
    zero = jnp.zeros(shape, BF16)
    tiles = []
    for group in range(site // (QUARTERS + 1)):
        last = None
        for m in range(QUARTERS):
            slot = group * QUARTERS + m
            value = ref[:, slot * LANES : (slot + 1) * LANES]
            tiles.append(jnp.where(keep, value, zero))
            piece = pltpu.roll(value, LANES - bond + m * quarter, 1)
            last = piece if last is None else jnp.where(lane >= m * quarter, piece, last)
        tiles.append(jnp.where(keep, last, zero))
    return tiles


def sketched(stack, sketch):
    return product(jnp.concatenate([stack, stack], 1), jnp.concatenate(halves(sketch), 0))


def inverse_factors(grams, bond):
    count = -(-bond // ROWS) * ROWS
    shape = (count, LANES)
    row, lane = index_of(shape, 0), index_of(shape, 1)
    inside = (row < bond) & (lane < bond)
    eye = jnp.where(row == lane, 1.0, 0.0)
    work = [jnp.where(inside, gram[:count], eye) for gram in grams]
    done = [[] for _ in grams]
    for first in range(0, count, ROWS):
        height = count - first
        row, lane = index_of((height, LANES), 0), index_of((height, LANES), 1)
        block = (lane >= first) & (lane < first + ROWS)
        start = jnp.where(row == lane - first, 1.0, 0.0)
        small_row, small_lane = index_of((ROWS, LANES), 0), index_of((ROWS, LANES), 1)
        columns = []
        for n, matrix in enumerate(work):
            columns.append(
                [
                    jnp.broadcast_to(matrix[:, first + j : first + j + 1], (height, LANES))
                    for j in range(ROWS)
                ]
            )
            work[n] = jnp.where(block, start, matrix)
        pivots = [jnp.ones((ROWS, LANES), F32) for _ in work]
        for j in range(ROWS):
            for n in range(len(work)):
                column = columns[n]
                pivot = column[j][j : j + 1, :]
                factor = jnp.where(row > j, column[j] * (1.0 / pivot), 0.0)
                work[n] = work[n] - factor * work[n][j : j + 1, :]
                for later in range(j + 1, ROWS):
                    column[later] = column[later] - factor * column[later][j : j + 1, :]
                pivots[n] = jnp.where(small_row == j, pivot, pivots[n])
        for n in range(len(work)):
            scaled = work[n][:ROWS] * lax.rsqrt(pivots[n])
            done[n].append(jnp.where(small_lane <= small_row + first, scaled, 0.0))
            work[n] = work[n][ROWS:]
    tail = jnp.zeros((LANES - count, LANES), F32)
    keep = (index_of((LANES, LANES), 0) < bond) & (index_of((LANES, LANES), 1) < bond)
    return [jnp.where(keep, jnp.concatenate(parts + [tail], 0), 0.0) for parts in done]


def store_halves(values, high, low):
    high[...], low[...] = halves(values)


def gram_and_overlap(other, high, low):
    left = jnp.concatenate([high[...], other], 1)
    both = product(left, jnp.concatenate([high[...], low[...]], 1), TN)
    mixed = both[:LANES, LANES:]
    gram = both[:LANES, :LANES] + mixed + mixed.T
    return gram, both[LANES:, :LANES] + both[LANES:, LANES:]


def overlap(other, high, low):
    both = product(other, jnp.concatenate([high[...], low[...]], 1), TN)
    return both[:, :LANES] + both[:, LANES:]


def frame_from(high, low, inverse):
    inverse_high, inverse_low = halves(inverse)
    left = jnp.concatenate([high[...], low[...], high[...]], 1)
    return product(left, jnp.concatenate([inverse_high, inverse_high, inverse_low], 1), NT)


def scaled_corner(values, bond):
    mean = jnp.sum(values * values) / (bond * bond)
    return (values / jnp.sqrt(mean + 1e-06)).astype(BF16)


def half_tiles(corner, pieces):
    return [product(corner, piece) for piece in pieces]


def fill(stack, tiles):
    for k, tile in enumerate(tiles):
        stack[k * LANES : (k + 1) * LANES, :] = tile.astype(stack.dtype)


def store_frame_rows(high, low, inverse, rows_ref, plain, tail, site):
    main = site - 1
    bond_rows = plain.shape[0] // main
    inverse_high, inverse_low = halves(inverse)
    left = jnp.concatenate([inverse_high, inverse_high, inverse_low], 1)[:bond_rows]
    for k in range(site):
        rows = slice(k * LANES, (k + 1) * LANES)
        tile = product(left, jnp.concatenate([high[rows, :], low[rows, :], high[rows, :]], 1), NT)
        if k < main:
            plain[pl.ds(k, bond_rows, stride=main), :] = tile
        else:
            for group in range(tail.shape[0] // TAIL):
                begin = group * TAIL
                tail[begin : begin + GROUP, :] = tile[group * GROUP : (group + 1) * GROUP]
    rows_ref[: plain.shape[0], :] = plain[...].astype(BF16)
    rows_ref[plain.shape[0] :, :] = tail[...].astype(BF16)


def half_kernel(bond, site, corner, edge, packed):
    pack(half_tiles(square_of(corner, bond).astype(BF16), spread(edge, bond, site)), packed, bond)


def prepare_kernel(
    bond, site, c2, t2, t4, t1, above, below, upper_packed, lower_packed,
    t4_wide, t1_out, upper, upper_sketch, lower, lower_sketch, side_packed, side,
):
    t1_out[...] = t1[...]
    tiles = half_tiles(square_of(c2, bond).astype(BF16), spread(t2, bond, site))
    fill(side, tiles)
    pack(tiles, side_packed, bond)
    fill(upper, unpack(upper_packed, bond, site))
    fill(lower, unpack(lower_packed, bond, site))
    upper_sketch[...] = sketched(upper[...], square_of(above, bond))
    lower_sketch[...] = sketched(lower[...], square_of(below, bond))
    for k, piece in enumerate(spread(t4, bond, site)):
        t4_wide[:, k * LANES : (k + 1) * LANES] = piece


def vertical_kernel(
    bond, site, upper_packed, lower_packed, above, below, upper, upper_sketch, lower, lower_sketch,
    rows_ref, frame_out, corner_top, corner_bottom, stack, over, over_low, under, under_low, plain, tail,
):
    fill(stack, unpack(upper_packed, bond, site))
    store_halves(lower_sketch[...] + sketched(stack[...], square_of(above, bond)), under, under_low)
    fill(stack, unpack(lower_packed, bond, site))
    store_halves(upper_sketch[...] + sketched(stack[...], square_of(below, bond)), over, over_low)
    gram_over, mixed_over = gram_and_overlap(upper[...], over, over_low)
    gram_under, mixed_under = gram_and_overlap(lower[...], under, under_low)
    inverse_over, inverse_under = inverse_factors([gram_over, gram_under], bond)
    store_frame_rows(over, over_low, inverse_over, rows_ref, plain, tail, site)
    frame_out[...] = frame_from(under, under_low, inverse_under).astype(BF16)
    corner_top[...] = scaled_corner(product_split(inverse_over, mixed_over, NT), bond)
    corner_bottom[...] = scaled_corner(product_split(inverse_under, mixed_under, NT), bond)


def horizontal_kernel(
    bond, site, c1, edge, left, right, side, inverse_ref, frame_out, half, total, total_low
):
    corner = square_of(c1, bond).T.astype(BF16)
    fill(half, half_tiles(corner, [edge[:, k * LANES : (k + 1) * LANES] for k in range(site)]))
    stacks = jnp.concatenate([half[...], half[...], side[...], side[...]], 1)
    sketches = halves(square_of(left, bond)) + halves(square_of(right, bond))
    store_halves(product(stacks, jnp.concatenate(sketches, 0)), total, total_low)
    gram, mixed = gram_and_overlap(side[...], total, total_low)
    (inverse,) = inverse_factors([gram], bond)
    inverse_ref[...] = inverse[: inverse_ref.shape[0]]
    frame = frame_from(total, total_low, inverse)
    pack([frame[k * LANES : (k + 1) * LANES, :] for k in range(site)], frame_out, bond)
    corner_right = scaled_corner(product_split(inverse, mixed, NT), bond)
    frame_out[:, frame_out.shape[1] - LANES :] = corner_right


def early_kernel(bond, site, side_packed, right, t1, after, side_sketch, t1_wide, stack):
    for k, piece in enumerate(spread(t1, bond, site)):
        t1_wide[:, k * LANES : (k + 1) * LANES] = piece
    fill(stack, unpack(side_packed, bond, site))
    side_sketch[...] = sketched(stack[...], square_of(right, bond))


def arrive_kernel(
    bond, site, payload, side_sketch, left, inverse_ref,
    rows_ref, corner_left, forward, half, total, total_low, plain, tail,
):
    start = payload.shape[1] - 2 * LANES
    corner = square_of(payload.at[:, start : start + LANES], bond).T.astype(BF16)
    fill(half, half_tiles(corner, spread(payload, bond, site)))
    store_halves(side_sketch[...] + sketched(half[...], square_of(left, bond)), total, total_low)
    rest = jnp.zeros((LANES - inverse_ref.shape[0], LANES), F32)
    inverse = jnp.concatenate([inverse_ref[...], rest], 0)
    store_frame_rows(total, total_low, inverse, rows_ref, plain, tail, site)
    mixed = overlap(half[...], total, total_low)
    corner_left[...] = scaled_corner(product_split(mixed, inverse, NT), bond)
    forward[...] = payload[...]


def finish_kernel(bond, payload, frame, left_corner, left_edge, left_bottom, top_right):
    start = payload.shape[1] - 2 * LANES
    left_edge[...] = payload[:, :start]
    left_corner[...] = payload[:, start : start + LANES]
    left_bottom[...] = payload[:, start + LANES :]
    top_right[...] = frame[:, frame.shape[1] - LANES :]


def absorb_kernel(bond, site, first, counts, rows_ref, edge, tensor, frame, *refs):
    mixed_even, mixed_odd, spare_even, spare_odd, pushed_even, pushed_odd, last, result = refs[-8:]
    if first:
        corner, bottom, dense, wide = refs[:4]
        frame_out = frame
    else:
        dense, frame_out = refs[0], refs[1]
        fill(frame_out, unpack(frame, bond, site))
    main = site - 1
    groups = bond // GROUP
    tall = GROUP * main
    slot = spare_even.shape[0] // TAIL
    spare_even[...] = jnp.zeros_like(spare_even)
    spare_odd[...] = jnp.zeros_like(spare_odd)
    ahead = tall + bond * main
    result[ahead:, :] = jnp.zeros((result.shape[0] - ahead, LANES), F32)

    def frames_of(group):
        body = rows_ref[pl.ds(pl.multiple_of(group * tall, tall), tall), :]
        begin = rows_ref.shape[0] - groups * TAIL + group * TAIL
        tail = rows_ref[pl.ds(pl.multiple_of(begin, TAIL), TAIL), :]
        return jnp.concatenate([body, tail], 0)

    def mix(frames, mixed, spare, unit):
        j = 2 * unit
        sides = min(2, site - j)
        both = product(frames, edge[:, j * LANES : (j + sides) * LANES])
        for side in range(sides):
            lanes = slice(side * LANES, (side + 1) * LANES)
            spare[pl.ds(j + side, TAIL, stride=slot), :] = both[tall:, lanes]
        for p in range(GROUP):
            parts = [
                both[p * main : (p + 1) * main, side * LANES : (side + 1) * LANES]
                for side in range(sides)
            ]
            end = (j + sides) * main
            if sides == 1:
                end = mixed.shape[0]
                parts.append(spare[p * slot : (p + 1) * slot, :])
                parts.append(jnp.zeros((end - j * main - main - slot, LANES), F32))
            mixed[j * main : end, p * LANES : (p + 1) * LANES] = (
                jnp.concatenate(parts, 0).astype(BF16)
            )

    def push(group, mixed, pushed, begin, count):
        out = product(tensor[...], mixed[:, begin * LANES : (begin + count) * LANES])
        for pair in range(count // 2):
            sides = (2 * pair, 2 * pair + 1)
            rows = slice((begin + 2 * pair) * main, (begin + 2 * pair + 2) * main)
            for k in range(site):
                parts = [
                    out[k * main : (k + 1) * main, side * LANES : (side + 1) * LANES]
                    for side in sides
                ]
                pushed[rows, k * LANES : (k + 1) * LANES] = jnp.concatenate(parts, 0).astype(BF16)
            for side in sides:
                place = group * GROUP + begin + side
                last[pl.ds(place, site, stride=LANES), :] = out[
                    site * main : site * main + site, side * LANES : (side + 1) * LANES
                ]

    def cuts():
        step = -(-site // CUTS) // 2 * 2
        starts = [n * step for n in range(CUTS)] + [site]
        return [slice(low * LANES, high * LANES) for low, high in zip(starts, starts[1:])]

    def close(group, total):
        result[pl.ds(pl.multiple_of((group + 1) * tall, tall), tall), :] = total

    units = (site + 1) // 2

    def stage(group, mixed, pushed, mixed_next, spare_next, pushed_before):
        frames = frames_of(jnp.minimum(group + 1, groups - 1))
        total = jnp.zeros((tall, LANES), F32)
        parts = cuts()
        begin = 0
        for n, count in enumerate(counts):
            push(group, mixed, pushed, begin, count)
            begin += count
            for unit in range(n * units // len(counts), (n + 1) * units // len(counts)):
                mix(frames, mixed_next, spare_next, unit)
            for part in parts[n * CUTS // len(counts) : (n + 1) * CUTS // len(counts)]:
                total = total + product(pushed_before[:, part], frame_out[part, :])
        close(group - 1, total)

    frames = frames_of(0)
    for unit in range(units):
        mix(frames, mixed_even, spare_even, unit)

    def step(index, carry):
        stage(2 * index, mixed_even, pushed_even, mixed_odd, spare_odd, pushed_odd)
        stage(2 * index + 1, mixed_odd, pushed_odd, mixed_even, spare_even, pushed_even)
        return carry

    lax.fori_loop(0, groups // 2, step, 0)
    close(groups - 1, product(pushed_odd[...], frame_out[...]))
    tiles = [result[pl.ds(tall + k, LANES, stride=main), :] for k in range(main)]
    total = jnp.zeros((LANES, LANES), F32)
    for k in range(site):
        rows = pl.ds(k * LANES, LANES)
        total = total + product(last[rows, :].astype(BF16), frame_out[rows, :])
    tiles.append(jnp.where(index_of(total.shape, 0) < bond, total, 0.0))
    squares = tiles[0] * tiles[0]
    for tile in tiles[1:]:
        squares = squares + tile * tile
    scale = 1.0 / jnp.sqrt(jnp.sum(squares) / (bond * bond * site) + 1e-06)
    tiles = [(tile * scale).astype(BF16) for tile in tiles]
    gather_dense(tiles, dense, bond)
    if first:
        for k, tile in enumerate(tiles):
            wide[:, k * LANES : (k + 1) * LANES] = tile
        start = dense.shape[1] - 2 * LANES
        dense[:, start : start + LANES] = square_of(corner, bond).astype(BF16)
        dense[:, start + LANES :] = square_of(bottom, bond).astype(BF16)


def pick_kernel(pattern, tensors, after, out, *tiles):
    height, count, width = tensors.shape
    values = tensors[...].astype(F32).reshape(height * count, width)
    for n, tile in enumerate(tiles):
        end = min(width, (n + 1) * LANES)
        tile[:, : end - n * LANES] = values[:, n * LANES : end]
        rows = tile[pl.ds(pattern[0], height, stride=count), :]
        out[:, n * LANES : end] = rows[:, : end - n * LANES].astype(BF16)


def arrange_kernel(tensor, rows, columns, after, out):
    square = tensor.shape[0]
    pick_rows = jnp.where(index_of((rows.shape[0], square), 1) == rows[...], 1.0, 0.0).astype(BF16)
    pick_columns = jnp.where(index_of((square, columns.shape[1]), 0) == columns[...], 1.0, 0.0)
    turned = product(pick_rows, tensor[...], NT).astype(BF16)
    out[...] = product(turned, pick_columns.astype(BF16)).astype(BF16)


def places(site):
    main = site - 1
    size = -(-site * site // LANES) * LANES
    rows = np.full((2, size), -1, np.int32)
    columns = np.full((2, size), -1, np.int32)
    for other in range(site):
        for inner in range(site):
            at = other * main + inner if inner < main else site * main + other
            rows[0, at] = other * site + inner
            rows[1, at] = inner * site + other
            columns[0, at] = inner * site + other
            columns[1, at] = other * site + inner
    return rows, columns


def block_of(arg):
    shape = arg.shape
    if len(shape) == 1:
        return pl.BlockSpec(memory_space=pltpu.SMEM)
    if shape[0] % 16 == 0 and shape[1] % LANES == 0:
        return pl.BlockSpec(memory_space=pltpu.VMEM)
    return pl.BlockSpec(tuple(-(-size // LANES) * LANES for size in shape), lambda i: (0, 0))


def cost(microseconds):
    return pl.CostEstimate(
        flops=microseconds * 1_000_000_000, bytes_accessed=microseconds * 1_000_000, transcendentals=0
    )


def call(kernel, args, outs, scratch, limit, microseconds, unread=0):
    specs = [block_of(arg) for arg in args]
    if unread:
        specs[-unread:] = [pl.BlockSpec(memory_space=pl.ANY)] * unread
    return pl.pallas_call(
        kernel,
        grid=(1,),
        in_specs=specs,
        out_specs=[block_of(out) for out in outs],
        out_shape=outs,
        scratch_shapes=scratch,
        compiler_params=pltpu.CompilerParams(vmem_limit_bytes=limit * MIB),
        cost_estimate=cost(microseconds),
    )(*args)


def shape_of(shape, dtype=BF16):
    return jax.ShapeDtypeStruct(shape, dtype)


def shift(value, axis, steps):
    count = lax.axis_size(axis)
    pairs = [(source, (source + steps) % count) for source in range(count)]
    return lax.ppermute(value, axis, pairs)


def shift_both(value, steps_col, steps_row):
    columns, rows = lax.axis_size("col"), lax.axis_size("row")
    pairs = []
    for x in range(columns):
        for y in range(rows):
            target = (x + steps_col) % columns * rows + (y + steps_row) % rows
            pairs.append((x * rows + y, target))
    return lax.ppermute(value, ("col", "row"), pairs)


def body(c1, c2, c4, t1, t2, t3, t4, tensors, pattern, below, above, right, left):
    bond = c1.shape[0]
    site = t1.shape[1] // bond
    square = site * site
    tall = site * LANES
    bond_rows = -(-bond // ROWS) * ROWS
    body_rows = bond_rows * (site - 1)
    tail_rows = bond // GROUP * TAIL
    frame_rows = shape_of((body_rows + tail_rows, LANES))
    packed = shape_of((bond, site // (QUARTERS + 1) * QUARTERS * LANES))
    dense = shape_of((bond, site * bond))
    wide = shape_of((LANES, tall))
    stack = shape_of((tall, LANES))
    stack_f32 = shape_of((tall, LANES), F32)
    corner = shape_of((bond, bond))
    payload = shape_of((bond, -(-site * bond // LANES) * LANES + 2 * LANES))
    half_bf16 = pltpu.VMEM((tall, LANES), BF16)
    frame_scratch = [pltpu.VMEM((body_rows, LANES), F32), pltpu.VMEM((tail_rows, LANES), F32)]
    rows, columns = places(site)

    def pick(index, after):
        count = tensors.shape[0]
        return pl.pallas_call(
            pick_kernel,
            grid=(-(-square // LANES),),
            in_specs=[
                pl.BlockSpec(memory_space=pltpu.SMEM),
                pl.BlockSpec((LANES, count, square), lambda i: (i, 0, 0)),
                pl.BlockSpec(memory_space=pl.ANY),
            ],
            out_specs=pl.BlockSpec((LANES, square), lambda i: (i, 0)),
            out_shape=shape_of((square, square)),
            scratch_shapes=[pltpu.VMEM((LANES * count, LANES), F32)] * -(-square // LANES),
            compiler_params=pltpu.CompilerParams(vmem_limit_bytes=16 * MIB),
            cost_estimate=cost(2),
        )(index, tensors.transpose(1, 0, 2), after)

    def arrange(which, tensor, after):
        height, depth = rows.shape[1], columns.shape[1]
        vmem = pl.BlockSpec(memory_space=pltpu.VMEM)
        return pl.pallas_call(
            arrange_kernel,
            in_specs=[vmem, vmem, vmem, pl.BlockSpec(memory_space=pl.ANY)],
            out_specs=vmem,
            out_shape=shape_of((height, depth)),
            compiler_params=pltpu.CompilerParams(vmem_limit_bytes=16 * MIB),
            cost_estimate=cost(2),
        )(
            tensor,
            rows[which].reshape(height, 1),
            columns[which].reshape(1, depth),
            after,
        )

    def absorb(first, rows_in, edge, tensor, frame, *more):
        main = site - 1
        mixed = pltpu.VMEM((tensor.shape[1], GROUP * LANES), BF16)
        spare = pltpu.VMEM((TAIL * (-(-site // ROWS) * ROWS), LANES), F32)
        pushed = pltpu.VMEM((GROUP * main, tall), BF16)
        return call(
            functools.partial(absorb_kernel, bond, site, first, (2,) * (GROUP // 2)),
            (rows_in, edge, tensor, frame) + more,
            [payload, wide] if first else [dense],
            ([] if first else [half_bf16])
            + [mixed, mixed, spare, spare, pushed, pushed]
            + [pltpu.VMEM((tall, LANES), F32), pltpu.VMEM(((LANES + GROUP) * main, LANES), F32)],
            28,
            25,
        )

    def half_of(corner, edge):
        return call(functools.partial(half_kernel, bond, site), (corner, edge), [packed], [], 60, 2)[0]

    upper_packed = half_of(c1, t1)
    upper_next = shift(upper_packed, "row", -1)
    lower_packed = half_of(c4, t3)
    lower_back = shift(lower_packed, "row", 1)
    prepared = call(
        functools.partial(prepare_kernel, bond, site),
        (c2, t2, t4, t1, above, below, upper_packed, lower_packed),
        [wide, dense, stack, stack_f32, stack, stack_f32, packed, stack],
        [],
        16,
        2,
    )
    t4_wide, t1_held, upper, upper_sketch, lower, lower_sketch, side_packed, side = prepared
    tensor = pick(pattern.reshape(1), side)
    tensor_left = arrange(0, tensor, side)
    t1_back = shift(t1_held, "row", 1)
    side_back = shift_both(side_packed, 1, 1)
    tensor_back = shift(tensor, "row", 1)
    rows_left, frame_below, corner_top, corner_bottom = call(
        functools.partial(vertical_kernel, bond, site),
        (upper_next, lower_back, above, below, upper, upper_sketch, lower, lower_sketch),
        [frame_rows, stack, corner, corner],
        [half_bf16] * 5 + frame_scratch,
        20,
        8,
    )
    left_new, edge_wide = absorb(True, rows_left, t4_wide, tensor_left, frame_below, corner_top, corner_bottom)
    left_back = shift_both(left_new, 1, 1)
    inverse, frame_right = call(
        functools.partial(horizontal_kernel, bond, site),
        (corner_top, edge_wide, left, right, side),
        [shape_of((-(-bond // HALF_TILE) * HALF_TILE, LANES), F32), shape_of((bond, packed.shape[1] + LANES))],
        [half_bf16] * 3,
        16,
        5,
    )
    inverse_back = shift_both(inverse, 1, 1)
    frame_back = shift(frame_right, "row", 1)
    tensor_top = arrange(1, tensor_back, inverse)
    early_sketch, t1_wide = call(
        functools.partial(early_kernel, bond, site),
        (side_back, right, t1_back, inverse),
        [stack_f32, wide],
        [half_bf16],
        16,
        2,
        1,
    )
    rows_top, top_left, forward = call(
        functools.partial(arrive_kernel, bond, site),
        (left_back, early_sketch, left, inverse_back),
        [frame_rows, corner, payload],
        [half_bf16] * 3 + frame_scratch,
        16,
        4,
    )
    left_here = shift(forward, "row", -1)
    (top_edge,) = absorb(False, rows_top, t1_wide, tensor_top, frame_back)
    left_corner, left_edge, left_bottom, top_right = call(
        functools.partial(finish_kernel, bond),
        (left_here, frame_back),
        [corner, dense, corner, corner],
        [],
        8,
        1,
    )
    return (left_corner, left_edge, left_bottom, top_left, top_edge, top_right)


def solution(mesh):
    block, whole = P("col", "row"), P()
    in_specs = (block,) * 7 + (whole, block) + (whole,) * 4
    return jax.shard_map(
        body, mesh=mesh, in_specs=in_specs, out_specs=(block,) * 6, check_vma=False
    )
```

```python
import functools

import jax
import jax.numpy as jnp
import numpy as np
from jax import lax
from jax.experimental import pallas as pl
from jax.experimental.pallas import tpu as pltpu
from jax.sharding import PartitionSpec as P

LANES = 128
ROWS = 8
HALF_TILE = 16
GROUP = 10
CUTS = 4
QUARTERS = 4
MIB = 1 << 20
F32 = jnp.float32
BF16 = jnp.bfloat16

NN = (((1,), (0,)), ((), ()))
NT = (((1,), (1,)), ((), ()))
TN = (((0,), (0,)), ((), ()))


def product(left, right, dims=NN):
    return lax.dot_general(left, right, dims, preferred_element_type=F32)


def halves(values):
    high = values.astype(BF16)
    return high, (values - high.astype(F32)).astype(BF16)


def product_split(left, right, dims=NN):
    left_high, left_low = halves(left)
    right_high, right_low = halves(right)
    axis_left, axis_right = dims[0][0][0], dims[0][1][0]
    both = jnp.concatenate([left_high, left_low], axis_left)
    twice = jnp.concatenate([right_high, right_high], axis_right)
    return product(both, twice, dims) + product(left_high, right_low, dims)


def index_of(shape, axis):
    return lax.broadcasted_iota(jnp.int32, shape, axis)


def square_of(ref, bond):
    shape = (LANES, LANES)
    keep = (index_of(shape, 0) < bond) & (index_of(shape, 1) < bond)
    return jnp.where(keep, ref[...].astype(F32), 0.0)


def spread(ref, bond, site):
    shape = (LANES, LANES)
    row, lane = index_of(shape, 0), index_of(shape, 1)
    keep = (row < bond) & (lane < bond)
    pieces = []
    for k in range(site):
        tile, offset = divmod(k * bond, LANES)
        piece = ref[:, tile * LANES : (tile + 1) * LANES].astype(F32)
        if offset:
            piece = pltpu.roll(piece, LANES - offset, 1)
        if offset + bond > LANES:
            more = ref[:, (tile + 1) * LANES : (tile + 2) * LANES].astype(F32)
            piece = jnp.where(lane < LANES - offset, piece, pltpu.roll(more, LANES - offset, 1))
        pieces.append(jnp.where(keep, piece, 0.0).astype(BF16))
    return pieces


def gather_dense(tiles, ref, bond):
    lane = index_of((LANES, LANES), 1)
    total = len(tiles) * bond
    for tile in range(-(-total // LANES)):
        begin = tile * LANES
        value = None
        for k in range(begin // bond, min(len(tiles) - 1, (begin + LANES - 1) // bond) + 1):
            shift = k * bond - begin
            piece = pltpu.roll(tiles[k], shift % LANES, 1) if shift % LANES else tiles[k]
            value = piece if value is None else jnp.where(lane >= shift, piece, value)
        ref[:, begin : begin + LANES] = value.astype(ref.dtype)


def pack(tiles, ref, bond):
    quarter = bond // QUARTERS
    lane = index_of((LANES, LANES), 1)
    for group in range(len(tiles) // (QUARTERS + 1)):
        first = group * (QUARTERS + 1)
        for m in range(QUARTERS):
            piece = pltpu.roll(tiles[first + QUARTERS], bond - m * quarter, 1)
            slot = group * QUARTERS + m
            value = jnp.where(lane < bond, tiles[first + m], piece)
            ref[:, slot * LANES : (slot + 1) * LANES] = value.astype(ref.dtype)


def unpack(ref, bond, site):
    quarter = bond // QUARTERS
    shape = (LANES, LANES)
    row, lane = index_of(shape, 0), index_of(shape, 1)
    keep = (row < bond) & (lane < bond)
    tiles = []
    for group in range(site // (QUARTERS + 1)):
        last = None
        for m in range(QUARTERS):
            slot = group * QUARTERS + m
            value = ref[:, slot * LANES : (slot + 1) * LANES].astype(F32)
            tiles.append(jnp.where(keep, value, 0.0).astype(BF16))
            piece = pltpu.roll(value, LANES - bond + m * quarter, 1)
            last = piece if last is None else jnp.where(lane >= m * quarter, piece, last)
        tiles.append(jnp.where(keep, last, 0.0).astype(BF16))
    return tiles


def sketched(stack, sketch):
    return product(jnp.concatenate([stack, stack], 1), jnp.concatenate(halves(sketch), 0))


def inverse_factors(grams, bond):
    count = -(-bond // ROWS) * ROWS
    shape = (count, LANES)
    row, lane = index_of(shape, 0), index_of(shape, 1)
    inside = (row < bond) & (lane < bond)
    eye = jnp.where(row == lane, 1.0, 0.0)
    work = [jnp.where(inside, gram[:count], eye) for gram in grams]
    done = [[] for _ in grams]
    for first in range(0, count, ROWS):
        height = count - first
        row, lane = index_of((height, LANES), 0), index_of((height, LANES), 1)
        block = (lane >= first) & (lane < first + ROWS)
        start = jnp.where(row == lane - first, 1.0, 0.0)
        small_row, small_lane = index_of((ROWS, LANES), 0), index_of((ROWS, LANES), 1)
        columns = []
        for n, matrix in enumerate(work):
            columns.append(
                [
                    jnp.broadcast_to(matrix[:, first + j : first + j + 1], (height, LANES))
                    for j in range(ROWS)
                ]
            )
            work[n] = jnp.where(block, start, matrix)
        pivots = [jnp.ones((ROWS, LANES), F32) for _ in work]
        for j in range(ROWS):
            for n in range(len(work)):
                column = columns[n]
                pivot = column[j][j : j + 1, :]
                factor = jnp.where(row > j, column[j] * (1.0 / pivot), 0.0)
                work[n] = work[n] - factor * work[n][j : j + 1, :]
                for later in range(j + 1, ROWS):
                    column[later] = column[later] - factor * column[later][j : j + 1, :]
                pivots[n] = jnp.where(small_row == j, pivot, pivots[n])
        for n in range(len(work)):
            scaled = work[n][:ROWS] * lax.rsqrt(pivots[n])
            done[n].append(jnp.where(small_lane <= small_row + first, scaled, 0.0))
            work[n] = work[n][ROWS:]
    tail = jnp.zeros((LANES - count, LANES), F32)
    keep = (index_of((LANES, LANES), 0) < bond) & (index_of((LANES, LANES), 1) < bond)
    return [jnp.where(keep, jnp.concatenate(parts + [tail], 0), 0.0) for parts in done]


def store_halves(values, high, low):
    high[...], low[...] = halves(values)


def gram_and_overlap(other, high, low):
    left = jnp.concatenate([high[...], other], 1)
    both = product(left, jnp.concatenate([high[...], low[...]], 1), TN)
    mixed = both[:LANES, LANES:]
    gram = both[:LANES, :LANES] + mixed + mixed.T
    return gram, both[LANES:, :LANES] + both[LANES:, LANES:]


def overlap(other, high, low):
    both = product(other, jnp.concatenate([high[...], low[...]], 1), TN)
    return both[:, :LANES] + both[:, LANES:]


def frame_from(high, low, inverse):
    inverse_high, inverse_low = halves(inverse)
    left = jnp.concatenate([high[...], low[...], high[...]], 1)
    return product(left, jnp.concatenate([inverse_high, inverse_high, inverse_low], 1), NT)


def scaled_corner(values, bond):
    mean = jnp.sum(values * values) / (bond * bond)
    return (values / jnp.sqrt(mean + 1e-06)).astype(BF16)


def half_tiles(corner, pieces):
    return [product(corner, piece) for piece in pieces]


def fill(stack, tiles):
    for k, tile in enumerate(tiles):
        stack[k * LANES : (k + 1) * LANES, :] = tile.astype(stack.dtype)


def store_frame_rows(high, low, inverse, rows_ref, plain, tail, site):
    main = site - 1
    bond_rows = plain.shape[0] // main
    inverse_high, inverse_low = halves(inverse)
    left = jnp.concatenate([inverse_high, inverse_high, inverse_low], 1)[:bond_rows]
    for k in range(site):
        rows = slice(k * LANES, (k + 1) * LANES)
        tile = product(left, jnp.concatenate([high[rows, :], low[rows, :], high[rows, :]], 1), NT)
        if k < main:
            plain[pl.ds(k, bond_rows, stride=main), :] = tile
        else:
            for group in range(tail.shape[0] // HALF_TILE):
                begin = group * HALF_TILE
                tail[begin : begin + GROUP, :] = tile[group * GROUP : (group + 1) * GROUP]
    rows_ref[: plain.shape[0], :] = plain[...].astype(BF16)
    rows_ref[plain.shape[0] :, :] = tail[...].astype(BF16)


def halves_kernel(bond, site, c1, t1, c4, t3, upper_packed, lower_packed):
    for corner, edge, packed in ((c1, t1, upper_packed), (c4, t3, lower_packed)):
        pack(half_tiles(square_of(corner, bond).astype(BF16), spread(edge, bond, site)), packed, bond)


def prepare_kernel(
    bond, site, c2, t2, t4, t1, above, below, right, upper_packed, lower_packed,
    t4_wide, t1_out, upper, upper_sketch, lower, lower_sketch, side_packed, side, side_sketch,
):
    t1_out[...] = t1[...]
    tiles = half_tiles(square_of(c2, bond).astype(BF16), spread(t2, bond, site))
    fill(side, tiles)
    pack(tiles, side_packed, bond)
    fill(upper, unpack(upper_packed, bond, site))
    fill(lower, unpack(lower_packed, bond, site))
    upper_sketch[...] = sketched(upper[...], square_of(above, bond))
    lower_sketch[...] = sketched(lower[...], square_of(below, bond))
    side_sketch[...] = sketched(side[...], square_of(right, bond))
    for k, piece in enumerate(spread(t4, bond, site)):
        t4_wide[:, k * LANES : (k + 1) * LANES] = piece


def vertical_kernel(
    bond, site, upper_packed, lower_packed, above, below, upper, upper_sketch, lower, lower_sketch,
    rows_ref, frame_out, corner_top, corner_bottom, stack, over, over_low, under, under_low, plain, tail,
):
    fill(stack, unpack(upper_packed, bond, site))
    store_halves(lower_sketch[...] + sketched(stack[...], square_of(above, bond)), under, under_low)
    fill(stack, unpack(lower_packed, bond, site))
    store_halves(upper_sketch[...] + sketched(stack[...], square_of(below, bond)), over, over_low)
    gram_over, mixed_over = gram_and_overlap(upper[...], over, over_low)
    gram_under, mixed_under = gram_and_overlap(lower[...], under, under_low)
    inverse_over, inverse_under = inverse_factors([gram_over, gram_under], bond)
    store_frame_rows(over, over_low, inverse_over, rows_ref, plain, tail, site)
    frame_out[...] = frame_from(under, under_low, inverse_under).astype(BF16)
    corner_top[...] = scaled_corner(product_split(inverse_over, mixed_over, NT), bond)
    corner_bottom[...] = scaled_corner(product_split(inverse_under, mixed_under, NT), bond)


def horizontal_kernel(
    bond, site, c1, edge, left, side, side_sketch, inverse_ref, frame_out, half, total, total_low
):
    corner = square_of(c1, bond).T.astype(BF16)
    fill(half, half_tiles(corner, [edge[:, k * LANES : (k + 1) * LANES] for k in range(site)]))
    store_halves(side_sketch[...] + sketched(half[...], square_of(left, bond)), total, total_low)
    gram, mixed = gram_and_overlap(side[...], total, total_low)
    (inverse,) = inverse_factors([gram], bond)
    inverse_ref[...] = inverse[: inverse_ref.shape[0]]
    frame = frame_from(total, total_low, inverse)
    pack([frame[k * LANES : (k + 1) * LANES, :] for k in range(site)], frame_out, bond)
    corner_right = scaled_corner(product_split(inverse, mixed, NT), bond)
    frame_out[:, frame_out.shape[1] - LANES :] = corner_right


def early_kernel(bond, site, side_packed, right, t1, after, side_sketch, t1_wide, stack):
    for k, piece in enumerate(spread(t1, bond, site)):
        t1_wide[:, k * LANES : (k + 1) * LANES] = piece
    fill(stack, unpack(side_packed, bond, site))
    side_sketch[...] = sketched(stack[...], square_of(right, bond))


def arrive_kernel(
    bond, site, payload, side_sketch, left, inverse_ref,
    rows_ref, corner_left, forward, half, total, total_low, plain, tail,
):
    start = payload.shape[1] - 2 * LANES
    corner = square_of(payload.at[:, start : start + LANES], bond).T.astype(BF16)
    fill(half, half_tiles(corner, spread(payload, bond, site)))
    store_halves(side_sketch[...] + sketched(half[...], square_of(left, bond)), total, total_low)
    rest = jnp.zeros((LANES - inverse_ref.shape[0], LANES), F32)
    inverse = jnp.concatenate([inverse_ref[...], rest], 0)
    store_frame_rows(total, total_low, inverse, rows_ref, plain, tail, site)
    mixed = overlap(half[...], total, total_low)
    corner_left[...] = scaled_corner(product_split(mixed, inverse, NT), bond)
    forward[...] = payload[...]


def finish_kernel(bond, payload, frame, left_corner, left_edge, left_bottom, top_right):
    start = payload.shape[1] - 2 * LANES
    left_edge[...] = payload[:, :start]
    left_corner[...] = payload[:, start : start + LANES]
    left_bottom[...] = payload[:, start + LANES :]
    top_right[...] = frame[:, frame.shape[1] - LANES :]


def absorb_kernel(bond, site, first, rows_ref, edge, tensor, frame, *refs):
    mixed_even, mixed_odd, spare_even, spare_odd, pushed_even, pushed_odd, last, result = refs[-8:]
    if first:
        corner, bottom, dense, wide = refs[:4]
        frame_out = frame
    else:
        dense, frame_out = refs[0], refs[1]
        fill(frame_out, unpack(frame, bond, site))
    main = site - 1
    groups = bond // GROUP
    tall = GROUP * main
    slot = spare_even.shape[0] // HALF_TILE
    spare_even[...] = jnp.zeros_like(spare_even)
    spare_odd[...] = jnp.zeros_like(spare_odd)
    ahead = tall + bond * main
    result[ahead:, :] = jnp.zeros((result.shape[0] - ahead, LANES), F32)

    def frames_of(group):
        body = rows_ref[pl.ds(pl.multiple_of(group * tall, tall), tall), :]
        begin = rows_ref.shape[0] - groups * HALF_TILE + group * HALF_TILE
        tail = rows_ref[pl.ds(pl.multiple_of(begin, HALF_TILE), HALF_TILE), :]
        return jnp.concatenate([body, tail], 0)

    def mix(frames, mixed, spare, unit):
        j = 2 * unit
        sides = min(2, site - j)
        both = product(frames, edge[:, j * LANES : (j + sides) * LANES])
        for side in range(sides):
            lanes = slice(side * LANES, (side + 1) * LANES)
            spare[pl.ds(j + side, HALF_TILE, stride=slot), :] = both[tall:, lanes]
        for p in range(GROUP):
            parts = [
                both[p * main : (p + 1) * main, side * LANES : (side + 1) * LANES]
                for side in range(sides)
            ]
            end = (j + sides) * main
            if sides == 1:
                end = mixed.shape[0]
                parts.append(spare[p * slot : (p + 1) * slot, :])
                parts.append(jnp.zeros((end - j * main - main - slot, LANES), F32))
            mixed[j * main : end, p * LANES : (p + 1) * LANES] = (
                jnp.concatenate(parts, 0).astype(BF16)
            )

    def push(group, mixed, pushed, pair):
        out = product(tensor[...], mixed[:, 2 * pair * LANES : (2 * pair + 2) * LANES])
        for k in range(site):
            parts = [
                out[k * main : (k + 1) * main, side * LANES : (side + 1) * LANES]
                for side in range(2)
            ]
            pushed[2 * pair * main : (2 * pair + 2) * main, k * LANES : (k + 1) * LANES] = (
                jnp.concatenate(parts, 0).astype(BF16)
            )
        for side in range(2):
            place = group * GROUP + 2 * pair + side
            last[pl.ds(place, site, stride=LANES), :] = out[
                site * main : site * main + site, side * LANES : (side + 1) * LANES
            ]

    def cuts():
        step = -(-site // CUTS) // 2 * 2
        starts = [n * step for n in range(CUTS)] + [site]
        return [slice(low * LANES, high * LANES) for low, high in zip(starts, starts[1:])]

    def close(group, total):
        result[pl.ds(pl.multiple_of((group + 1) * tall, tall), tall), :] = total

    units = (site + 1) // 2

    def stage(group, mixed, pushed, mixed_next, spare_next, pushed_before):
        frames = frames_of(jnp.minimum(group + 1, groups - 1))
        total = jnp.zeros((tall, LANES), F32)
        pairs = GROUP // 2
        parts = cuts()
        for n in range(pairs):
            push(group, mixed, pushed, n)
            for unit in range(n * units // pairs, (n + 1) * units // pairs):
                mix(frames, mixed_next, spare_next, unit)
            if n < CUTS:
                total = total + product(pushed_before[:, parts[n]], frame_out[parts[n], :])
        close(group - 1, total)

    frames = frames_of(0)
    for unit in range(units):
        mix(frames, mixed_even, spare_even, unit)

    def step(index, carry):
        stage(2 * index, mixed_even, pushed_even, mixed_odd, spare_odd, pushed_odd)
        stage(2 * index + 1, mixed_odd, pushed_odd, mixed_even, spare_even, pushed_even)
        return carry

    lax.fori_loop(0, groups // 2, step, 0)
    close(groups - 1, product(pushed_odd[...], frame_out[...]))
    tiles = [result[pl.ds(tall + k, LANES, stride=main), :] for k in range(main)]
    total = jnp.zeros((LANES, LANES), F32)
    for k in range(site):
        rows = pl.ds(k * LANES, LANES)
        total = total + product(last[rows, :].astype(BF16), frame_out[rows, :])
    tiles.append(jnp.where(index_of(total.shape, 0) < bond, total, 0.0))
    squares = tiles[0] * tiles[0]
    for tile in tiles[1:]:
        squares = squares + tile * tile
    scale = 1.0 / jnp.sqrt(jnp.sum(squares) / (bond * bond * site) + 1e-06)
    tiles = [tile * scale for tile in tiles]
    gather_dense(tiles, dense, bond)
    if first:
        for k, tile in enumerate(tiles):
            wide[:, k * LANES : (k + 1) * LANES] = tile.astype(BF16)
        start = dense.shape[1] - 2 * LANES
        dense[:, start : start + LANES] = square_of(corner, bond).astype(BF16)
        dense[:, start + LANES :] = square_of(bottom, bond).astype(BF16)


def pick_kernel(pattern, tensors, out, *tiles):
    height, count, width = tensors.shape
    values = tensors[...].astype(F32).reshape(height * count, width)
    for n, tile in enumerate(tiles):
        end = min(width, (n + 1) * LANES)
        tile[:, : end - n * LANES] = values[:, n * LANES : end]
        rows = tile[pl.ds(pattern[0], height, stride=count), :]
        out[:, n * LANES : end] = rows[:, : end - n * LANES].astype(BF16)


def arrange_kernel(tensor, rows, columns, after, out):
    square = tensor.shape[0]
    pick_rows = jnp.where(index_of((rows.shape[0], square), 1) == rows[...], 1.0, 0.0).astype(BF16)
    pick_columns = jnp.where(index_of((square, columns.shape[1]), 0) == columns[...], 1.0, 0.0)
    turned = product(pick_rows, tensor[...], NT).astype(BF16)
    out[...] = product(turned, pick_columns.astype(BF16)).astype(BF16)


def places(site):
    main = site - 1
    size = -(-site * site // LANES) * LANES
    rows = np.full((2, size), -1, np.int32)
    columns = np.full((2, size), -1, np.int32)
    for other in range(site):
        for inner in range(site):
            at = other * main + inner if inner < main else site * main + other
            rows[0, at] = other * site + inner
            rows[1, at] = inner * site + other
            columns[0, at] = inner * site + other
            columns[1, at] = other * site + inner
    return rows, columns


def block_of(arg):
    shape = arg.shape
    if len(shape) == 1:
        return pl.BlockSpec(memory_space=pltpu.SMEM)
    if shape[0] % 16 == 0 and shape[1] % LANES == 0:
        return pl.BlockSpec(memory_space=pltpu.VMEM)
    return pl.BlockSpec(tuple(-(-size // LANES) * LANES for size in shape), lambda i: (0, 0))


def cost(microseconds):
    return pl.CostEstimate(
        flops=microseconds * 1_000_000_000, bytes_accessed=microseconds * 1_000_000, transcendentals=0
    )


def call(kernel, args, outs, scratch, limit, microseconds, unread=0):
    specs = [block_of(arg) for arg in args]
    if unread:
        specs[-unread:] = [pl.BlockSpec(memory_space=pl.ANY)] * unread
    return pl.pallas_call(
        kernel,
        grid=(1,),
        in_specs=specs,
        out_specs=[block_of(out) for out in outs],
        out_shape=outs,
        scratch_shapes=scratch,
        compiler_params=pltpu.CompilerParams(vmem_limit_bytes=limit * MIB),
        cost_estimate=cost(microseconds),
    )(*args)


def shape_of(shape, dtype=BF16):
    return jax.ShapeDtypeStruct(shape, dtype)


def shift(value, axis, steps):
    count = lax.axis_size(axis)
    pairs = [(source, (source + steps) % count) for source in range(count)]
    return lax.ppermute(value, axis, pairs)


def shift_both(value, steps_col, steps_row):
    columns, rows = lax.axis_size("col"), lax.axis_size("row")
    pairs = []
    for x in range(columns):
        for y in range(rows):
            target = (x + steps_col) % columns * rows + (y + steps_row) % rows
            pairs.append((x * rows + y, target))
    return lax.ppermute(value, ("col", "row"), pairs)


def body(c1, c2, c4, t1, t2, t3, t4, tensors, pattern, below, above, right, left):
    bond = c1.shape[0]
    site = t1.shape[1] // bond
    square = site * site
    tall = site * LANES
    bond_rows = -(-bond // ROWS) * ROWS
    body_rows = bond_rows * (site - 1)
    tail_rows = bond // GROUP * HALF_TILE
    frame_rows = shape_of((body_rows + tail_rows, LANES))
    packed = shape_of((bond, site // (QUARTERS + 1) * QUARTERS * LANES))
    dense = shape_of((bond, site * bond))
    wide = shape_of((LANES, tall))
    stack = shape_of((tall, LANES))
    stack_f32 = shape_of((tall, LANES), F32)
    corner = shape_of((bond, bond))
    payload = shape_of((bond, -(-site * bond // LANES) * LANES + 2 * LANES))
    half_bf16 = pltpu.VMEM((tall, LANES), BF16)
    frame_scratch = [pltpu.VMEM((body_rows, LANES), F32), pltpu.VMEM((tail_rows, LANES), F32)]
    rows, columns = places(site)

    def pick(index):
        count = tensors.shape[0]
        return pl.pallas_call(
            pick_kernel,
            grid=(-(-square // LANES),),
            in_specs=[
                pl.BlockSpec(memory_space=pltpu.SMEM),
                pl.BlockSpec((LANES, count, square), lambda i: (i, 0, 0)),
            ],
            out_specs=pl.BlockSpec((LANES, square), lambda i: (i, 0)),
            out_shape=shape_of((square, square)),
            scratch_shapes=[pltpu.VMEM((LANES * count, LANES), F32)] * -(-square // LANES),
            compiler_params=pltpu.CompilerParams(vmem_limit_bytes=16 * MIB),
            cost_estimate=cost(2),
        )(index, tensors.transpose(1, 0, 2))

    def arrange(which, tensor, after):
        height, depth = rows.shape[1], columns.shape[1]
        vmem = pl.BlockSpec(memory_space=pltpu.VMEM)
        return pl.pallas_call(
            arrange_kernel,
            in_specs=[vmem, vmem, vmem, pl.BlockSpec(memory_space=pl.ANY)],
            out_specs=vmem,
            out_shape=shape_of((height, depth)),
            compiler_params=pltpu.CompilerParams(vmem_limit_bytes=16 * MIB),
            cost_estimate=cost(2),
        )(
            tensor,
            rows[which].reshape(height, 1),
            columns[which].reshape(1, depth),
            after,
        )

    def absorb(first, rows_in, edge, tensor, frame, *more):
        main = site - 1
        mixed = pltpu.VMEM((tensor.shape[1], GROUP * LANES), BF16)
        spare = pltpu.VMEM((HALF_TILE * (-(-site // ROWS) * ROWS), LANES), F32)
        pushed = pltpu.VMEM((GROUP * main, tall), BF16)
        return call(
            functools.partial(absorb_kernel, bond, site, first),
            (rows_in, edge, tensor, frame) + more,
            [payload, wide] if first else [dense],
            ([] if first else [half_bf16])
            + [mixed, mixed, spare, spare, pushed, pushed]
            + [pltpu.VMEM((tall, LANES), F32), pltpu.VMEM(((LANES + GROUP) * main, LANES), F32)],
            28,
            25,
        )

    upper_packed, lower_packed = call(
        functools.partial(halves_kernel, bond, site),
        (c1, t1, c4, t3),
        [packed, packed],
        [],
        60,
        2,
    )
    upper_next = shift(upper_packed, "row", -1)
    lower_back = shift(lower_packed, "row", 1)
    tensor = pick(pattern.reshape(1))
    tensor_left = arrange(0, tensor, upper_packed)
    prepared = call(
        functools.partial(prepare_kernel, bond, site),
        (c2, t2, t4, t1, above, below, right, upper_packed, lower_packed),
        [wide, dense, stack, stack_f32, stack, stack_f32, packed, stack, stack_f32],
        [],
        16,
        2,
    )
    t4_wide, t1_held, upper, upper_sketch, lower, lower_sketch, side_packed, side, side_sketch = prepared
    t1_back = shift(t1_held, "row", 1)
    side_back = shift_both(side_packed, 1, 1)
    tensor_back = shift(tensor, "row", 1)
    rows_left, frame_below, corner_top, corner_bottom = call(
        functools.partial(vertical_kernel, bond, site),
        (upper_next, lower_back, above, below, upper, upper_sketch, lower, lower_sketch),
        [frame_rows, stack, corner, corner],
        [half_bf16] * 5 + frame_scratch,
        20,
        8,
    )
    left_new, edge_wide = absorb(True, rows_left, t4_wide, tensor_left, frame_below, corner_top, corner_bottom)
    left_back = shift_both(left_new, 1, 1)
    inverse, frame_right = call(
        functools.partial(horizontal_kernel, bond, site),
        (corner_top, edge_wide, left, side, side_sketch),
        [shape_of((-(-bond // HALF_TILE) * HALF_TILE, LANES), F32), shape_of((bond, packed.shape[1] + LANES))],
        [half_bf16] * 3,
        16,
        5,
    )
    inverse_back = shift_both(inverse, 1, 1)
    frame_back = shift(frame_right, "row", 1)
    tensor_top = arrange(1, tensor_back, inverse)
    early_sketch, t1_wide = call(
        functools.partial(early_kernel, bond, site),
        (side_back, right, t1_back, inverse),
        [stack_f32, wide],
        [half_bf16],
        16,
        2,
        1,
    )
    rows_top, top_left, forward = call(
        functools.partial(arrive_kernel, bond, site),
        (left_back, early_sketch, left, inverse_back),
        [frame_rows, corner, payload],
        [half_bf16] * 3 + frame_scratch,
        16,
        4,
    )
    left_here = shift(forward, "row", -1)
    (top_edge,) = absorb(False, rows_top, t1_wide, tensor_top, frame_back)
    left_corner, left_edge, left_bottom, top_right = call(
        functools.partial(finish_kernel, bond),
        (left_here, frame_back),
        [corner, dense, corner, corner],
        [],
        8,
        1,
    )
    return (left_corner, left_edge, left_bottom, top_left, top_edge, top_right)


def solution(mesh):
    block, whole = P("col", "row"), P()
    in_specs = (block,) * 7 + (whole, block) + (whole,) * 4
    return jax.shard_map(
        body, mesh=mesh, in_specs=in_specs, out_specs=(block,) * 6, check_vma=False
    )
```
